32 devices in a mesh: cells: 8 (over y, x, core), comp: 4 (over z).
Axes of the slice: x: 2, y: 2, z: 4, core: 2. Of those that a mesh axis runs over, the one named last changes fastest.
Arguments:
- factor_field: float32 [16, 256, 256], P(None, ('cells', 'comp')), may hold values from -90 to 90
- profile: float32 [512, 128], P('comp'), may hold values from -4 to 4
- mixing: float32 [16, 512], P(None, 'comp'), may hold values from -1.5 to 1.5
- factor_mom: float32 [16, 256, 256], P(None, ('cells', 'comp')), may hold values from -6 to 6
- profile_mom: float32 [512, 128], P('comp'), may hold values from -6 to 6
- mixing_mom: float32 [16, 512], P(None, 'comp'), may hold values from -6 to 6
- field_tau: float32 [16], replicated, may hold values from 0.5 to 5
- counts: int32 [128, 256, 256], P(None, 'cells'), may hold values from 0 to 15
- land_mask: int32 [256, 256], P('cells'), may hold values 0 or 1
- log_exposure: float32 [256, 256], P('cells'), may hold values from -4 to -2
Outputs:
- new_field: float32 [16, 256, 256], P(None, ('cells', 'comp'))
- new_profile: float32 [512, 128], P('comp')
- new_mixing: float32 [16, 512], P(None, 'comp')
- new_factor_mom: float32 [16, 256, 256], P(None, ('cells', 'comp'))
- new_profile_mom: float32 [512, 128], P('comp')
- new_mixing_mom: float32 [16, 512], P(None, 'comp')
- hamiltonian: float32 [], replicated
The draws below stay inside these ranges and needn't reach their ends.
All inputs are finite; a program needn't handle non-finite values. No bound on the sum of `land_mask` on one device may be relied on, other than what follows from the above.
Results may differ from the reference program's by a relative error of at most 0.0003.
Values sent between devices are 32-bit elements; how exact they have to be, the bound alone decides.
No kernel may reach another device: no remote copies, remote signals or barrier semaphores. Data moves between devices by JAX's collectives and lax.ppermute only.
A program may use at most 64 MiB of HBM per device.

```python
import math
import jax
import jax.numpy as jnp
from jax import lax

FAC = 16
K = 128
COMP = 512
RX = 32
GY = 256
GX = 256
N_CELLS = 8


def draw_counts(key, part):
    level_key = jax.random.fold_in(key, 11)
    spot_key = jax.random.fold_in(key, 23)
    empty_key = jax.random.fold_in(key, 37)
    cells_all = GX * GY
    ticket = jax.random.randint(level_key, (K, cells_all), 0, 10000)
    sparse = (ticket >= 7400).astype(jnp.int32) + (ticket >= 9600).astype(jnp.int32)
    sparse = sparse + (ticket >= 9950).astype(jnp.int32) + (ticket >= 9995).astype(jnp.int32)
    hot_cell = jax.random.randint(spot_key, (K,), 0, cells_all)
    empty_cell = (hot_cell + 1 + jax.random.randint(empty_key, (K,), 0, cells_all - 1)) % cells_all
    category_ids = jnp.arange(K, dtype=jnp.int32)
    sparse = sparse.at[category_ids, empty_cell].set(0)
    sparse = sparse.at[category_ids, hot_cell].set(15)
    return sparse.reshape(K, GX, GY)


def draw_factor_field(key, part):
    base_key = jax.random.fold_in(key, 41)
    place_key = jax.random.fold_in(key, 43)
    power_key = jax.random.fold_in(key, 47)
    sign_key = jax.random.fold_in(key, 53)
    cells_all = GX * GY
    spikes = 8
    base = jnp.clip(jax.random.normal(base_key, (FAC, cells_all), jnp.float32), -6.0, 6.0)
    places = jax.random.permutation(place_key, cells_all)[:spikes].astype(jnp.int32)
    power = jax.random.uniform(power_key, (spikes,), jnp.float32, 40.0, 90.0)
    signs = jnp.where(jax.random.bernoulli(sign_key, 0.5, (FAC, spikes)), 1.0, -1.0).astype(jnp.float32)
    base = base.at[:, places].set(signs * power[None, :])
    return base.reshape(FAC, GX, GY).astype(jnp.float32)


def plant(values, stream_key, low, high):
    place = [jax.random.randint(jax.random.fold_in(stream_key, axis), (), 0, length) for axis, length in enumerate(values.shape)]
    main_axis = values.shape.index(max(values.shape))
    neighbour = place[:main_axis] + [(place[main_axis] + 1) % values.shape[main_axis]] + place[main_axis + 1:]
    return values.at[tuple(place)].set(low).at[tuple(neighbour)].set(high)


def shard_levels(rng, dims, shards, low, largest):
    loudness, own = 1.0, jax.random.fold_in(rng, 6)
    for dim, parts in shards:
        draws = jnp.exp(jax.random.uniform(jax.random.fold_in(own, dim), (parts,), jnp.float32, low / len(shards), largest / len(shards)))
        loudness = loudness * jnp.repeat(draws, dims[dim] // parts).reshape([-1 if axis == dim else 1 for axis in range(len(dims))])
    return loudness


def bell_draw(stream_key, shape, scale, bound, shards=(), kind=jnp.bfloat16):
    gain = shard_levels(stream_key, shape, shards, -0.22, 0.18) if shards else 1.0
    drawn = jax.random.normal(stream_key, shape, jnp.float32) * scale * gain
    return jnp.minimum(jnp.maximum(drawn, -bound), bound).astype(kind)


def setup_inputs(seed: int = 0) -> dict:
    seeds = jax.random.split(jax.random.key(seed), 11)
    return {
        "factor_field": draw_factor_field(jax.random.fold_in(seeds[10], 71), 0),
        "profile": bell_draw(seeds[1], (COMP, K), 1.0, 4.0, ((0, 4),), jnp.float32),
        "mixing": bell_draw(seeds[2], (FAC, COMP), FAC ** -0.5, 1.5, ((1, 4),), jnp.float32),
        "factor_mom": bell_draw(seeds[3], (FAC, GX, GY), 1.0, 6.0, ((1, 32),), jnp.float32),
        "profile_mom": bell_draw(seeds[4], (COMP, K), 1.0, 6.0, ((0, 4),), jnp.float32),
        "mixing_mom": bell_draw(seeds[5], (FAC, COMP), 1.0, 6.0, ((1, 4),), jnp.float32),
        "field_tau": jnp.clip(jnp.exp(jax.random.uniform(seeds[6], (FAC,), jnp.float32, math.log(0.5), math.log(5.0))), 0.5, 5.0),
        "counts": draw_counts(jax.random.fold_in(seeds[10], 71), 0),
        "land_mask": plant((jax.random.randint(seeds[8], (GX, GY), 0, 4) < 3).astype(jnp.int32), jax.random.fold_in(seeds[8], 1), 0, 1),
        "log_exposure": jnp.clip(-4.0 + 2.0 * jax.random.uniform(seeds[9], (GX, GY), jnp.float32) ** shard_levels(seeds[9], (GX, GY), ((0, 8),), -0.2, 0.2), -4.0, -2.0),
    }


def field_prior(padded, land_pad, field_tau):
    ridge = 0.1
    step_x = padded[:, 1:, :] - padded[:, :-1, :]
    edge_x = land_pad[1:, :] * land_pad[:-1, :]
    flux_x = edge_x[None, :, :] * step_x
    centre = padded[:, 1:-1, :]
    land_mid = land_pad[1:-1, :]
    step_y = centre[:, :, 1:] - centre[:, :, :-1]
    edge_y = land_mid[:, 1:] * land_mid[:, :-1]
    flux_y = edge_y[None, :, :] * step_y
    lap_x = flux_x[:, :-1, :] - flux_x[:, 1:, :]
    lap_y = jnp.pad(flux_y, ((0, 0), (0, 0), (1, 0))) - jnp.pad(flux_y, ((0, 0), (0, 0), (0, 1)))
    tau_cube = field_tau[:, None, None]
    grad = -tau_cube * (lap_x + lap_y + ridge * centre)
    energy = 0.5 * jnp.sum(tau_cube * (flux_x[:, 1:, :] * step_x[:, 1:, :]))
    energy = energy + 0.5 * jnp.sum(tau_cube * (flux_y * step_y))
    energy = energy + 0.5 * ridge * jnp.sum(tau_cube * (centre * centre))
    return grad, energy


def tile_scores(flat_tile, count_rows, exposure, profile, mixing):
    prof_exp = jnp.exp(profile)
    rate_total = jnp.sum(prof_exp, axis=1)
    mix_logit = jnp.dot(mixing.T, flat_tile, precision=lax.Precision.HIGHEST)
    fit_score = jnp.dot(profile, count_rows, precision=lax.Precision.HIGHEST) - rate_total[:, None] * exposure[None, :]
    return mix_logit, mix_logit + fit_score


def tile_grads(flat_tile, count_rows, land_weight, exposure, mixing, mix_logit, joint_score, log_mix, log_joint):
    prior_share = jnp.exp(mix_logit - log_mix[None, :])
    posterior = jnp.exp(joint_score - log_joint[None, :])
    post_land = posterior * land_weight[None, :]
    gap_weight = (posterior - prior_share) * land_weight[None, :]
    grad_counts = jnp.dot(post_land, count_rows.T, precision=lax.Precision.HIGHEST)
    rate_mass = jnp.sum(post_land * exposure[None, :], axis=1)
    grad_mix = jnp.dot(flat_tile, gap_weight.T, precision=lax.Precision.HIGHEST)
    field_lik = jnp.dot(mixing, gap_weight, precision=lax.Precision.HIGHEST)
    log_dens = jnp.sum(land_weight * (log_joint - log_mix))
    return grad_counts, rate_mass, grad_mix, field_lik, log_dens


def log_terms(factor_field, profile, mixing, counts, land_mask, log_exposure, field_tau):
    nfac = factor_field.shape[0]
    ncat = counts.shape[0]
    width = RX * GY
    f_tiles = factor_field.reshape(nfac, N_CELLS, width).transpose(1, 0, 2)
    c_tiles = counts.reshape(ncat, N_CELLS, width).transpose(1, 0, 2)
    l_tiles = land_mask.reshape(N_CELLS, width)
    e_tiles = log_exposure.reshape(N_CELLS, width)

    def scan_tile(running, tile_item):
        flat_tile, count_int, land_int, log_exp = tile_item
        count_rows = count_int.astype(jnp.float32)
        land_weight = land_int.astype(jnp.float32)
        exposure = jnp.exp(log_exp)
        mix_logit, joint_score = tile_scores(flat_tile, count_rows, exposure, profile, mixing)
        top_mix = jnp.max(mix_logit, axis=0)
        log_mix = top_mix + jnp.log(jnp.sum(jnp.exp(mix_logit - top_mix[None, :]), axis=0))
        top_joint = jnp.max(joint_score, axis=0)
        log_joint = top_joint + jnp.log(jnp.sum(jnp.exp(joint_score - top_joint[None, :]), axis=0))
        grad_counts, rate_mass, grad_mix, field_lik, log_dens = tile_grads(
            flat_tile, count_rows, land_weight, exposure, mixing, mix_logit, joint_score, log_mix, log_joint)
        running = (running[0] + grad_counts, running[1] + rate_mass, running[2] + grad_mix, running[3] + log_dens)
        return running, field_lik

    start = (jnp.zeros(profile.shape, jnp.float32), jnp.zeros((profile.shape[0],), jnp.float32),
             jnp.zeros(mixing.shape, jnp.float32), jnp.zeros((), jnp.float32))
    totals, lik_tiles = lax.scan(scan_tile, start, (f_tiles, c_tiles, l_tiles, e_tiles))
    field_lik = lik_tiles.transpose(1, 0, 2).reshape(factor_field.shape)
    land_float = land_mask.astype(jnp.float32)
    padded = jnp.pad(factor_field, ((0, 0), (1, 1), (0, 0)))
    land_pad = jnp.pad(land_float, ((1, 1), (0, 0)))
    prior_grad, prior_energy = field_prior(padded, land_pad, field_tau)
    grad_field = prior_grad + field_lik
    grad_profile = totals[0] - jnp.exp(profile) * totals[1][:, None] - 0.25 * profile
    grad_mixing = totals[2] - mixing
    log_dens = totals[3] - prior_energy - 0.125 * jnp.sum(profile * profile) - 0.5 * jnp.sum(mixing * mixing)
    return log_dens, grad_field, grad_profile, grad_mixing


def reference(factor_field, profile, mixing, factor_mom, profile_mom, mixing_mom, field_tau, counts, land_mask, log_exposure):
    step_field = 0.05
    step_profile = 0.002
    step_mixing = 0.002
    first = log_terms(factor_field, profile, mixing, counts, land_mask, log_exposure, field_tau)
    half_field = factor_mom + 0.5 * step_field * first[1]
    half_profile = profile_mom + 0.5 * step_profile * first[2]
    half_mixing = mixing_mom + 0.5 * step_mixing * first[3]
    new_field = factor_field + step_field * half_field
    new_profile = profile + step_profile * half_profile
    new_mixing = mixing + step_mixing * half_mixing
    second = log_terms(new_field, new_profile, new_mixing, counts, land_mask, log_exposure, field_tau)
    new_factor_mom = half_field + 0.5 * step_field * second[1]
    new_profile_mom = half_profile + 0.5 * step_profile * second[2]
    new_mixing_mom = half_mixing + 0.5 * step_mixing * second[3]
    kinetic = 0.5 * (jnp.sum(new_factor_mom * new_factor_mom) + jnp.sum(new_profile_mom * new_profile_mom)
                     + jnp.sum(new_mixing_mom * new_mixing_mom))
    hamiltonian = (kinetic - second[0]) / (GX * GY)
    return new_field, new_profile, new_mixing, new_factor_mom, new_profile_mom, new_mixing_mom, hamiltonian
```

```python
import functools
import math

import jax
import jax.numpy as jnp
from jax import lax
from jax.experimental import pallas as pl
from jax.experimental.pallas import tpu as pltpu
from jax.sharding import PartitionSpec as P


def extended(cells, sides, width):
    for axis, dim in sides:
        count = lax.axis_size(axis)
        ends = count - 1
        head = lax.slice_in_dim(cells, 0, width, axis=dim)
        tail = lax.slice_in_dim(cells, cells.shape[dim] - width, cells.shape[dim], axis=dim)
        cells = jnp.concatenate(
            [
                lax.ppermute(tail, axis, [(i, (i + 1) % count) for i in range(ends)]),
                cells,
                lax.ppermute(head, axis, [((i + 1) % count, i) for i in range(ends)]),
            ],
            axis=dim,
        )
    return cells


def field_prior(padded, land_pad, field_tau):
    ridge = 0.1
    step_x = padded[:, 1:, :] - padded[:, :-1, :]
    edge_x = land_pad[1:, :] * land_pad[:-1, :]
    flux_x = edge_x[None, :, :] * step_x
    centre = padded[:, 1:-1, :]
    land_mid = land_pad[1:-1, :]
    step_y = centre[:, :, 1:] - centre[:, :, :-1]
    edge_y = land_mid[:, 1:] * land_mid[:, :-1]
    flux_y = edge_y[None, :, :] * step_y
    lap_x = flux_x[:, :-1, :] - flux_x[:, 1:, :]
    lap_y = jnp.pad(flux_y, ((0, 0), (0, 0), (1, 0))) - jnp.pad(flux_y, ((0, 0), (0, 0), (0, 1)))
    tau_cube = field_tau[:, None, None]
    grad = -tau_cube * (lap_x + lap_y + ridge * centre)
    energy = 0.5 * jnp.sum(tau_cube * (flux_x[:, 1:, :] * step_x[:, 1:, :]))
    energy = energy + 0.5 * jnp.sum(tau_cube * (flux_y * step_y))
    energy = energy + 0.5 * ridge * jnp.sum(tau_cube * (centre * centre))
    return (grad, energy)


def tile_scores(flat_tile, count_rows, exposure, profile, mixing):
    prof_exp = jnp.exp(profile)
    rate_total = jnp.sum(prof_exp, axis=1)
    mix_logit = jnp.dot(mixing.T, flat_tile, precision=lax.Precision.HIGHEST)
    fit_score = (
        jnp.dot(profile, count_rows, precision=lax.Precision.HIGHEST)
        - rate_total[:, None] * exposure[None, :]
    )
    return (mix_logit, mix_logit + fit_score)


def tile_grads(
    flat_tile, count_rows, land_weight, exposure, mixing, mix_logit, joint_score, log_mix, log_joint
):
    prior_share = jnp.exp(mix_logit - log_mix[None, :])
    posterior = jnp.exp(joint_score - log_joint[None, :])
    post_land = posterior * land_weight[None, :]
    gap_weight = (posterior - prior_share) * land_weight[None, :]
    grad_counts = jnp.dot(post_land, count_rows.T, precision=lax.Precision.HIGHEST)
    rate_mass = jnp.sum(post_land * exposure[None, :], axis=1)
    grad_mix = jnp.dot(flat_tile, gap_weight.T, precision=lax.Precision.HIGHEST)
    field_lik = jnp.dot(mixing, gap_weight, precision=lax.Precision.HIGHEST)
    log_dens = jnp.sum(land_weight * (log_joint - log_mix))
    return (grad_counts, rate_mass, grad_mix, field_lik, log_dens)


def log_sum(scores):
    top = jnp.max(scores, axis=0)
    return top + jnp.log(jnp.sum(jnp.exp(scores - top[None, :]), axis=0))


def plain_device(
    factor_field,
    profile,
    mixing,
    factor_mom,
    profile_mom,
    mixing_mom,
    field_tau,
    counts,
    land_mask,
    log_exposure,
):
    step_field = 0.05
    step_profile = 0.002
    step_mixing = 0.002
    tile_rows, tile_cols = land_mask.shape
    ncat = counts.shape[0]
    share_rows = factor_field.shape[1]
    comp_rank = lax.axis_index("comp")
    cells_rank = lax.axis_index("cells")
    first_cells = cells_rank == 0
    land_pad = extended(land_mask, (("cells", 0),), 1).astype(jnp.float32)
    row_start = comp_rank * share_rows
    count_rows = lax.dynamic_slice_in_dim(counts, row_start, share_rows, 1)
    count_rows = count_rows.reshape(ncat, share_rows * tile_cols).astype(jnp.float32)
    land_weight = (
        lax.dynamic_slice_in_dim(land_mask, row_start, share_rows, 0)
        .reshape(-1)
        .astype(jnp.float32)
    )
    exposure = jnp.exp(lax.dynamic_slice_in_dim(log_exposure, row_start, share_rows, 0).reshape(-1))
    land_near = lax.dynamic_slice_in_dim(land_pad, row_start, share_rows + 2, 0)

    def evaluate(share_field, profile_now, mixing_now):
        padded = extended(share_field, ((("cells", "comp"), 1),), 1)
        prior_grad, prior_energy = field_prior(padded, land_near, field_tau)
        profile_all, mixing_all = (
            lax.all_gather(profile_now, "comp", axis=0, tiled=True),
            lax.all_gather(mixing_now, "comp", axis=1, tiled=True),
        )
        flat_tile = share_field.reshape(share_field.shape[0], -1)
        mix_logit, joint_score = tile_scores(
            flat_tile, count_rows, exposure, profile_all, mixing_all
        )
        log_mix = log_sum(mix_logit)
        log_joint = log_sum(joint_score)
        grad_counts, rate_mass, grad_mix, field_lik, log_dens = tile_grads(
            flat_tile,
            count_rows,
            land_weight,
            exposure,
            mixing_all,
            mix_logit,
            joint_score,
            log_mix,
            log_joint,
        )
        grad_counts, rate_mass, mix_rows = (
            lax.psum_scatter(grad_counts, "comp", scatter_dimension=0, tiled=True),
            lax.psum_scatter(rate_mass, "comp", scatter_dimension=0, tiled=True),
            lax.psum_scatter(grad_mix.T, "comp", scatter_dimension=0, tiled=True),
        )
        grad_mix = mix_rows.T
        grad_field = prior_grad + field_lik.reshape(share_field.shape)
        log_part = log_dens - prior_energy
        grad_counts, rate_mass, grad_mix = lax.psum((grad_counts, rate_mass, grad_mix), "cells")
        grad_profile = grad_counts - jnp.exp(profile_now) * rate_mass[:, None] - 0.25 * profile_now
        grad_mixing = grad_mix - mixing_now
        param_prior = -0.125 * jnp.sum(profile_now * profile_now) - 0.5 * jnp.sum(
            mixing_now * mixing_now
        )
        log_part = log_part + jnp.where(first_cells, param_prior, 0.0)
        return (log_part, grad_field, grad_profile, grad_mixing)

    first = evaluate(factor_field, profile, mixing)
    half_field = factor_mom + 0.5 * step_field * first[1]
    half_profile = profile_mom + 0.5 * step_profile * first[2]
    half_mixing = mixing_mom + 0.5 * step_mixing * first[3]
    new_field = factor_field + step_field * half_field
    new_profile = profile + step_profile * half_profile
    new_mixing = mixing + step_mixing * half_mixing
    second = evaluate(new_field, new_profile, new_mixing)
    new_factor_mom = half_field + 0.5 * step_field * second[1]
    new_profile_mom = half_profile + 0.5 * step_profile * second[2]
    new_mixing_mom = half_mixing + 0.5 * step_mixing * second[3]
    kinetic = 0.5 * jnp.sum(new_factor_mom * new_factor_mom)
    kinetic = kinetic + jnp.where(
        first_cells,
        0.5
        * (jnp.sum(new_profile_mom * new_profile_mom) + jnp.sum(new_mixing_mom * new_mixing_mom)),
        0.0,
    )
    log_total, kinetic_total = lax.psum((second[0], kinetic), ("cells", "comp"))
    cell_count = tile_rows * tile_cols * lax.axis_size("cells")
    hamiltonian = (kinetic_total - log_total) / cell_count
    return (
        new_field,
        new_profile,
        new_mixing,
        new_factor_mom,
        new_profile_mom,
        new_mixing_mom,
        hamiltonian,
    )


STEP_FIELD = 0.05
STEP_PARAM = 0.002
RIDGE = 0.1
LOG2E = math.log2(math.e)
LN2 = math.log(2.0)
LANES = 128
F32 = jnp.float32
BF16 = jnp.bfloat16


def pieces(values, count):
    parts = []
    for _ in range(count):
        part = values.astype(BF16)
        parts.append(part)
        values = values - part.astype(F32)
    return parts


def dot(left, right, dims=((1,), (0,))):
    return lax.dot_general(left, right, (dims, ((), ())), preferred_element_type=F32)


def partner(values, axis, flip):
    count = lax.axis_size(axis)
    return lax.ppermute(values, axis, [(i, i ^ flip) for i in range(count)])


def all_sum(keep, send):
    pairs = keep.shape[0]
    ring = lax.axis_size("comp")
    chunks = keep + partner(send, "cells", 1)
    total = chunks[0]
    for part in [partner(chunks[k], "cells", 2 * k) for k in range(1, pairs)]:
        total = total + part
    parts = [partner(total, "comp", k) for k in range(1, ring)]
    for part in parts:
        total = total + part
    near = jnp.stack([total] + [partner(total, "cells", 2 * k) for k in range(1, pairs)])
    return near, partner(near, "cells", 1)


def chunk_index(cells_rank, k, other):
    core = cells_rank % 2
    return (((cells_rank // 2) ^ k) * 2) + (1 - core if other else core)


def gather_chunks(flat_ref, near_ref, far_ref, cells_rank):
    pairs, rows, _ = near_ref.shape
    for k in range(pairs):
        for source, other in ((near_ref, False), (far_ref, True)):
            start = pl.multiple_of(chunk_index(cells_rank, k, other) * rows, 8)
            flat_ref[pl.ds(start, rows), :] = source[k]


def spread_chunks(flat_ref, keep_ref, send_ref, cells_rank):
    pairs, rows, _ = keep_ref.shape
    for k in range(pairs):
        for target, other in ((keep_ref, False), (send_ref, True)):
            start = pl.multiple_of(chunk_index(cells_rank, k, other) * rows, 8)
            target[k] = flat_ref[pl.ds(start, rows), :]


def load_params(flat_ref, left_ref, mix_ref, load_ref, ncomp, nfac):
    lane = lax.broadcasted_iota(jnp.int32, (LANES, LANES), 1)
    first = 6 * nfac
    for q in range(ncomp // LANES):
        rows = pl.ds(q * LANES, LANES)
        prof = flat_ref[rows, :]
        high, mid, low = pieces(prof * LOG2E, 3)
        left_ref[rows, 0:LANES] = high
        left_ref[rows, 2 * LANES : 3 * LANES] = mid
        left_ref[rows, 3 * LANES : 4 * LANES] = low
        rate = jnp.sum(jnp.exp(prof), axis=1, keepdims=True) * LOG2E
        rate_high, rate_mid, rate_low = [part.astype(F32) for part in pieces(rate, 3)]
        load = flat_ref[pl.ds(ncomp + q * nfac, nfac), :]
        w_high, w_mid, w_low = [part.astype(F32) for part in pieces(load * LOG2E, 3)]
        stack = jnp.concatenate(
            [w_high, w_high, w_high, w_mid, w_mid, w_low, jnp.zeros((LANES - first, LANES), F32)], axis=0
        )
        turned = stack.T
        mix_ref[rows, :] = turned.astype(BF16)
        rate_part = jnp.where(
            (lane >= first) & (lane < first + 3),
            rate_high,
            jnp.where(
                (lane >= first + 3) & (lane < first + 5), rate_mid, jnp.where(lane == first + 5, rate_low, 0.0)
            ),
        )
        left_ref[rows, LANES : 2 * LANES] = (turned - rate_part).astype(BF16)
        load_high, load_mid = pieces(load, 2)
        load_ref[0:nfac, q * LANES : (q + 1) * LANES] = load_high
        load_ref[nfac : 2 * nfac, q * LANES : (q + 1) * LANES] = load_mid


def load_cells(counts_ref, field_ref, logexp_ref, right_ref, wide_ref):
    share, ncat, cols = counts_ref.shape
    nfac = field_ref.shape[1]
    exposure = jnp.exp(logexp_ref[...])
    sub = lax.broadcasted_iota(jnp.int32, (LANES - 6 * nfac, cols), 0)
    for r in range(share):
        count = counts_ref[r]
        high, mid, low = pieces(field_ref[r], 3)
        e_high, e_mid, e_low = [part.astype(F32) for part in pieces(exposure[r : r + 1, :], 3)]
        e_rows = jnp.where((sub == 0) | (sub == 3) | (sub == 5), e_high, 0.0)
        e_rows = jnp.where((sub == 1) | (sub == 4), e_mid, e_rows)
        e_rows = jnp.where(sub == 2, e_low, e_rows).astype(BF16)
        extra = jnp.concatenate([high, mid, low, high, mid, high, e_rows], axis=0)
        right_ref[r, 0:ncat, :] = count
        right_ref[r, LANES : 2 * LANES, :] = extra
        right_ref[r, 2 * LANES : 2 * LANES + ncat, :] = count
        right_ref[r, 3 * LANES : 3 * LANES + ncat, :] = count
        for side in range(2):
            wide_ref[r, 0:ncat, side * cols : (side + 1) * cols] = count
            wide_ref[r, LANES : 2 * LANES, side * cols : (side + 1) * cols] = extra


def load_prior(field_ref, low_ref, high_ref, land, tau_ref, prior_ref):
    share, nfac, cols = field_ref.shape
    row = lax.broadcasted_iota(jnp.int32, (nfac, cols), 0)
    col = lax.broadcasted_iota(jnp.int32, (nfac, cols), 1)
    tau = jnp.zeros((nfac, cols), F32)
    for j in range(nfac):
        tau = jnp.where(row == j, tau_ref[j], tau)
    inner = col < cols - 1
    energy = jnp.zeros((nfac, cols), F32)
    ups = [low_ref[0:nfac, :]] + [field_ref[r] for r in range(share)] + [high_ref[0:nfac, :]]
    lands = [low_ref[nfac : nfac + 1, :]] + [land[r : r + 1, :] for r in range(share)]
    lands = lands + [high_ref[nfac : nfac + 1, :]]
    lands = [jnp.broadcast_to(x, (nfac, cols)) for x in lands]
    for r in range(share):
        here = ups[r + 1]
        step_up = here - ups[r]
        step_down = here - ups[r + 2]
        edge_up = lands[r] * lands[r + 1]
        edge_down = lands[r + 1] * lands[r + 2]
        step_right = here - pltpu.roll(here, cols - 1, 1)
        edge_right = jnp.where(inner, lands[r + 1] * pltpu.roll(lands[r + 1], cols - 1, 1), 0.0)
        flux_right = edge_right * step_right
        flux_down = edge_down * step_down
        laplace = edge_up * step_up + flux_down + flux_right - pltpu.roll(flux_right, 1, 1)
        prior_ref[r] = -tau * (laplace + RIDGE * here)
        energy = energy + 0.5 * tau * (flux_down * step_down + flux_right * step_right + RIDGE * (here * here))
    return energy


def row_shares(
    r, ncomp, right_ref, wide_ref, left_ref, mix_ref, load_ref, land_ref, score_ref, logit_ref, post_ref, gap_ref,
    acc_ref, accw_ref,
):
    cols = right_ref.shape[2]
    nfac = load_ref.shape[0] // 2
    block = 64
    score_ref[...] = dot(left_ref[...], right_ref[r])
    logit_ref[...] = dot(mix_ref[...], right_ref[r, LANES : 2 * LANES, :])
    top_s = jnp.full((8, cols), -jnp.inf, F32)
    top_a = jnp.full((8, cols), -jnp.inf, F32)
    for i in range(0, ncomp, block):
        top_s = jnp.maximum(top_s, jnp.max(score_ref[i : i + block, :].reshape(block // 8, 8, cols), axis=0))
        top_a = jnp.maximum(top_a, jnp.max(logit_ref[i : i + block, :].reshape(block // 8, 8, cols), axis=0))
    top_s = jnp.max(top_s, axis=0, keepdims=True)
    top_a = jnp.max(top_a, axis=0, keepdims=True)
    sum_s = jnp.zeros((8, cols), F32)
    sum_a = jnp.zeros((8, cols), F32)
    for i in range(0, ncomp, block):
        part_s = jnp.exp2(score_ref[i : i + block, :] - top_s)
        part_a = jnp.exp2(logit_ref[i : i + block, :] - top_a)
        score_ref[i : i + block, :] = part_s
        logit_ref[i : i + block, :] = part_a
        sum_s = sum_s + jnp.sum(part_s.reshape(block // 8, 8, cols), axis=0)
        sum_a = sum_a + jnp.sum(part_a.reshape(block // 8, 8, cols), axis=0)
    sum_s = jnp.sum(sum_s, axis=0, keepdims=True)
    sum_a = jnp.sum(sum_a, axis=0, keepdims=True)
    land = land_ref[r][0:1, :]
    inv_s = land / sum_s
    inv_a = land / sum_a
    for i in range(0, ncomp, block):
        post = score_ref[i : i + block, :] * inv_s
        gap = post - logit_ref[i : i + block, :] * inv_a
        for target, values in ((post_ref, post), (gap_ref, gap)):
            high, low = pieces(values, 2)
            target[i : i + block, 0:cols] = high
            target[i : i + block, cols : 2 * cols] = low
    last = ((1,), (1,))
    acc_ref[...] += dot(post_ref[...], wide_ref[r], last)
    accw_ref[...] += dot(gap_ref[...], wide_ref[r, LANES : 2 * LANES, :], last)
    lik = dot(load_ref[...], gap_ref[...])
    lik = lik[0:nfac] + lik[nfac : 2 * nfac]
    lik = lik[:, 0:cols] + lik[:, cols : 2 * cols]
    log_dens = land * (LN2 * ((top_s + jnp.log2(sum_s)) - (top_a + jnp.log2(sum_a))))
    return lik, log_dens


def param_grads(flat_ref, acc_ref, accw_ref, grad_ref, ncomp, nfac):
    lane = lax.broadcasted_iota(jnp.int32, (LANES, LANES), 1)
    rate_lanes = (lane >= 6 * nfac) & (lane < 6 * nfac + 3)
    for q in range(ncomp // LANES):
        rows = pl.ds(q * LANES, LANES)
        mass = jnp.sum(jnp.where(rate_lanes, acc_ref[rows, LANES : 2 * LANES], 0.0), axis=1, keepdims=True)
        grad_ref[rows, :] = acc_ref[rows, 0:LANES] - jnp.exp(flat_ref[rows, :]) * mass
        turned = accw_ref[rows, :].T
        grad_ref[pl.ds(ncomp + q * nfac, nfac), :] = (
            turned[0:nfac] + turned[nfac : 2 * nfac] + turned[2 * nfac : 3 * nfac]
        )


def first_kernel(
    ncomp, rank_ref, tau_ref, counts_ref, field_ref, mom_ref, land_ref, logexp_ref, low_ref, high_ref, pmom_ref, wmom_ref,
    *refs,
):
    ring = ncomp // pmom_ref.shape[0]
    part_refs = refs[:ring]
    (new_ref, half_ref, top_ref, bottom_ref, grad_ref, keep_ref, send_ref) = refs[ring : ring + 7]
    (flat, left, mix, load, right, wide, prior, land_rows, score, logit, post, gap, acc, accw) = refs[ring + 7 :]
    cells_rank, comp_rank = rank_ref[0], rank_ref[1]
    share, nfac, cols = field_ref.shape
    mine = pmom_ref.shape[0]
    for k in range(ring):
        group = comp_rank ^ k
        flat[pl.ds(pl.multiple_of(group * mine, mine), mine), :] = part_refs[k][0:mine, :]
        flat[pl.ds(pl.multiple_of(ncomp + group * nfac, nfac), nfac), :] = part_refs[k][mine : mine + nfac, :]
    land = land_ref[...].astype(F32)
    for r in range(share):
        land_rows[r] = jnp.broadcast_to(land[r : r + 1, :], (8, cols))
    load_params(flat, left, mix, load, ncomp, nfac)
    load_cells(counts_ref, field_ref, logexp_ref, right, wide)
    load_prior(field_ref, low_ref, high_ref, land, tau_ref, prior)
    acc[...] = jnp.zeros_like(acc)
    accw[...] = jnp.zeros_like(accw)

    def step(r, carry):
        lik, _ = row_shares(
            r, ncomp, right, wide, left, mix, load, land_rows, score, logit, post, gap, acc, accw
        )
        prior[r] = prior[r] + lik
        return carry

    lax.fori_loop(0, share, step, 0)
    for r in range(share):
        half = mom_ref[r] + 0.5 * STEP_FIELD * prior[r]
        fresh = field_ref[r] + STEP_FIELD * half
        half_ref[r] = half
        new_ref[r] = fresh
        if r == 0:
            top_ref[...] = fresh
        if r == share - 1:
            bottom_ref[...] = fresh
    param_grads(flat, acc, accw, grad_ref, ncomp, nfac)
    nparam = grad_ref.shape[0]
    if flat.shape[0] > nparam:
        flat[nparam:, :] = jnp.zeros((flat.shape[0] - nparam, LANES), F32)
    flat[0:nparam, :] = 0.5 * STEP_PARAM * STEP_PARAM * grad_ref[...]
    own_prof, own_load = part_refs[0][0:mine, :], part_refs[0][mine : mine + nfac, :]
    owner = cells_rank == 0
    base_prof = own_prof + STEP_PARAM * (pmom_ref[...] - 0.5 * STEP_PARAM * 0.25 * own_prof)
    base_load = own_load + STEP_PARAM * (wmom_ref[...] - 0.5 * STEP_PARAM * own_load)
    flat[pl.ds(pl.multiple_of(comp_rank * mine, mine), mine), :] += jnp.where(owner, base_prof, 0.0)
    flat[pl.ds(pl.multiple_of(ncomp + comp_rank * nfac, nfac), nfac), :] += jnp.where(owner, base_load, 0.0)
    spread_chunks(flat, keep_ref, send_ref, cells_rank)


def second_kernel(
    ncomp, rank_ref, tau_ref, counts_ref, field_ref, half_ref, land_ref, logexp_ref, low_ref, high_ref, pmom_ref, wmom_ref,
    own_ref, near_ref, far_ref, grad0_ref, mom_ref, prof_ref, mixing_ref, keep_ref, send_ref,
    flat, left, mix, load, right, wide, prior, land_rows, score, logit, post, gap, acc, accw, out, grad,
):
    cells_rank, comp_rank = rank_ref[0], rank_ref[1]
    share, nfac, cols = field_ref.shape
    mine = pmom_ref.shape[0]
    nparam = grad0_ref.shape[0]
    gather_chunks(flat, near_ref, far_ref, cells_rank)
    new_prof = flat[pl.ds(pl.multiple_of(comp_rank * mine, mine), mine), :]
    new_load = flat[pl.ds(pl.multiple_of(ncomp + comp_rank * nfac, nfac), nfac), :]
    prof_ref[...] = new_prof
    mixing_ref[...] = new_load
    land = land_ref[...].astype(F32)
    for r in range(share):
        land_rows[r] = jnp.broadcast_to(land[r : r + 1, :], (8, cols))
    load_params(flat, left, mix, load, ncomp, nfac)
    load_cells(counts_ref, field_ref, logexp_ref, right, wide)
    energy = load_prior(field_ref, low_ref, high_ref, land, tau_ref, prior)
    acc[...] = jnp.zeros_like(acc)
    accw[...] = jnp.zeros_like(accw)

    def step(r, log_dens):
        lik, part = row_shares(
            r, ncomp, right, wide, left, mix, load, land_rows, score, logit, post, gap, acc, accw
        )
        prior[r] = prior[r] + lik
        return log_dens + part

    log_dens = lax.fori_loop(0, share, step, jnp.zeros((1, cols), F32))
    for r in range(share):
        fresh = half_ref[r] + 0.5 * STEP_FIELD * prior[r]
        mom_ref[r] = fresh
        energy = energy + 0.5 * (fresh * fresh)
    param_grads(flat, acc, accw, grad, ncomp, nfac)
    first_device = (cells_rank == 0) & (comp_rank == 0)
    prof_all = flat[0:ncomp, :]
    load_all = flat[ncomp:nparam, :]
    param_energy = jnp.sum(0.125 * (prof_all * prof_all)) + jnp.sum(0.5 * (load_all * load_all))
    total = jnp.sum(energy) - jnp.sum(log_dens) + jnp.where(first_device, param_energy, 0.0)
    out[0:nparam, :] = 0.5 * STEP_PARAM * (grad0_ref[...] + grad[...])
    tail = out.shape[0] - nparam
    spot = lax.broadcasted_iota(jnp.int32, (tail, LANES), 0) + lax.broadcasted_iota(jnp.int32, (tail, LANES), 1)
    out[nparam:, :] = jnp.where(spot == 0, total, 0.0)
    owner = cells_rank == 0
    old_prof, old_load = own_ref[0:mine, :], own_ref[mine : mine + nfac, :]
    base_prof = pmom_ref[...] - 0.5 * STEP_PARAM * 0.25 * (old_prof + new_prof)
    base_load = wmom_ref[...] - 0.5 * STEP_PARAM * (old_load + new_load)
    out[pl.ds(pl.multiple_of(comp_rank * mine, mine), mine), :] += jnp.where(owner, base_prof, 0.0)
    out[pl.ds(pl.multiple_of(ncomp + comp_rank * nfac, nfac), nfac), :] += jnp.where(owner, base_load, 0.0)
    spread_chunks(out, keep_ref, send_ref, cells_rank)


def last_kernel(ncomp, nparam, cells, rank_ref, near_ref, far_ref, prof_ref, mixing_ref, ham_ref, flat):
    cells_rank, comp_rank = rank_ref[0], rank_ref[1]
    mine, nfac = prof_ref.shape[0], mixing_ref.shape[0]
    gather_chunks(flat, near_ref, far_ref, cells_rank)
    prof_ref[...] = flat[pl.ds(pl.multiple_of(comp_rank * mine, mine), mine), :]
    mixing_ref[...] = flat[pl.ds(pl.multiple_of(ncomp + comp_rank * nfac, nfac), nfac), :]
    momenta = flat[0:nparam, :]
    rest = flat[nparam:, :]
    ham_ref[0, 0] = (0.5 * jnp.sum(momenta * momenta) + jnp.sum(rest)) / cells


def fast_device(
    factor_field, profile, mixing, factor_mom, profile_mom, mixing_mom, field_tau, counts, land_mask, log_exposure
):
    nfac, share, cols = factor_field.shape
    mine, ncat = profile.shape
    tile_rows = land_mask.shape[0]
    ring = lax.axis_size("comp")
    tiles = lax.axis_size("cells")
    ncomp = mine * ring
    nparam = ncomp + nfac * ncomp // LANES
    pairs = tiles // 2
    round_up = lambda rows: -(-rows // (8 * tiles)) * 8
    chunk_one = round_up(nparam)
    chunk_two = round_up(nparam + 1)
    comp_rank = lax.axis_index("comp")
    cells_rank = lax.axis_index("cells")
    ranks = jnp.stack([cells_rank, comp_rank]).astype(jnp.int32)
    pack = jnp.concatenate([profile, mixing], axis=0)
    parts = [pack] + [partner(pack, "comp", k) for k in range(1, ring)]

    count_rows = lax.dynamic_slice_in_dim(counts, comp_rank * share, share, 1).swapaxes(0, 1).astype(BF16)
    field_rows = factor_field.swapaxes(0, 1)
    mom_rows = factor_mom.swapaxes(0, 1)
    both = ("cells", "comp")
    last = tiles * ring - 1
    forward = [(i, i + 1) for i in range(last)]
    backward = [(i + 1, i) for i in range(last)]
    land_edge = lambda row: lax.dynamic_slice_in_dim(land_mask, row, 1, 0).astype(F32)
    edges = [
        jnp.concatenate([factor_field[:, r, :], jnp.broadcast_to(land_edge(comp_rank * share + r), (8, cols))], axis=0)
        for r in (share - 1, 0)
    ]
    low = lax.ppermute(edges[0], both, forward)
    high = lax.ppermute(edges[1], both, backward)

    def full(*shape):
        zeros = (0,) * len(shape)
        return pl.BlockSpec(shape, lambda i, ranks: zeros)

    smem = pl.BlockSpec(memory_space=pltpu.SMEM)
    cell_specs = [
        smem,
        full(share, ncat, cols),
        full(share, nfac, cols),
    ]
    row_spec = pl.BlockSpec((share, cols), lambda i, ranks: (ranks[1], 0))
    edge_spec = full(nfac + 8, cols)
    param_specs = [full(mine, ncat), full(nfac, mine)]
    pack_spec = full(mine + nfac, ncat)
    shape = lambda *dims: jax.ShapeDtypeStruct(dims, F32)
    work = [
        pltpu.VMEM((ncomp, 4 * LANES), BF16),
        pltpu.VMEM((ncomp, LANES), BF16),
        pltpu.VMEM((2 * nfac, ncomp), BF16),
        pltpu.VMEM((share, 4 * LANES, cols), BF16),
        pltpu.VMEM((share, 2 * LANES, 2 * cols), BF16),
        pltpu.VMEM((share, nfac, cols), F32),
        pltpu.VMEM((share, 8, cols), F32),
        pltpu.VMEM((ncomp, cols), F32),
        pltpu.VMEM((ncomp, cols), F32),
        pltpu.VMEM((ncomp, 2 * cols), BF16),
        pltpu.VMEM((ncomp, 2 * cols), BF16),
        pltpu.VMEM((ncomp, 2 * LANES), F32),
        pltpu.VMEM((ncomp, LANES), F32),
    ]
    params = pltpu.CompilerParams(vmem_limit_bytes=40 * 1024 * 1024, dimension_semantics=("arbitrary",))

    def call(body, name, ins, outs, scratch):
        return pl.pallas_call(
            body,
            name=name,
            grid_spec=pltpu.PrefetchScalarGridSpec(
                num_scalar_prefetch=1,
                grid=(1,),
                in_specs=ins,
                out_specs=[spec for spec, _ in outs],
                scratch_shapes=scratch,
            ),
            out_shape=[out for _, out in outs],
            compiler_params=params,
        )

    def block(*dims):
        return (full(*dims), shape(*dims))

    first = call(
        functools.partial(first_kernel, ncomp),
        "first_gradient",
        cell_specs + [full(share, nfac, cols), row_spec, row_spec, edge_spec, edge_spec] + param_specs + [pack_spec] * ring,
        [
            block(share, nfac, cols),
            block(share, nfac, cols),
            block(nfac, cols),
            block(nfac, cols),
            block(nparam, LANES),
            block(pairs, chunk_one, LANES),
            block(pairs, chunk_one, LANES),
        ],
        [pltpu.VMEM((tiles * chunk_one, LANES), F32)] + work,
    )
    new_field, half, top, bottom, grad, keep, send = first(
        ranks, field_tau, count_rows, field_rows, mom_rows, land_mask, log_exposure, low, high, profile_mom, mixing_mom,
        *parts,
    )
    low_next = jnp.concatenate([lax.ppermute(bottom, both, forward), low[nfac:]], axis=0)
    high_next = jnp.concatenate([lax.ppermute(top, both, backward), high[nfac:]], axis=0)
    near, far = all_sum(keep, send)
    second = call(
        functools.partial(second_kernel, ncomp),
        "second_gradient",
        cell_specs
        + [full(share, nfac, cols), row_spec, row_spec, edge_spec, edge_spec]
        + param_specs
        + [pack_spec, full(pairs, chunk_one, LANES), full(pairs, chunk_one, LANES), full(nparam, LANES)],
        [
            block(share, nfac, cols),
            block(mine, ncat),
            block(nfac, mine),
            block(pairs, chunk_two, LANES),
            block(pairs, chunk_two, LANES),
        ],
        [pltpu.VMEM((tiles * chunk_one, LANES), F32)]
        + work
        + [pltpu.VMEM((tiles * chunk_two, LANES), F32), pltpu.VMEM((nparam, LANES), F32)],
    )
    new_mom, new_profile, new_mixing, keep, send = second(
        ranks, field_tau, count_rows, new_field, half, land_mask, log_exposure, low_next, high_next, profile_mom, mixing_mom,
        pack, near, far, grad,
    )
    near, far = all_sum(keep, send)
    final = call(
        functools.partial(last_kernel, ncomp, nparam, tile_rows * cols * tiles),
        "momenta",
        [full(pairs, chunk_two, LANES), full(pairs, chunk_two, LANES)],
        [block(mine, ncat), block(nfac, mine), (smem, shape(1, 1))],
        [pltpu.VMEM((tiles * chunk_two, LANES), F32)],
    )
    new_profile_mom, new_mixing_mom, hamiltonian = final(ranks, near, far)
    return (
        new_field.swapaxes(0, 1),
        new_profile,
        new_mixing,
        new_mom.swapaxes(0, 1),
        new_profile_mom,
        new_mixing_mom,
        hamiltonian.reshape(()),
    )


def power_of_two(count):
    return count & (count - 1) == 0


def choose_device(*args):
    factor_field, profile, mixing = args[:3]
    nfac, share, cols = factor_field.shape
    mine, ncat = profile.shape
    tiles, ring = lax.axis_size("cells"), lax.axis_size("comp")
    fits = mine == LANES and ncat == LANES and nfac % 16 == 0 and 6 * nfac + 6 <= LANES
    fits = fits and share == 8 and cols % LANES == 0
    fits = fits and power_of_two(tiles) and tiles > 1 and power_of_two(ring)
    return fast_device(*args) if fits else plain_device(*args)


def solution(mesh):
    in_specs = (
        P(None, ("cells", "comp"), None),
        P("comp", None),
        P(None, "comp"),
        P(None, ("cells", "comp"), None),
        P("comp", None),
        P(None, "comp"),
        P(),
        P(None, "cells", None),
        P("cells", None),
        P("cells", None),
    )
    out_specs = (
        P(None, ("cells", "comp"), None),
        P("comp", None),
        P(None, "comp"),
        P(None, ("cells", "comp"), None),
        P("comp", None),
        P(None, "comp"),
        P(),
    )
    return jax.shard_map(
        choose_device, mesh=mesh, in_specs=in_specs, out_specs=out_specs, check_vma=False
    )
```

```python
import functools
import math

import jax
import jax.numpy as jnp
from jax import lax
from jax.experimental import pallas as pl
from jax.experimental.pallas import tpu as pltpu
from jax.sharding import PartitionSpec as P


def extended(cells, sides, width):
    for axis, dim in sides:
        count = lax.axis_size(axis)
        ends = count - 1
        head = lax.slice_in_dim(cells, 0, width, axis=dim)
        tail = lax.slice_in_dim(cells, cells.shape[dim] - width, cells.shape[dim], axis=dim)
        cells = jnp.concatenate(
            [
                lax.ppermute(tail, axis, [(i, (i + 1) % count) for i in range(ends)]),
                cells,
                lax.ppermute(head, axis, [((i + 1) % count, i) for i in range(ends)]),
            ],
            axis=dim,
        )
    return cells


def field_prior(padded, land_pad, field_tau):
    ridge = 0.1
    step_x = padded[:, 1:, :] - padded[:, :-1, :]
    edge_x = land_pad[1:, :] * land_pad[:-1, :]
    flux_x = edge_x[None, :, :] * step_x
    centre = padded[:, 1:-1, :]
    land_mid = land_pad[1:-1, :]
    step_y = centre[:, :, 1:] - centre[:, :, :-1]
    edge_y = land_mid[:, 1:] * land_mid[:, :-1]
    flux_y = edge_y[None, :, :] * step_y
    lap_x = flux_x[:, :-1, :] - flux_x[:, 1:, :]
    lap_y = jnp.pad(flux_y, ((0, 0), (0, 0), (1, 0))) - jnp.pad(flux_y, ((0, 0), (0, 0), (0, 1)))
    tau_cube = field_tau[:, None, None]
    grad = -tau_cube * (lap_x + lap_y + ridge * centre)
    energy = 0.5 * jnp.sum(tau_cube * (flux_x[:, 1:, :] * step_x[:, 1:, :]))
    energy = energy + 0.5 * jnp.sum(tau_cube * (flux_y * step_y))
    energy = energy + 0.5 * ridge * jnp.sum(tau_cube * (centre * centre))
    return (grad, energy)


def tile_scores(flat_tile, count_rows, exposure, profile, mixing):
    prof_exp = jnp.exp(profile)
    rate_total = jnp.sum(prof_exp, axis=1)
    mix_logit = jnp.dot(mixing.T, flat_tile, precision=lax.Precision.HIGHEST)
    fit_score = (
        jnp.dot(profile, count_rows, precision=lax.Precision.HIGHEST)
        - rate_total[:, None] * exposure[None, :]
    )
    return (mix_logit, mix_logit + fit_score)


def tile_grads(
    flat_tile, count_rows, land_weight, exposure, mixing, mix_logit, joint_score, log_mix, log_joint
):
    prior_share = jnp.exp(mix_logit - log_mix[None, :])
    posterior = jnp.exp(joint_score - log_joint[None, :])
    post_land = posterior * land_weight[None, :]
    gap_weight = (posterior - prior_share) * land_weight[None, :]
    grad_counts = jnp.dot(post_land, count_rows.T, precision=lax.Precision.HIGHEST)
    rate_mass = jnp.sum(post_land * exposure[None, :], axis=1)
    grad_mix = jnp.dot(flat_tile, gap_weight.T, precision=lax.Precision.HIGHEST)
    field_lik = jnp.dot(mixing, gap_weight, precision=lax.Precision.HIGHEST)
    log_dens = jnp.sum(land_weight * (log_joint - log_mix))
    return (grad_counts, rate_mass, grad_mix, field_lik, log_dens)


def log_sum(scores):
    top = jnp.max(scores, axis=0)
    return top + jnp.log(jnp.sum(jnp.exp(scores - top[None, :]), axis=0))


def plain_device(
    factor_field,
    profile,
    mixing,
    factor_mom,
    profile_mom,
    mixing_mom,
    field_tau,
    counts,
    land_mask,
    log_exposure,
):
    step_field = 0.05
    step_profile = 0.002
    step_mixing = 0.002
    tile_rows, tile_cols = land_mask.shape
    ncat = counts.shape[0]
    share_rows = factor_field.shape[1]
    comp_rank = lax.axis_index("comp")
    cells_rank = lax.axis_index("cells")
    first_cells = cells_rank == 0
    land_pad = extended(land_mask, (("cells", 0),), 1).astype(jnp.float32)
    row_start = comp_rank * share_rows
    count_rows = lax.dynamic_slice_in_dim(counts, row_start, share_rows, 1)
    count_rows = count_rows.reshape(ncat, share_rows * tile_cols).astype(jnp.float32)
    land_weight = (
        lax.dynamic_slice_in_dim(land_mask, row_start, share_rows, 0)
        .reshape(-1)
        .astype(jnp.float32)
    )
    exposure = jnp.exp(lax.dynamic_slice_in_dim(log_exposure, row_start, share_rows, 0).reshape(-1))
    land_near = lax.dynamic_slice_in_dim(land_pad, row_start, share_rows + 2, 0)

    def evaluate(share_field, profile_now, mixing_now):
        padded = extended(share_field, ((("cells", "comp"), 1),), 1)
        prior_grad, prior_energy = field_prior(padded, land_near, field_tau)
        profile_all, mixing_all = (
            lax.all_gather(profile_now, "comp", axis=0, tiled=True),
            lax.all_gather(mixing_now, "comp", axis=1, tiled=True),
        )
        flat_tile = share_field.reshape(share_field.shape[0], -1)
        mix_logit, joint_score = tile_scores(
            flat_tile, count_rows, exposure, profile_all, mixing_all
        )
        log_mix = log_sum(mix_logit)
        log_joint = log_sum(joint_score)
        grad_counts, rate_mass, grad_mix, field_lik, log_dens = tile_grads(
            flat_tile,
            count_rows,
            land_weight,
            exposure,
            mixing_all,
            mix_logit,
            joint_score,
            log_mix,
            log_joint,
        )
        grad_counts, rate_mass, mix_rows = (
            lax.psum_scatter(grad_counts, "comp", scatter_dimension=0, tiled=True),
            lax.psum_scatter(rate_mass, "comp", scatter_dimension=0, tiled=True),
            lax.psum_scatter(grad_mix.T, "comp", scatter_dimension=0, tiled=True),
        )
        grad_mix = mix_rows.T
        grad_field = prior_grad + field_lik.reshape(share_field.shape)
        log_part = log_dens - prior_energy
        grad_counts, rate_mass, grad_mix = lax.psum((grad_counts, rate_mass, grad_mix), "cells")
        grad_profile = grad_counts - jnp.exp(profile_now) * rate_mass[:, None] - 0.25 * profile_now
        grad_mixing = grad_mix - mixing_now
        param_prior = -0.125 * jnp.sum(profile_now * profile_now) - 0.5 * jnp.sum(
            mixing_now * mixing_now
        )
        log_part = log_part + jnp.where(first_cells, param_prior, 0.0)
        return (log_part, grad_field, grad_profile, grad_mixing)

    first = evaluate(factor_field, profile, mixing)
    half_field = factor_mom + 0.5 * step_field * first[1]
    half_profile = profile_mom + 0.5 * step_profile * first[2]
    half_mixing = mixing_mom + 0.5 * step_mixing * first[3]
    new_field = factor_field + step_field * half_field
    new_profile = profile + step_profile * half_profile
    new_mixing = mixing + step_mixing * half_mixing
    second = evaluate(new_field, new_profile, new_mixing)
    new_factor_mom = half_field + 0.5 * step_field * second[1]
    new_profile_mom = half_profile + 0.5 * step_profile * second[2]
    new_mixing_mom = half_mixing + 0.5 * step_mixing * second[3]
    kinetic = 0.5 * jnp.sum(new_factor_mom * new_factor_mom)
    kinetic = kinetic + jnp.where(
        first_cells,
        0.5
        * (jnp.sum(new_profile_mom * new_profile_mom) + jnp.sum(new_mixing_mom * new_mixing_mom)),
        0.0,
    )
    log_total, kinetic_total = lax.psum((second[0], kinetic), ("cells", "comp"))
    cell_count = tile_rows * tile_cols * lax.axis_size("cells")
    hamiltonian = (kinetic_total - log_total) / cell_count
    return (
        new_field,
        new_profile,
        new_mixing,
        new_factor_mom,
        new_profile_mom,
        new_mixing_mom,
        hamiltonian,
    )


STEP_FIELD = 0.05
STEP_PARAM = 0.002
RIDGE = 0.1
LOG2E = math.log2(math.e)
LN2 = math.log(2.0)
LANES = 128
F32 = jnp.float32
BF16 = jnp.bfloat16


def pieces(values, count):
    parts = []
    for _ in range(count):
        part = values.astype(BF16)
        parts.append(part)
        values = values - part.astype(F32)
    return parts


def dot(left, right, dims=((1,), (0,))):
    return lax.dot_general(left, right, (dims, ((), ())), preferred_element_type=F32)


def partner(values, axis, flip):
    count = lax.axis_size(axis)
    return lax.ppermute(values, axis, [(i, i ^ flip) for i in range(count)])


def all_sum(keep, send):
    pairs = keep.shape[0]
    ring = lax.axis_size("comp")
    chunks = keep + partner(send, "cells", 1)
    total = chunks[0]
    for part in [partner(chunks[k], "cells", 2 * k) for k in range(1, pairs)]:
        total = total + part
    parts = [partner(total, "comp", k) for k in range(1, ring)]
    for part in parts:
        total = total + part
    near = jnp.stack([total] + [partner(total, "cells", 2 * k) for k in range(1, pairs)])
    return near, partner(near, "cells", 1)


def chunk_index(cells_rank, k, other):
    core = cells_rank % 2
    return (((cells_rank // 2) ^ k) * 2) + (1 - core if other else core)


def gather_chunks(flat_ref, near_ref, far_ref, cells_rank):
    pairs, rows, _ = near_ref.shape
    for k in range(pairs):
        for source, other in ((near_ref, False), (far_ref, True)):
            start = pl.multiple_of(chunk_index(cells_rank, k, other) * rows, 8)
            flat_ref[pl.ds(start, rows), :] = source[k]


def spread_chunks(flat_ref, keep_ref, send_ref, cells_rank):
    pairs, rows, _ = keep_ref.shape
    for k in range(pairs):
        for target, other in ((keep_ref, False), (send_ref, True)):
            start = pl.multiple_of(chunk_index(cells_rank, k, other) * rows, 8)
            target[k] = flat_ref[pl.ds(start, rows), :]


def load_params(flat_ref, left_ref, mix_ref, load_ref, ncomp, nfac):
    lane = lax.broadcasted_iota(jnp.int32, (LANES, LANES), 1)
    first = 6 * nfac
    for q in range(ncomp // LANES):
        rows = pl.ds(q * LANES, LANES)
        prof = flat_ref[rows, :]
        high, mid, low = pieces(prof * LOG2E, 3)
        left_ref[rows, 0:LANES] = high
        left_ref[rows, 2 * LANES : 3 * LANES] = mid
        left_ref[rows, 3 * LANES : 4 * LANES] = low
        rate = jnp.sum(jnp.exp(prof), axis=1, keepdims=True) * LOG2E
        rate_high, rate_mid, rate_low = [part.astype(F32) for part in pieces(rate, 3)]
        load = flat_ref[pl.ds(ncomp + q * nfac, nfac), :]
        w_high, w_mid, w_low = [part.astype(F32) for part in pieces(load * LOG2E, 3)]
        stack = jnp.concatenate(
            [w_high, w_high, w_high, w_mid, w_mid, w_low, jnp.zeros((LANES - first, LANES), F32)], axis=0
        )
        turned = stack.T
        mix_ref[rows, :] = turned.astype(BF16)
        rate_part = jnp.where(
            (lane >= first) & (lane < first + 3),
            rate_high,
            jnp.where(
                (lane >= first + 3) & (lane < first + 5), rate_mid, jnp.where(lane == first + 5, rate_low, 0.0)
            ),
        )
        left_ref[rows, LANES : 2 * LANES] = (turned - rate_part).astype(BF16)
        load_high, load_mid = pieces(load, 2)
        load_ref[0:nfac, q * LANES : (q + 1) * LANES] = load_high
        load_ref[nfac : 2 * nfac, q * LANES : (q + 1) * LANES] = load_mid


def load_cells(counts_ref, field_ref, logexp_ref, right_ref, wide_ref):
    share, ncat, cols = counts_ref.shape
    nfac = field_ref.shape[1]
    exposure = jnp.exp(logexp_ref[...])
    sub = lax.broadcasted_iota(jnp.int32, (LANES - 6 * nfac, cols), 0)
    for r in range(share):
        count = counts_ref[r]
        high, mid, low = pieces(field_ref[r], 3)
        e_high, e_mid, e_low = [part.astype(F32) for part in pieces(exposure[r : r + 1, :], 3)]
        e_rows = jnp.where((sub == 0) | (sub == 3) | (sub == 5), e_high, 0.0)
        e_rows = jnp.where((sub == 1) | (sub == 4), e_mid, e_rows)
        e_rows = jnp.where(sub == 2, e_low, e_rows).astype(BF16)
        extra = jnp.concatenate([high, mid, low, high, mid, high, e_rows], axis=0)
        right_ref[r, 0:ncat, :] = count
        right_ref[r, LANES : 2 * LANES, :] = extra
        right_ref[r, 2 * LANES : 2 * LANES + ncat, :] = count
        right_ref[r, 3 * LANES : 3 * LANES + ncat, :] = count
        for side in range(2):
            wide_ref[r, 0:ncat, side * cols : (side + 1) * cols] = count
            wide_ref[r, LANES : 2 * LANES, side * cols : (side + 1) * cols] = extra


def load_prior(field_ref, low_ref, high_ref, land, tau_ref, prior_ref):
    share, nfac, cols = field_ref.shape
    row = lax.broadcasted_iota(jnp.int32, (nfac, cols), 0)
    col = lax.broadcasted_iota(jnp.int32, (nfac, cols), 1)
    tau = jnp.zeros((nfac, cols), F32)
    for j in range(nfac):
        tau = jnp.where(row == j, tau_ref[j], tau)
    inner = col < cols - 1
    energy = jnp.zeros((nfac, cols), F32)
    ups = [low_ref[0:nfac, :]] + [field_ref[r] for r in range(share)] + [high_ref[0:nfac, :]]
    lands = [low_ref[nfac : nfac + 1, :]] + [land[r : r + 1, :] for r in range(share)]
    lands = lands + [high_ref[nfac : nfac + 1, :]]
    lands = [jnp.broadcast_to(x, (nfac, cols)) for x in lands]
    for r in range(share):
        here = ups[r + 1]
        step_up = here - ups[r]
        step_down = here - ups[r + 2]
        edge_up = lands[r] * lands[r + 1]
        edge_down = lands[r + 1] * lands[r + 2]
        step_right = here - pltpu.roll(here, cols - 1, 1)
        edge_right = jnp.where(inner, lands[r + 1] * pltpu.roll(lands[r + 1], cols - 1, 1), 0.0)
        flux_right = edge_right * step_right
        flux_down = edge_down * step_down
        laplace = edge_up * step_up + flux_down + flux_right - pltpu.roll(flux_right, 1, 1)
        prior_ref[r] = -tau * (laplace + RIDGE * here)
        energy = energy + 0.5 * tau * (flux_down * step_down + flux_right * step_right + RIDGE * (here * here))
    return energy


def row_scores(r, right_ref, left_ref, mix_ref, score_ref, logit_ref):
    tops = []
    for target, values in (
        (score_ref, dot(left_ref[...], right_ref[r])),
        (logit_ref, dot(mix_ref[...], right_ref[r, LANES : 2 * LANES, :])),
    ):
        target[...] = values
        ncomp, cols = values.shape
        tops.append(jnp.max(jnp.max(values.reshape(ncomp // 8, 8, cols), axis=0), axis=0, keepdims=True))
    return tops


def row_shares(tops, land, score_ref, logit_ref, post_ref, gap_ref):
    ncomp, cols = score_ref.shape
    block = 32
    top_s, top_a = tops
    sum_s = jnp.zeros((8, cols), F32)
    sum_a = jnp.zeros((8, cols), F32)
    for i in range(0, ncomp, block):
        part_s = jnp.exp2(score_ref[i : i + block, :] - top_s)
        part_a = jnp.exp2(logit_ref[i : i + block, :] - top_a)
        score_ref[i : i + block, :] = part_s
        logit_ref[i : i + block, :] = part_a
        sum_s = sum_s + jnp.sum(part_s.reshape(block // 8, 8, cols), axis=0)
        sum_a = sum_a + jnp.sum(part_a.reshape(block // 8, 8, cols), axis=0)
    sum_s = jnp.sum(sum_s, axis=0, keepdims=True)
    sum_a = jnp.sum(sum_a, axis=0, keepdims=True)
    log_s = top_s + jnp.log2(sum_s)
    log_a = top_a + jnp.log2(sum_a)
    inv_s = land / sum_s
    inv_a = land / sum_a
    for i in range(0, ncomp, block):
        post = score_ref[i : i + block, :] * inv_s
        gap = post - logit_ref[i : i + block, :] * inv_a
        for target, values in ((post_ref, post), (gap_ref, gap)):
            high, low = pieces(values, 2)
            target[i : i + block, 0:cols] = high
            target[i : i + block, cols : 2 * cols] = low
    return land * (LN2 * (log_s - log_a))


def row_products(r, wide_ref, load_ref, post_ref, gap_ref, acc_ref, accw_ref, prior_ref):
    nfac = load_ref.shape[0] // 2
    cols = prior_ref.shape[2]
    last = ((1,), (1,))
    acc = dot(post_ref[...], wide_ref[r], last)
    accw = dot(gap_ref[...], wide_ref[r, LANES : 2 * LANES, :], last)
    if r == 0:
        acc_ref[...] = acc
        accw_ref[...] = accw
    else:
        acc_ref[...] += acc
        accw_ref[...] += accw
    lik = dot(load_ref[...], gap_ref[...])
    lik = lik[0:nfac] + lik[nfac : 2 * nfac]
    prior_ref[r] += lik[:, 0:cols] + lik[:, cols : 2 * cols]


def all_rows(land, right, wide, left, mix, load, scores, logits, posts, gaps, acc, accw, prior):
    share, _, cols = prior.shape
    log_dens = jnp.zeros((1, cols), F32)
    tops = {}
    for r in range(share + 2):
        if r < share:
            tops[r] = row_scores(r, right, left, mix, scores[r % 2], logits[r % 2])
        if 0 <= r - 1 < share:
            p = r - 1
            log_dens = log_dens + row_shares(
                tops[p], land[p : p + 1, :], scores[p % 2], logits[p % 2], posts[p % 2], gaps[p % 2]
            )
        if 0 <= r - 2:
            p = r - 2
            row_products(p, wide, load, posts[p % 2], gaps[p % 2], acc, accw, prior)
    return log_dens


def param_grads(flat_ref, acc_ref, accw_ref, grad_ref, ncomp, nfac):
    lane = lax.broadcasted_iota(jnp.int32, (LANES, LANES), 1)
    rate_lanes = (lane >= 6 * nfac) & (lane < 6 * nfac + 3)
    for q in range(ncomp // LANES):
        rows = pl.ds(q * LANES, LANES)
        mass = jnp.sum(jnp.where(rate_lanes, acc_ref[rows, LANES : 2 * LANES], 0.0), axis=1, keepdims=True)
        grad_ref[rows, :] = acc_ref[rows, 0:LANES] - jnp.exp(flat_ref[rows, :]) * mass
        turned = accw_ref[rows, :].T
        grad_ref[pl.ds(ncomp + q * nfac, nfac), :] = (
            turned[0:nfac] + turned[nfac : 2 * nfac] + turned[2 * nfac : 3 * nfac]
        )


def first_kernel(
    ncomp, rank_ref, tau_ref, counts_ref, field_ref, mom_ref, land_ref, logexp_ref, low_ref, high_ref, pmom_ref, wmom_ref,
    *refs,
):
    ring = ncomp // pmom_ref.shape[0]
    part_refs = refs[:ring]
    (new_ref, half_ref, top_ref, bottom_ref, grad_ref, keep_ref, send_ref) = refs[ring : ring + 7]
    (flat, left, mix, load, right, wide, prior, score0, score1, logit0, logit1, post0, post1, gap0, gap1, acc, accw) = (
        refs[ring + 7 :]
    )
    cells_rank, comp_rank = rank_ref[0], rank_ref[1]
    share, nfac, cols = field_ref.shape
    mine = pmom_ref.shape[0]
    for k in range(ring):
        group = comp_rank ^ k
        flat[pl.ds(pl.multiple_of(group * mine, mine), mine), :] = part_refs[k][0:mine, :]
        flat[pl.ds(pl.multiple_of(ncomp + group * nfac, nfac), nfac), :] = part_refs[k][mine : mine + nfac, :]
    land = land_ref[...].astype(F32)
    load_params(flat, left, mix, load, ncomp, nfac)
    load_cells(counts_ref, field_ref, logexp_ref, right, wide)
    load_prior(field_ref, low_ref, high_ref, land, tau_ref, prior)

    all_rows(
        land, right, wide, left, mix, load, (score0, score1), (logit0, logit1), (post0, post1), (gap0, gap1), acc, accw,
        prior,
    )
    for r in range(share):
        half = mom_ref[r] + 0.5 * STEP_FIELD * prior[r]
        fresh = field_ref[r] + STEP_FIELD * half
        half_ref[r] = half
        new_ref[r] = fresh
        if r == 0:
            top_ref[...] = fresh
        if r == share - 1:
            bottom_ref[...] = fresh
    param_grads(flat, acc, accw, grad_ref, ncomp, nfac)
    nparam = grad_ref.shape[0]
    if flat.shape[0] > nparam:
        flat[nparam:, :] = jnp.zeros((flat.shape[0] - nparam, LANES), F32)
    flat[0:nparam, :] = 0.5 * STEP_PARAM * STEP_PARAM * grad_ref[...]
    own_prof, own_load = part_refs[0][0:mine, :], part_refs[0][mine : mine + nfac, :]
    owner = cells_rank == 0
    base_prof = own_prof + STEP_PARAM * (pmom_ref[...] - 0.5 * STEP_PARAM * 0.25 * own_prof)
    base_load = own_load + STEP_PARAM * (wmom_ref[...] - 0.5 * STEP_PARAM * own_load)
    flat[pl.ds(pl.multiple_of(comp_rank * mine, mine), mine), :] += jnp.where(owner, base_prof, 0.0)
    flat[pl.ds(pl.multiple_of(ncomp + comp_rank * nfac, nfac), nfac), :] += jnp.where(owner, base_load, 0.0)
    spread_chunks(flat, keep_ref, send_ref, cells_rank)


def second_kernel(
    ncomp, rank_ref, tau_ref, counts_ref, field_ref, half_ref, land_ref, logexp_ref, low_ref, high_ref, pmom_ref, wmom_ref,
    own_ref, near_ref, far_ref, grad0_ref, mom_ref, prof_ref, mixing_ref, keep_ref, send_ref,
    flat, left, mix, load, right, wide, prior, score0, score1, logit0, logit1, post0, post1, gap0, gap1, acc, accw, out,
    grad,
):
    cells_rank, comp_rank = rank_ref[0], rank_ref[1]
    share, nfac, cols = field_ref.shape
    mine = pmom_ref.shape[0]
    nparam = grad0_ref.shape[0]
    gather_chunks(flat, near_ref, far_ref, cells_rank)
    new_prof = flat[pl.ds(pl.multiple_of(comp_rank * mine, mine), mine), :]
    new_load = flat[pl.ds(pl.multiple_of(ncomp + comp_rank * nfac, nfac), nfac), :]
    prof_ref[...] = new_prof
    mixing_ref[...] = new_load
    land = land_ref[...].astype(F32)
    load_params(flat, left, mix, load, ncomp, nfac)
    load_cells(counts_ref, field_ref, logexp_ref, right, wide)
    energy = load_prior(field_ref, low_ref, high_ref, land, tau_ref, prior)

    log_dens = all_rows(
        land, right, wide, left, mix, load, (score0, score1), (logit0, logit1), (post0, post1), (gap0, gap1), acc, accw,
        prior,
    )
    for r in range(share):
        fresh = half_ref[r] + 0.5 * STEP_FIELD * prior[r]
        mom_ref[r] = fresh
        energy = energy + 0.5 * (fresh * fresh)
    param_grads(flat, acc, accw, grad, ncomp, nfac)
    first_device = (cells_rank == 0) & (comp_rank == 0)
    prof_all = flat[0:ncomp, :]
    load_all = flat[ncomp:nparam, :]
    param_energy = jnp.sum(0.125 * (prof_all * prof_all)) + jnp.sum(0.5 * (load_all * load_all))
    total = jnp.sum(energy) - jnp.sum(log_dens) + jnp.where(first_device, param_energy, 0.0)
    out[0:nparam, :] = 0.5 * STEP_PARAM * (grad0_ref[...] + grad[...])
    tail = out.shape[0] - nparam
    spot = lax.broadcasted_iota(jnp.int32, (tail, LANES), 0) + lax.broadcasted_iota(jnp.int32, (tail, LANES), 1)
    out[nparam:, :] = jnp.where(spot == 0, total, 0.0)
    owner = cells_rank == 0
    old_prof, old_load = own_ref[0:mine, :], own_ref[mine : mine + nfac, :]
    base_prof = pmom_ref[...] - 0.5 * STEP_PARAM * 0.25 * (old_prof + new_prof)
    base_load = wmom_ref[...] - 0.5 * STEP_PARAM * (old_load + new_load)
    out[pl.ds(pl.multiple_of(comp_rank * mine, mine), mine), :] += jnp.where(owner, base_prof, 0.0)
    out[pl.ds(pl.multiple_of(ncomp + comp_rank * nfac, nfac), nfac), :] += jnp.where(owner, base_load, 0.0)
    spread_chunks(out, keep_ref, send_ref, cells_rank)


def last_kernel(ncomp, nparam, cells, rank_ref, near_ref, far_ref, prof_ref, mixing_ref, ham_ref, flat):
    cells_rank, comp_rank = rank_ref[0], rank_ref[1]
    mine, nfac = prof_ref.shape[0], mixing_ref.shape[0]
    gather_chunks(flat, near_ref, far_ref, cells_rank)
    prof_ref[...] = flat[pl.ds(pl.multiple_of(comp_rank * mine, mine), mine), :]
    mixing_ref[...] = flat[pl.ds(pl.multiple_of(ncomp + comp_rank * nfac, nfac), nfac), :]
    momenta = flat[0:nparam, :]
    rest = flat[nparam:, :]
    ham_ref[0, 0] = (0.5 * jnp.sum(momenta * momenta) + jnp.sum(rest)) / cells


def fast_device(
    factor_field, profile, mixing, factor_mom, profile_mom, mixing_mom, field_tau, counts, land_mask, log_exposure
):
    nfac, share, cols = factor_field.shape
    mine, ncat = profile.shape
    tile_rows = land_mask.shape[0]
    ring = lax.axis_size("comp")
    tiles = lax.axis_size("cells")
    ncomp = mine * ring
    nparam = ncomp + nfac * ncomp // LANES
    pairs = tiles // 2
    round_up = lambda rows: -(-rows // (8 * tiles)) * 8
    chunk_one = round_up(nparam)
    chunk_two = round_up(nparam + 1)
    comp_rank = lax.axis_index("comp")
    cells_rank = lax.axis_index("cells")
    ranks = jnp.stack([cells_rank, comp_rank]).astype(jnp.int32)
    pack = jnp.concatenate([profile, mixing], axis=0)
    parts = [pack] + [partner(pack, "comp", k) for k in range(1, ring)]

    count_rows = lax.dynamic_slice_in_dim(counts, comp_rank * share, share, 1).swapaxes(0, 1).astype(BF16)
    field_rows = factor_field.swapaxes(0, 1)
    mom_rows = factor_mom.swapaxes(0, 1)
    both = ("cells", "comp")
    last = tiles * ring - 1
    forward = [(i, i + 1) for i in range(last)]
    backward = [(i + 1, i) for i in range(last)]
    land_edge = lambda row: lax.dynamic_slice_in_dim(land_mask, row, 1, 0).astype(F32)
    edges = [
        jnp.concatenate([factor_field[:, r, :], jnp.broadcast_to(land_edge(comp_rank * share + r), (8, cols))], axis=0)
        for r in (share - 1, 0)
    ]
    low = lax.ppermute(edges[0], both, forward)
    high = lax.ppermute(edges[1], both, backward)

    def full(*shape):
        zeros = (0,) * len(shape)
        return pl.BlockSpec(shape, lambda i, ranks: zeros)

    smem = pl.BlockSpec(memory_space=pltpu.SMEM)
    cell_specs = [
        smem,
        full(share, ncat, cols),
        full(share, nfac, cols),
    ]
    row_spec = pl.BlockSpec((share, cols), lambda i, ranks: (ranks[1], 0))
    edge_spec = full(nfac + 8, cols)
    param_specs = [full(mine, ncat), full(nfac, mine)]
    pack_spec = full(mine + nfac, ncat)
    shape = lambda *dims: jax.ShapeDtypeStruct(dims, F32)
    work = [
        pltpu.VMEM((ncomp, 4 * LANES), BF16),
        pltpu.VMEM((ncomp, LANES), BF16),
        pltpu.VMEM((2 * nfac, ncomp), BF16),
        pltpu.VMEM((share, 4 * LANES, cols), BF16),
        pltpu.VMEM((share, 2 * LANES, 2 * cols), BF16),
        pltpu.VMEM((share, nfac, cols), F32),
    ]
    work += [pltpu.VMEM((ncomp, cols), F32)] * 4 + [pltpu.VMEM((ncomp, 2 * cols), BF16)] * 4
    work += [
        pltpu.VMEM((ncomp, 2 * LANES), F32),
        pltpu.VMEM((ncomp, LANES), F32),
    ]
    params = pltpu.CompilerParams(vmem_limit_bytes=40 * 1024 * 1024, dimension_semantics=("arbitrary",))

    def call(body, name, ins, outs, scratch):
        return pl.pallas_call(
            body,
            name=name,
            grid_spec=pltpu.PrefetchScalarGridSpec(
                num_scalar_prefetch=1,
                grid=(1,),
                in_specs=ins,
                out_specs=[spec for spec, _ in outs],
                scratch_shapes=scratch,
            ),
            out_shape=[out for _, out in outs],
            compiler_params=params,
        )

    def block(*dims):
        return (full(*dims), shape(*dims))

    first = call(
        functools.partial(first_kernel, ncomp),
        "first_gradient",
        cell_specs + [full(share, nfac, cols), row_spec, row_spec, edge_spec, edge_spec] + param_specs + [pack_spec] * ring,
        [
            block(share, nfac, cols),
            block(share, nfac, cols),
            block(nfac, cols),
            block(nfac, cols),
            block(nparam, LANES),
            block(pairs, chunk_one, LANES),
            block(pairs, chunk_one, LANES),
        ],
        [pltpu.VMEM((tiles * chunk_one, LANES), F32)] + work,
    )
    new_field, half, top, bottom, grad, keep, send = first(
        ranks, field_tau, count_rows, field_rows, mom_rows, land_mask, log_exposure, low, high, profile_mom, mixing_mom,
        *parts,
    )
    low_next = jnp.concatenate([lax.ppermute(bottom, both, forward), low[nfac:]], axis=0)
    high_next = jnp.concatenate([lax.ppermute(top, both, backward), high[nfac:]], axis=0)
    near, far = all_sum(keep, send)
    second = call(
        functools.partial(second_kernel, ncomp),
        "second_gradient",
        cell_specs
        + [full(share, nfac, cols), row_spec, row_spec, edge_spec, edge_spec]
        + param_specs
        + [pack_spec, full(pairs, chunk_one, LANES), full(pairs, chunk_one, LANES), full(nparam, LANES)],
        [
            block(share, nfac, cols),
            block(mine, ncat),
            block(nfac, mine),
            block(pairs, chunk_two, LANES),
            block(pairs, chunk_two, LANES),
        ],
        [pltpu.VMEM((tiles * chunk_one, LANES), F32)]
        + work
        + [pltpu.VMEM((tiles * chunk_two, LANES), F32), pltpu.VMEM((nparam, LANES), F32)],
    )
    new_mom, new_profile, new_mixing, keep, send = second(
        ranks, field_tau, count_rows, new_field, half, land_mask, log_exposure, low_next, high_next, profile_mom, mixing_mom,
        pack, near, far, grad,
    )
    near, far = all_sum(keep, send)
    final = call(
        functools.partial(last_kernel, ncomp, nparam, tile_rows * cols * tiles),
        "momenta",
        [full(pairs, chunk_two, LANES), full(pairs, chunk_two, LANES)],
        [block(mine, ncat), block(nfac, mine), (smem, shape(1, 1))],
        [pltpu.VMEM((tiles * chunk_two, LANES), F32)],
    )
    new_profile_mom, new_mixing_mom, hamiltonian = final(ranks, near, far)
    return (
        new_field.swapaxes(0, 1),
        new_profile,
        new_mixing,
        new_mom.swapaxes(0, 1),
        new_profile_mom,
        new_mixing_mom,
        hamiltonian.reshape(()),
    )


def power_of_two(count):
    return count & (count - 1) == 0


def choose_device(*args):
    factor_field, profile, mixing = args[:3]
    nfac, share, cols = factor_field.shape
    mine, ncat = profile.shape
    tiles, ring = lax.axis_size("cells"), lax.axis_size("comp")
    fits = mine == LANES and ncat == LANES and nfac % 16 == 0 and 6 * nfac + 6 <= LANES
    fits = fits and share == 8 and cols % LANES == 0
    fits = fits and power_of_two(tiles) and tiles > 1 and power_of_two(ring)
    return fast_device(*args) if fits else plain_device(*args)


def solution(mesh):
    in_specs = (
        P(None, ("cells", "comp"), None),
        P("comp", None),
        P(None, "comp"),
        P(None, ("cells", "comp"), None),
        P("comp", None),
        P(None, "comp"),
        P(),
        P(None, "cells", None),
        P("cells", None),
        P("cells", None),
    )
    out_specs = (
        P(None, ("cells", "comp"), None),
        P("comp", None),
        P(None, "comp"),
        P(None, ("cells", "comp"), None),
        P("comp", None),
        P(None, "comp"),
        P(),
    )
    return jax.shard_map(
        choose_device, mesh=mesh, in_specs=in_specs, out_specs=out_specs, check_vma=False
    )
```

```python
import functools
import math

import jax
import jax.numpy as jnp
from jax import lax
from jax.experimental import pallas as pl
from jax.experimental.pallas import tpu as pltpu
from jax.sharding import PartitionSpec as P


def extended(cells, sides, width):
    for axis, dim in sides:
        count = lax.axis_size(axis)
        ends = count - 1
        head = lax.slice_in_dim(cells, 0, width, axis=dim)
        tail = lax.slice_in_dim(cells, cells.shape[dim] - width, cells.shape[dim], axis=dim)
        cells = jnp.concatenate(
            [
                lax.ppermute(tail, axis, [(i, (i + 1) % count) for i in range(ends)]),
                cells,
                lax.ppermute(head, axis, [((i + 1) % count, i) for i in range(ends)]),
            ],
            axis=dim,
        )
    return cells


def field_prior(padded, land_pad, field_tau):
    ridge = 0.1
    step_x = padded[:, 1:, :] - padded[:, :-1, :]
    edge_x = land_pad[1:, :] * land_pad[:-1, :]
    flux_x = edge_x[None, :, :] * step_x
    centre = padded[:, 1:-1, :]
    land_mid = land_pad[1:-1, :]
    step_y = centre[:, :, 1:] - centre[:, :, :-1]
    edge_y = land_mid[:, 1:] * land_mid[:, :-1]
    flux_y = edge_y[None, :, :] * step_y
    lap_x = flux_x[:, :-1, :] - flux_x[:, 1:, :]
    lap_y = jnp.pad(flux_y, ((0, 0), (0, 0), (1, 0))) - jnp.pad(flux_y, ((0, 0), (0, 0), (0, 1)))
    tau_cube = field_tau[:, None, None]
    grad = -tau_cube * (lap_x + lap_y + ridge * centre)
    energy = 0.5 * jnp.sum(tau_cube * (flux_x[:, 1:, :] * step_x[:, 1:, :]))
    energy = energy + 0.5 * jnp.sum(tau_cube * (flux_y * step_y))
    energy = energy + 0.5 * ridge * jnp.sum(tau_cube * (centre * centre))
    return (grad, energy)


def tile_scores(flat_tile, count_rows, exposure, profile, mixing):
    prof_exp = jnp.exp(profile)
    rate_total = jnp.sum(prof_exp, axis=1)
    mix_logit = jnp.dot(mixing.T, flat_tile, precision=lax.Precision.HIGHEST)
    fit_score = (
        jnp.dot(profile, count_rows, precision=lax.Precision.HIGHEST)
        - rate_total[:, None] * exposure[None, :]
    )
    return (mix_logit, mix_logit + fit_score)


def tile_grads(
    flat_tile, count_rows, land_weight, exposure, mixing, mix_logit, joint_score, log_mix, log_joint
):
    prior_share = jnp.exp(mix_logit - log_mix[None, :])
    posterior = jnp.exp(joint_score - log_joint[None, :])
    post_land = posterior * land_weight[None, :]
    gap_weight = (posterior - prior_share) * land_weight[None, :]
    grad_counts = jnp.dot(post_land, count_rows.T, precision=lax.Precision.HIGHEST)
    rate_mass = jnp.sum(post_land * exposure[None, :], axis=1)
    grad_mix = jnp.dot(flat_tile, gap_weight.T, precision=lax.Precision.HIGHEST)
    field_lik = jnp.dot(mixing, gap_weight, precision=lax.Precision.HIGHEST)
    log_dens = jnp.sum(land_weight * (log_joint - log_mix))
    return (grad_counts, rate_mass, grad_mix, field_lik, log_dens)


def log_sum(scores):
    top = jnp.max(scores, axis=0)
    return top + jnp.log(jnp.sum(jnp.exp(scores - top[None, :]), axis=0))


def plain_device(
    factor_field,
    profile,
    mixing,
    factor_mom,
    profile_mom,
    mixing_mom,
    field_tau,
    counts,
    land_mask,
    log_exposure,
):
    step_field = 0.05
    step_profile = 0.002
    step_mixing = 0.002
    tile_rows, tile_cols = land_mask.shape
    ncat = counts.shape[0]
    share_rows = factor_field.shape[1]
    comp_rank = lax.axis_index("comp")
    cells_rank = lax.axis_index("cells")
    first_cells = cells_rank == 0
    land_pad = extended(land_mask, (("cells", 0),), 1).astype(jnp.float32)
    row_start = comp_rank * share_rows
    count_rows = lax.dynamic_slice_in_dim(counts, row_start, share_rows, 1)
    count_rows = count_rows.reshape(ncat, share_rows * tile_cols).astype(jnp.float32)
    land_weight = (
        lax.dynamic_slice_in_dim(land_mask, row_start, share_rows, 0)
        .reshape(-1)
        .astype(jnp.float32)
    )
    exposure = jnp.exp(lax.dynamic_slice_in_dim(log_exposure, row_start, share_rows, 0).reshape(-1))
    land_near = lax.dynamic_slice_in_dim(land_pad, row_start, share_rows + 2, 0)

    def evaluate(share_field, profile_now, mixing_now):
        padded = extended(share_field, ((("cells", "comp"), 1),), 1)
        prior_grad, prior_energy = field_prior(padded, land_near, field_tau)
        profile_all, mixing_all = (
            lax.all_gather(profile_now, "comp", axis=0, tiled=True),
            lax.all_gather(mixing_now, "comp", axis=1, tiled=True),
        )
        flat_tile = share_field.reshape(share_field.shape[0], -1)
        mix_logit, joint_score = tile_scores(
            flat_tile, count_rows, exposure, profile_all, mixing_all
        )
        log_mix = log_sum(mix_logit)
        log_joint = log_sum(joint_score)
        grad_counts, rate_mass, grad_mix, field_lik, log_dens = tile_grads(
            flat_tile,
            count_rows,
            land_weight,
            exposure,
            mixing_all,
            mix_logit,
            joint_score,
            log_mix,
            log_joint,
        )
        grad_counts, rate_mass, mix_rows = (
            lax.psum_scatter(grad_counts, "comp", scatter_dimension=0, tiled=True),
            lax.psum_scatter(rate_mass, "comp", scatter_dimension=0, tiled=True),
            lax.psum_scatter(grad_mix.T, "comp", scatter_dimension=0, tiled=True),
        )
        grad_mix = mix_rows.T
        grad_field = prior_grad + field_lik.reshape(share_field.shape)
        log_part = log_dens - prior_energy
        grad_counts, rate_mass, grad_mix = lax.psum((grad_counts, rate_mass, grad_mix), "cells")
        grad_profile = grad_counts - jnp.exp(profile_now) * rate_mass[:, None] - 0.25 * profile_now
        grad_mixing = grad_mix - mixing_now
        param_prior = -0.125 * jnp.sum(profile_now * profile_now) - 0.5 * jnp.sum(
            mixing_now * mixing_now
        )
        log_part = log_part + jnp.where(first_cells, param_prior, 0.0)
        return (log_part, grad_field, grad_profile, grad_mixing)

    first = evaluate(factor_field, profile, mixing)
    half_field = factor_mom + 0.5 * step_field * first[1]
    half_profile = profile_mom + 0.5 * step_profile * first[2]
    half_mixing = mixing_mom + 0.5 * step_mixing * first[3]
    new_field = factor_field + step_field * half_field
    new_profile = profile + step_profile * half_profile
    new_mixing = mixing + step_mixing * half_mixing
    second = evaluate(new_field, new_profile, new_mixing)
    new_factor_mom = half_field + 0.5 * step_field * second[1]
    new_profile_mom = half_profile + 0.5 * step_profile * second[2]
    new_mixing_mom = half_mixing + 0.5 * step_mixing * second[3]
    kinetic = 0.5 * jnp.sum(new_factor_mom * new_factor_mom)
    kinetic = kinetic + jnp.where(
        first_cells,
        0.5
        * (jnp.sum(new_profile_mom * new_profile_mom) + jnp.sum(new_mixing_mom * new_mixing_mom)),
        0.0,
    )
    log_total, kinetic_total = lax.psum((second[0], kinetic), ("cells", "comp"))
    cell_count = tile_rows * tile_cols * lax.axis_size("cells")
    hamiltonian = (kinetic_total - log_total) / cell_count
    return (
        new_field,
        new_profile,
        new_mixing,
        new_factor_mom,
        new_profile_mom,
        new_mixing_mom,
        hamiltonian,
    )


STEP_FIELD = 0.05
STEP_PARAM = 0.002
RIDGE = 0.1
LOG2E = math.log2(math.e)
LN2 = math.log(2.0)
LANES = 128
F32 = jnp.float32
BF16 = jnp.bfloat16


def pieces(values, count):
    parts = []
    for _ in range(count):
        part = values.astype(BF16)
        parts.append(part)
        values = values - part.astype(F32)
    return parts


def dot(left, right, dims=((1,), (0,))):
    return lax.dot_general(left, right, (dims, ((), ())), preferred_element_type=F32)


def partner(values, axis, flip):
    count = lax.axis_size(axis)
    return lax.ppermute(values, axis, [(i, i ^ flip) for i in range(count)])


def all_sum(keep, send, near_edge=None, far_edge=None):
    pairs, rows, _ = keep.shape
    chunks = keep + partner(send, "cells", 1)
    total = chunks[0]
    for part in [partner(chunks[k], "cells", 2 * k) for k in range(1, pairs)]:
        total = total + part
    if near_edge is None:
        parts = [partner(total, "comp", k) for k in range(1, lax.axis_size("comp"))]
        near_got = None
        for part in parts:
            total = total + part
    else:
        first = partner(jnp.concatenate([total, near_edge], axis=0), "comp", 1)
        second = partner(total, "comp", 2)
        third = partner(jnp.concatenate([total, far_edge], axis=0), "comp", 3)
        near_got = first[rows:]
        total = jnp.concatenate([total + first[:rows] + second + third[:rows], third[rows:]], axis=0)
    near = jnp.stack([total] + [partner(total, "cells", 2 * k) for k in range(1, pairs)])
    return near, partner(near, "cells", 1), near_got


def chunk_index(cells_rank, k, other):
    core = cells_rank % 2
    return (((cells_rank // 2) ^ k) * 2) + (1 - core if other else core)


def gather_chunks(flat_ref, near_ref, far_ref, cells_rank, rows):
    for k in range(near_ref.shape[0]):
        for source, other in ((near_ref, False), (far_ref, True)):
            start = pl.multiple_of(chunk_index(cells_rank, k, other) * rows, 8)
            flat_ref[pl.ds(start, rows), :] = source[k, 0:rows, :]


def spread_chunks(flat_ref, keep_ref, send_ref, cells_rank):
    pairs, rows, _ = keep_ref.shape
    for k in range(pairs):
        for target, other in ((keep_ref, False), (send_ref, True)):
            start = pl.multiple_of(chunk_index(cells_rank, k, other) * rows, 8)
            target[k] = flat_ref[pl.ds(start, rows), :]


def load_params(flat_ref, left_ref, mix_ref, load_ref, ncomp, nfac):
    lane = lax.broadcasted_iota(jnp.int32, (LANES, LANES), 1)
    first = 6 * nfac
    for q in range(ncomp // LANES):
        rows = pl.ds(q * LANES, LANES)
        prof = flat_ref[rows, :]
        high, mid, low = pieces(prof * LOG2E, 3)
        left_ref[rows, 0:LANES] = high
        left_ref[rows, 2 * LANES : 3 * LANES] = mid
        left_ref[rows, 3 * LANES : 4 * LANES] = low
        rate = jnp.sum(jnp.exp(prof), axis=1, keepdims=True) * LOG2E
        rate_high, rate_mid, rate_low = [part.astype(F32) for part in pieces(rate, 3)]
        load = flat_ref[pl.ds(ncomp + q * nfac, nfac), :]
        w_high, w_mid, w_low = [part.astype(F32) for part in pieces(load * LOG2E, 3)]
        stack = jnp.concatenate(
            [w_high, w_high, w_high, w_mid, w_mid, w_low, jnp.zeros((LANES - first, LANES), F32)], axis=0
        )
        turned = stack.T
        mix_ref[rows, :] = turned.astype(BF16)
        rate_part = jnp.where(
            (lane >= first) & (lane < first + 3),
            rate_high,
            jnp.where(
                (lane >= first + 3) & (lane < first + 5), rate_mid, jnp.where(lane == first + 5, rate_low, 0.0)
            ),
        )
        left_ref[rows, LANES : 2 * LANES] = (turned - rate_part).astype(BF16)
        load_high, load_mid = pieces(load, 2)
        load_ref[0:nfac, q * LANES : (q + 1) * LANES] = load_high
        load_ref[nfac : 2 * nfac, q * LANES : (q + 1) * LANES] = load_mid


def load_cells(counts_ref, field_ref, logexp_ref, right_ref, wide_ref):
    share, ncat, cols = counts_ref.shape
    nfac = field_ref.shape[1]
    exposure = jnp.exp(logexp_ref[...])
    sub = lax.broadcasted_iota(jnp.int32, (LANES - 6 * nfac, cols), 0)
    for r in range(share):
        count = counts_ref[r]
        high, mid, low = pieces(field_ref[r], 3)
        e_high, e_mid, e_low = [part.astype(F32) for part in pieces(exposure[r : r + 1, :], 3)]
        e_rows = jnp.where((sub == 0) | (sub == 3) | (sub == 5), e_high, 0.0)
        e_rows = jnp.where((sub == 1) | (sub == 4), e_mid, e_rows)
        e_rows = jnp.where(sub == 2, e_low, e_rows).astype(BF16)
        extra = jnp.concatenate([high, mid, low, high, mid, high, e_rows], axis=0)
        right_ref[r, 0:ncat, :] = count
        right_ref[r, LANES : 2 * LANES, :] = extra
        right_ref[r, 2 * LANES : 2 * LANES + ncat, :] = count
        right_ref[r, 3 * LANES : 3 * LANES + ncat, :] = count
        for side in range(2):
            wide_ref[r, 0:ncat, side * cols : (side + 1) * cols] = count
            wide_ref[r, LANES : 2 * LANES, side * cols : (side + 1) * cols] = extra


def field_weights(tau_ref, nfac, cols):
    row = lax.broadcasted_iota(jnp.int32, (nfac, cols), 0)
    tau = jnp.zeros((nfac, cols), F32)
    for j in range(nfac):
        tau = jnp.where(row == j, tau_ref[j], tau)
    return tau


def load_prior(rows, lands, tau, prior_ref):
    nfac, cols = tau.shape
    inner = lax.broadcasted_iota(jnp.int32, (nfac, cols), 1) < cols - 1
    energy = jnp.zeros((nfac, cols), F32)
    lands = [jnp.broadcast_to(x, (nfac, cols)) for x in lands]
    for r in range(len(rows) - 2):
        here = rows[r + 1]
        step_right = here - pltpu.roll(here, cols - 1, 1)
        edge_right = jnp.where(inner, lands[r + 1] * pltpu.roll(lands[r + 1], cols - 1, 1), 0.0)
        flux_right = edge_right * step_right
        laplace = flux_right - pltpu.roll(flux_right, 1, 1)
        parts = flux_right * step_right + RIDGE * (here * here)
        if rows[r] is not None:
            laplace = laplace + lands[r] * lands[r + 1] * (here - rows[r])
        if rows[r + 2] is not None:
            step_down = here - rows[r + 2]
            flux_down = lands[r + 1] * lands[r + 2] * step_down
            laplace = laplace + flux_down
            parts = parts + flux_down * step_down
        prior_ref[r] = -tau * (laplace + RIDGE * here)
        energy = energy + 0.5 * tau * parts
    return energy


def pack_edge(edge_ref, field, fresh, land):
    nfac, cols = field.shape
    blocks = cols // LANES
    sub = lax.broadcasted_iota(jnp.int32, (8, LANES), 0)
    lands = jnp.zeros((8, LANES), F32)
    for b in range(blocks):
        lanes = slice(b * LANES, (b + 1) * LANES)
        edge_ref[b * nfac : (b + 1) * nfac, :] = field[:, lanes]
        edge_ref[(blocks + b) * nfac : (blocks + b + 1) * nfac, :] = fresh[:, lanes]
        lands = jnp.where(sub == b, land[:, lanes], lands)
    edge_ref[2 * blocks * nfac :, :] = lands


def unpack_edge(edge, nfac, cols):
    blocks = cols // LANES
    wide = lambda start, size, step: jnp.concatenate(
        [edge[start + b * step : start + b * step + size, :] for b in range(blocks)], axis=1
    )
    return wide(0, nfac, nfac), wide(blocks * nfac, nfac, nfac), wide(2 * blocks * nfac, 1, 1)


def row_scores(r, right_ref, left_ref, mix_ref, score_ref, logit_ref):
    tops = []
    for target, values in (
        (score_ref, dot(left_ref[...], right_ref[r])),
        (logit_ref, dot(mix_ref[...], right_ref[r, LANES : 2 * LANES, :])),
    ):
        target[...] = values
        ncomp, cols = values.shape
        tops.append(jnp.max(jnp.max(values.reshape(ncomp // 8, 8, cols), axis=0), axis=0, keepdims=True))
    return tops


def row_shares(tops, land, score_ref, logit_ref, post_ref, gap_ref):
    ncomp, cols = score_ref.shape
    block = 32
    top_s, top_a = tops
    sum_s = jnp.zeros((8, cols), F32)
    sum_a = jnp.zeros((8, cols), F32)
    for i in range(0, ncomp, block):
        part_s = jnp.exp2(score_ref[i : i + block, :] - top_s)
        part_a = jnp.exp2(logit_ref[i : i + block, :] - top_a)
        score_ref[i : i + block, :] = part_s
        logit_ref[i : i + block, :] = part_a
        sum_s = sum_s + jnp.sum(part_s.reshape(block // 8, 8, cols), axis=0)
        sum_a = sum_a + jnp.sum(part_a.reshape(block // 8, 8, cols), axis=0)
    sum_s = jnp.sum(sum_s, axis=0, keepdims=True)
    sum_a = jnp.sum(sum_a, axis=0, keepdims=True)
    log_s = top_s + jnp.log2(sum_s)
    log_a = top_a + jnp.log2(sum_a)
    inv_s = land / sum_s
    inv_a = land / sum_a
    for i in range(0, ncomp, block):
        post = score_ref[i : i + block, :] * inv_s
        gap = post - logit_ref[i : i + block, :] * inv_a
        for target, values in ((post_ref, post), (gap_ref, gap)):
            high, low = pieces(values, 2)
            target[i : i + block, 0:cols] = high
            target[i : i + block, cols : 2 * cols] = low
    return land * (LN2 * (log_s - log_a))


def row_products(r, wide_ref, load_ref, post_ref, gap_ref, acc_ref, accw_ref, prior_ref):
    nfac = load_ref.shape[0] // 2
    cols = prior_ref.shape[2]
    last = ((1,), (1,))
    acc = dot(post_ref[...], wide_ref[r], last)
    accw = dot(gap_ref[...], wide_ref[r, LANES : 2 * LANES, :], last)
    if r == 0:
        acc_ref[...] = acc
        accw_ref[...] = accw
    else:
        acc_ref[...] += acc
        accw_ref[...] += accw
    lik = dot(load_ref[...], gap_ref[...])
    lik = lik[0:nfac] + lik[nfac : 2 * nfac]
    prior_ref[r] += lik[:, 0:cols] + lik[:, cols : 2 * cols]


def all_rows(land, right, wide, left, mix, load, scores, logits, posts, gaps, acc, accw, prior):
    share, _, cols = prior.shape
    log_dens = jnp.zeros((1, cols), F32)
    tops = {}
    for r in range(share + 2):
        if r < share:
            tops[r] = row_scores(r, right, left, mix, scores[r % 2], logits[r % 2])
        if 0 <= r - 1 < share:
            p = r - 1
            log_dens = log_dens + row_shares(
                tops[p], land[p : p + 1, :], scores[p % 2], logits[p % 2], posts[p % 2], gaps[p % 2]
            )
        if 0 <= r - 2:
            p = r - 2
            row_products(p, wide, load, posts[p % 2], gaps[p % 2], acc, accw, prior)
    return log_dens


def param_grads(flat_ref, acc_ref, accw_ref, grad_ref, ncomp, nfac):
    lane = lax.broadcasted_iota(jnp.int32, (LANES, LANES), 1)
    rate_lanes = (lane >= 6 * nfac) & (lane < 6 * nfac + 3)
    for q in range(ncomp // LANES):
        rows = pl.ds(q * LANES, LANES)
        mass = jnp.sum(jnp.where(rate_lanes, acc_ref[rows, LANES : 2 * LANES], 0.0), axis=1, keepdims=True)
        grad_ref[rows, :] = acc_ref[rows, 0:LANES] - jnp.exp(flat_ref[rows, :]) * mass
        turned = accw_ref[rows, :].T
        grad_ref[pl.ds(ncomp + q * nfac, nfac), :] = (
            turned[0:nfac] + turned[nfac : 2 * nfac] + turned[2 * nfac : 3 * nfac]
        )


def first_kernel(
    ncomp, rank_ref, tau_ref, counts_ref, field_ref, mom_ref, land_ref, logexp_ref, pmom_ref, wmom_ref, *refs
):
    ring = ncomp // pmom_ref.shape[0]
    part_refs = refs[:ring]
    (new_ref, half_ref, near_ref, far_ref, grad_ref, keep_ref, send_ref) = refs[ring : ring + 7]
    (flat, left, mix, load, right, wide, prior, score0, score1, logit0, logit1, post0, post1, gap0, gap1, acc, accw) = (
        refs[ring + 7 :]
    )
    cells_rank, comp_rank = rank_ref[0], rank_ref[1]
    share, nfac, cols = field_ref.shape
    mine = pmom_ref.shape[0]
    for k in range(ring):
        group = comp_rank ^ k
        flat[pl.ds(pl.multiple_of(group * mine, mine), mine), :] = part_refs[k][0:mine, :]
        flat[pl.ds(pl.multiple_of(ncomp + group * nfac, nfac), nfac), :] = part_refs[k][mine : mine + nfac, :]
    land = land_ref[...].astype(F32)
    load_params(flat, left, mix, load, ncomp, nfac)
    load_cells(counts_ref, field_ref, logexp_ref, right, wide)
    lands = [land[r : r + 1, :] for r in range(share)]
    tau = field_weights(tau_ref, nfac, cols)
    load_prior([None] + [field_ref[r] for r in range(share)] + [None], lands[:1] + lands + lands[-1:], tau, prior)
    all_rows(
        land, right, wide, left, mix, load, (score0, score1), (logit0, logit1), (post0, post1), (gap0, gap1), acc, accw,
        prior,
    )
    for r in range(share):
        half = mom_ref[r] + 0.5 * STEP_FIELD * prior[r]
        half_ref[r] = half
        new_ref[r] = field_ref[r] + STEP_FIELD * half
    even = comp_rank % 2 == 0
    end = share - 1
    for target, flag in ((near_ref, even), (far_ref, jnp.logical_not(even))):
        pack_edge(
            target,
            jnp.where(flag, field_ref[end], field_ref[0]),
            jnp.where(flag, new_ref[end], new_ref[0]),
            jnp.where(flag, lands[end], lands[0]),
        )
    param_grads(flat, acc, accw, grad_ref, ncomp, nfac)
    nparam = grad_ref.shape[0]
    if flat.shape[0] > nparam:
        flat[nparam:, :] = jnp.zeros((flat.shape[0] - nparam, LANES), F32)
    flat[0:nparam, :] = 0.5 * STEP_PARAM * STEP_PARAM * grad_ref[...]
    own_prof, own_load = part_refs[0][0:mine, :], part_refs[0][mine : mine + nfac, :]
    owner = cells_rank == 0
    base_prof = own_prof + STEP_PARAM * (pmom_ref[...] - 0.5 * STEP_PARAM * 0.25 * own_prof)
    base_load = own_load + STEP_PARAM * (wmom_ref[...] - 0.5 * STEP_PARAM * own_load)
    flat[pl.ds(pl.multiple_of(comp_rank * mine, mine), mine), :] += jnp.where(owner, base_prof, 0.0)
    flat[pl.ds(pl.multiple_of(ncomp + comp_rank * nfac, nfac), nfac), :] += jnp.where(owner, base_load, 0.0)
    spread_chunks(flat, keep_ref, send_ref, cells_rank)


def second_kernel(
    ncomp, chunk, ring, tiles, rank_ref, tau_ref, counts_ref, field_ref, half_ref, land_ref, logexp_ref, pmom_ref, wmom_ref,
    old_top_ref, old_bottom_ref, own_ref, near_ref, far_ref, edge_ref, grad0_ref, new_ref, mom_ref, prof_ref, mixing_ref,
    keep_ref, send_ref,
    flat, left, mix, load, right, wide, prior, score0, score1, logit0, logit1, post0, post1, gap0, gap1, acc, accw, out,
    grad,
):
    cells_rank, comp_rank = rank_ref[0], rank_ref[1]
    share, nfac, cols = field_ref.shape
    mine = pmom_ref.shape[0]
    nparam = grad0_ref.shape[0]
    gather_chunks(flat, near_ref, far_ref, cells_rank, chunk)
    new_prof = flat[pl.ds(pl.multiple_of(comp_rank * mine, mine), mine), :]
    new_load = flat[pl.ds(pl.multiple_of(ncomp + comp_rank * nfac, nfac), nfac), :]
    prof_ref[...] = new_prof
    mixing_ref[...] = new_load
    land = land_ref[...].astype(F32)
    lands = [land[r : r + 1, :] for r in range(share)]
    tau = field_weights(tau_ref, nfac, cols)

    source = jnp.where(comp_rank == 0, cells_rank - 1, jnp.where(comp_rank == ring - 1, cells_rank + 1, cells_rank))
    source = jnp.clip(source, 0, tiles - 1)
    slot = (source // 2) ^ (cells_rank // 2)
    relay = jnp.where(source % 2 == cells_rank % 2, near_ref[slot, chunk:, :], far_ref[slot, chunk:, :])
    even = comp_rank % 2 == 0
    direct = edge_ref[...]
    above = unpack_edge(jnp.where(even, relay, direct), nfac, cols)
    below = unpack_edge(jnp.where(even, direct, relay), nfac, cols)
    land_above = jnp.where((comp_rank == 0) & (cells_rank == 0), 0.0, above[2])
    land_below = jnp.where((comp_rank == ring - 1) & (cells_rank == tiles - 1), 0.0, below[2])
    end = share - 1
    pull_up = -tau * (land_above * lands[0]) * (old_top_ref[0] - above[0])
    pull_down = -tau * (land_below * lands[end]) * (old_bottom_ref[0] - below[0])
    move = 0.5 * STEP_FIELD * STEP_FIELD
    for r in range(share):
        fresh = field_ref[r]
        if r == 0:
            fresh = fresh + move * pull_up
        if r == end:
            fresh = fresh + move * pull_down
        new_ref[r] = fresh
    load_params(flat, left, mix, load, ncomp, nfac)
    load_cells(counts_ref, new_ref, logexp_ref, right, wide)
    rows = [above[1] - move * pull_up] + [new_ref[r] for r in range(share)] + [below[1] - move * pull_down]
    energy = load_prior(rows, [land_above] + lands + [land_below], tau, prior)
    prior[0] += pull_up
    prior[end] += pull_down

    log_dens = all_rows(
        land, right, wide, left, mix, load, (score0, score1), (logit0, logit1), (post0, post1), (gap0, gap1), acc, accw,
        prior,
    )
    for r in range(share):
        fresh = half_ref[r] + 0.5 * STEP_FIELD * prior[r]
        mom_ref[r] = fresh
        energy = energy + 0.5 * (fresh * fresh)
    param_grads(flat, acc, accw, grad, ncomp, nfac)
    first_device = (cells_rank == 0) & (comp_rank == 0)
    prof_all = flat[0:ncomp, :]
    load_all = flat[ncomp:nparam, :]
    param_energy = jnp.sum(0.125 * (prof_all * prof_all)) + jnp.sum(0.5 * (load_all * load_all))
    total = jnp.sum(energy) - jnp.sum(log_dens) + jnp.where(first_device, param_energy, 0.0)
    out[0:nparam, :] = 0.5 * STEP_PARAM * (grad0_ref[...] + grad[...])
    tail = out.shape[0] - nparam
    spot = lax.broadcasted_iota(jnp.int32, (tail, LANES), 0) + lax.broadcasted_iota(jnp.int32, (tail, LANES), 1)
    out[nparam:, :] = jnp.where(spot == 0, total, 0.0)
    owner = cells_rank == 0
    old_prof, old_load = own_ref[0:mine, :], own_ref[mine : mine + nfac, :]
    base_prof = pmom_ref[...] - 0.5 * STEP_PARAM * 0.25 * (old_prof + new_prof)
    base_load = wmom_ref[...] - 0.5 * STEP_PARAM * (old_load + new_load)
    out[pl.ds(pl.multiple_of(comp_rank * mine, mine), mine), :] += jnp.where(owner, base_prof, 0.0)
    out[pl.ds(pl.multiple_of(ncomp + comp_rank * nfac, nfac), nfac), :] += jnp.where(owner, base_load, 0.0)
    spread_chunks(out, keep_ref, send_ref, cells_rank)


def last_kernel(ncomp, nparam, chunk, cells, rank_ref, near_ref, far_ref, prof_ref, mixing_ref, ham_ref, flat):
    cells_rank, comp_rank = rank_ref[0], rank_ref[1]
    mine, nfac = prof_ref.shape[0], mixing_ref.shape[0]
    gather_chunks(flat, near_ref, far_ref, cells_rank, chunk)
    prof_ref[...] = flat[pl.ds(pl.multiple_of(comp_rank * mine, mine), mine), :]
    mixing_ref[...] = flat[pl.ds(pl.multiple_of(ncomp + comp_rank * nfac, nfac), nfac), :]
    momenta = flat[0:nparam, :]
    rest = flat[nparam:, :]
    ham_ref[0, 0] = (0.5 * jnp.sum(momenta * momenta) + jnp.sum(rest)) / cells


def fast_device(
    factor_field, profile, mixing, factor_mom, profile_mom, mixing_mom, field_tau, counts, land_mask, log_exposure
):
    nfac, share, cols = factor_field.shape
    mine, ncat = profile.shape
    tile_rows = land_mask.shape[0]
    ring = lax.axis_size("comp")
    tiles = lax.axis_size("cells")
    ncomp = mine * ring
    nparam = ncomp + nfac * ncomp // LANES
    pairs = tiles // 2
    edge = 2 * nfac * cols // LANES + 8
    round_up = lambda rows: -(-rows // (8 * tiles)) * 8
    chunk_one = round_up(nparam)
    chunk_two = round_up(nparam + 1)
    comp_rank = lax.axis_index("comp")
    cells_rank = lax.axis_index("cells")
    ranks = jnp.stack([cells_rank, comp_rank]).astype(jnp.int32)
    pack = jnp.concatenate([profile, mixing], axis=0)
    parts = [pack] + [partner(pack, "comp", k) for k in range(1, ring)]

    count_rows = lax.dynamic_slice_in_dim(counts, comp_rank * share, share, 1).swapaxes(0, 1).astype(BF16)
    field_rows = factor_field.swapaxes(0, 1)
    mom_rows = factor_mom.swapaxes(0, 1)
    def full(*shape):
        zeros = (0,) * len(shape)
        return pl.BlockSpec(shape, lambda i, ranks: zeros)

    smem = pl.BlockSpec(memory_space=pltpu.SMEM)
    cell_specs = [
        smem,
        full(share, ncat, cols),
        full(share, nfac, cols),
    ]
    row_spec = pl.BlockSpec((share, cols), lambda i, ranks: (ranks[1], 0))
    param_specs = [full(mine, ncat), full(nfac, mine)]
    pack_spec = full(mine + nfac, ncat)
    shape = lambda *dims: jax.ShapeDtypeStruct(dims, F32)
    work = [
        pltpu.VMEM((ncomp, 4 * LANES), BF16),
        pltpu.VMEM((ncomp, LANES), BF16),
        pltpu.VMEM((2 * nfac, ncomp), BF16),
        pltpu.VMEM((share, 4 * LANES, cols), BF16),
        pltpu.VMEM((share, 2 * LANES, 2 * cols), BF16),
        pltpu.VMEM((share, nfac, cols), F32),
    ]
    work += [pltpu.VMEM((ncomp, cols), F32)] * 4 + [pltpu.VMEM((ncomp, 2 * cols), BF16)] * 4
    work += [
        pltpu.VMEM((ncomp, 2 * LANES), F32),
        pltpu.VMEM((ncomp, LANES), F32),
    ]
    params = pltpu.CompilerParams(vmem_limit_bytes=40 * 1024 * 1024, dimension_semantics=("arbitrary",))

    def call(body, name, ins, outs, scratch):
        return pl.pallas_call(
            body,
            name=name,
            grid_spec=pltpu.PrefetchScalarGridSpec(
                num_scalar_prefetch=1,
                grid=(1,),
                in_specs=ins,
                out_specs=[spec for spec, _ in outs],
                scratch_shapes=scratch,
            ),
            out_shape=[out for _, out in outs],
            compiler_params=params,
        )

    def block(*dims):
        return (full(*dims), shape(*dims))

    first = call(
        functools.partial(first_kernel, ncomp),
        "first_gradient",
        cell_specs + [full(share, nfac, cols), row_spec, row_spec] + param_specs + [pack_spec] * ring,
        [
            block(share, nfac, cols),
            block(share, nfac, cols),
            block(edge, LANES),
            block(edge, LANES),
            block(nparam, LANES),
            block(pairs, chunk_one, LANES),
            block(pairs, chunk_one, LANES),
        ],
        [pltpu.VMEM((tiles * chunk_one, LANES), F32)] + work,
    )
    new_field, half, near_edge, far_edge, grad, keep, send = first(
        ranks, field_tau, count_rows, field_rows, mom_rows, land_mask, log_exposure, profile_mom, mixing_mom, *parts,
    )
    near, far, got_edge = all_sum(keep, send, near_edge, far_edge)
    second = call(
        functools.partial(second_kernel, ncomp, chunk_one, ring, tiles),
        "second_gradient",
        cell_specs
        + [full(share, nfac, cols), row_spec, row_spec]
        + param_specs
        + [
            pl.BlockSpec((1, nfac, cols), lambda i, ranks: (0, 0, 0)),
            pl.BlockSpec((1, nfac, cols), lambda i, ranks: (share - 1, 0, 0)),
            pack_spec,
            full(pairs, chunk_one + edge, LANES),
            full(pairs, chunk_one + edge, LANES),
            full(edge, LANES),
            full(nparam, LANES),
        ],
        [
            block(share, nfac, cols),
            block(share, nfac, cols),
            block(mine, ncat),
            block(nfac, mine),
            block(pairs, chunk_two, LANES),
            block(pairs, chunk_two, LANES),
        ],
        [pltpu.VMEM((tiles * chunk_one, LANES), F32)]
        + work
        + [pltpu.VMEM((tiles * chunk_two, LANES), F32), pltpu.VMEM((nparam, LANES), F32)],
    )
    new_field, new_mom, new_profile, new_mixing, keep, send = second(
        ranks, field_tau, count_rows, new_field, half, land_mask, log_exposure, profile_mom, mixing_mom, field_rows,
        field_rows, pack, near, far, got_edge, grad,
    )
    near, far, _ = all_sum(keep, send)
    final = call(
        functools.partial(last_kernel, ncomp, nparam, chunk_two, tile_rows * cols * tiles),
        "momenta",
        [full(pairs, chunk_two, LANES), full(pairs, chunk_two, LANES)],
        [block(mine, ncat), block(nfac, mine), (smem, shape(1, 1))],
        [pltpu.VMEM((tiles * chunk_two, LANES), F32)],
    )
    new_profile_mom, new_mixing_mom, hamiltonian = final(ranks, near, far)
    return (
        new_field.swapaxes(0, 1),
        new_profile,
        new_mixing,
        new_mom.swapaxes(0, 1),
        new_profile_mom,
        new_mixing_mom,
        hamiltonian.reshape(()),
    )


def power_of_two(count):
    return count & (count - 1) == 0


def choose_device(*args):
    factor_field, profile, mixing = args[:3]
    nfac, share, cols = factor_field.shape
    mine, ncat = profile.shape
    tiles, ring = lax.axis_size("cells"), lax.axis_size("comp")
    fits = mine == LANES and ncat == LANES and nfac % 16 == 0 and 6 * nfac + 6 <= LANES
    fits = fits and share % 8 == 0 and cols % LANES == 0 and cols <= 8 * LANES
    fits = fits and power_of_two(tiles) and tiles > 1 and ring == 4
    return fast_device(*args) if fits else plain_device(*args)


def solution(mesh):
    in_specs = (
        P(None, ("cells", "comp"), None),
        P("comp", None),
        P(None, "comp"),
        P(None, ("cells", "comp"), None),
        P("comp", None),
        P(None, "comp"),
        P(),
        P(None, "cells", None),
        P("cells", None),
        P("cells", None),
    )
    out_specs = (
        P(None, ("cells", "comp"), None),
        P("comp", None),
        P(None, "comp"),
        P(None, ("cells", "comp"), None),
        P("comp", None),
        P(None, "comp"),
        P(),
    )
    return jax.shard_map(
        choose_device, mesh=mesh, in_specs=in_specs, out_specs=out_specs, check_vma=False
    )
```

```python
import functools
import math

import jax
import jax.numpy as jnp
from jax import lax
from jax.experimental import pallas as pl
from jax.experimental.pallas import tpu as pltpu
from jax.sharding import PartitionSpec as P


def extended(cells, sides, width):
    for axis, dim in sides:
        count = lax.axis_size(axis)
        ends = count - 1
        head = lax.slice_in_dim(cells, 0, width, axis=dim)
        tail = lax.slice_in_dim(cells, cells.shape[dim] - width, cells.shape[dim], axis=dim)
        cells = jnp.concatenate(
            [
                lax.ppermute(tail, axis, [(i, (i + 1) % count) for i in range(ends)]),
                cells,
                lax.ppermute(head, axis, [((i + 1) % count, i) for i in range(ends)]),
            ],
            axis=dim,
        )
    return cells


def field_prior(padded, land_pad, field_tau):
    ridge = 0.1
    step_x = padded[:, 1:, :] - padded[:, :-1, :]
    edge_x = land_pad[1:, :] * land_pad[:-1, :]
    flux_x = edge_x[None, :, :] * step_x
    centre = padded[:, 1:-1, :]
    land_mid = land_pad[1:-1, :]
    step_y = centre[:, :, 1:] - centre[:, :, :-1]
    edge_y = land_mid[:, 1:] * land_mid[:, :-1]
    flux_y = edge_y[None, :, :] * step_y
    lap_x = flux_x[:, :-1, :] - flux_x[:, 1:, :]
    lap_y = jnp.pad(flux_y, ((0, 0), (0, 0), (1, 0))) - jnp.pad(flux_y, ((0, 0), (0, 0), (0, 1)))
    tau_cube = field_tau[:, None, None]
    grad = -tau_cube * (lap_x + lap_y + ridge * centre)
    energy = 0.5 * jnp.sum(tau_cube * (flux_x[:, 1:, :] * step_x[:, 1:, :]))
    energy = energy + 0.5 * jnp.sum(tau_cube * (flux_y * step_y))
    energy = energy + 0.5 * ridge * jnp.sum(tau_cube * (centre * centre))
    return (grad, energy)


def tile_scores(flat_tile, count_rows, exposure, profile, mixing):
    prof_exp = jnp.exp(profile)
    rate_total = jnp.sum(prof_exp, axis=1)
    mix_logit = jnp.dot(mixing.T, flat_tile, precision=lax.Precision.HIGHEST)
    fit_score = (
        jnp.dot(profile, count_rows, precision=lax.Precision.HIGHEST)
        - rate_total[:, None] * exposure[None, :]
    )
    return (mix_logit, mix_logit + fit_score)


def tile_grads(
    flat_tile, count_rows, land_weight, exposure, mixing, mix_logit, joint_score, log_mix, log_joint
):
    prior_share = jnp.exp(mix_logit - log_mix[None, :])
    posterior = jnp.exp(joint_score - log_joint[None, :])
    post_land = posterior * land_weight[None, :]
    gap_weight = (posterior - prior_share) * land_weight[None, :]
    grad_counts = jnp.dot(post_land, count_rows.T, precision=lax.Precision.HIGHEST)
    rate_mass = jnp.sum(post_land * exposure[None, :], axis=1)
    grad_mix = jnp.dot(flat_tile, gap_weight.T, precision=lax.Precision.HIGHEST)
    field_lik = jnp.dot(mixing, gap_weight, precision=lax.Precision.HIGHEST)
    log_dens = jnp.sum(land_weight * (log_joint - log_mix))
    return (grad_counts, rate_mass, grad_mix, field_lik, log_dens)


def log_sum(scores):
    top = jnp.max(scores, axis=0)
    return top + jnp.log(jnp.sum(jnp.exp(scores - top[None, :]), axis=0))


def plain_device(
    factor_field,
    profile,
    mixing,
    factor_mom,
    profile_mom,
    mixing_mom,
    field_tau,
    counts,
    land_mask,
    log_exposure,
):
    step_field = 0.05
    step_profile = 0.002
    step_mixing = 0.002
    tile_rows, tile_cols = land_mask.shape
    ncat = counts.shape[0]
    share_rows = factor_field.shape[1]
    comp_rank = lax.axis_index("comp")
    cells_rank = lax.axis_index("cells")
    first_cells = cells_rank == 0
    land_pad = extended(land_mask, (("cells", 0),), 1).astype(jnp.float32)
    row_start = comp_rank * share_rows
    count_rows = lax.dynamic_slice_in_dim(counts, row_start, share_rows, 1)
    count_rows = count_rows.reshape(ncat, share_rows * tile_cols).astype(jnp.float32)
    land_weight = (
        lax.dynamic_slice_in_dim(land_mask, row_start, share_rows, 0)
        .reshape(-1)
        .astype(jnp.float32)
    )
    exposure = jnp.exp(lax.dynamic_slice_in_dim(log_exposure, row_start, share_rows, 0).reshape(-1))
    land_near = lax.dynamic_slice_in_dim(land_pad, row_start, share_rows + 2, 0)

    def evaluate(share_field, profile_now, mixing_now):
        padded = extended(share_field, ((("cells", "comp"), 1),), 1)
        prior_grad, prior_energy = field_prior(padded, land_near, field_tau)
        profile_all, mixing_all = (
            lax.all_gather(profile_now, "comp", axis=0, tiled=True),
            lax.all_gather(mixing_now, "comp", axis=1, tiled=True),
        )
        flat_tile = share_field.reshape(share_field.shape[0], -1)
        mix_logit, joint_score = tile_scores(
            flat_tile, count_rows, exposure, profile_all, mixing_all
        )
        log_mix = log_sum(mix_logit)
        log_joint = log_sum(joint_score)
        grad_counts, rate_mass, grad_mix, field_lik, log_dens = tile_grads(
            flat_tile,
            count_rows,
            land_weight,
            exposure,
            mixing_all,
            mix_logit,
            joint_score,
            log_mix,
            log_joint,
        )
        grad_counts, rate_mass, mix_rows = (
            lax.psum_scatter(grad_counts, "comp", scatter_dimension=0, tiled=True),
            lax.psum_scatter(rate_mass, "comp", scatter_dimension=0, tiled=True),
            lax.psum_scatter(grad_mix.T, "comp", scatter_dimension=0, tiled=True),
        )
        grad_mix = mix_rows.T
        grad_field = prior_grad + field_lik.reshape(share_field.shape)
        log_part = log_dens - prior_energy
        grad_counts, rate_mass, grad_mix = lax.psum((grad_counts, rate_mass, grad_mix), "cells")
        grad_profile = grad_counts - jnp.exp(profile_now) * rate_mass[:, None] - 0.25 * profile_now
        grad_mixing = grad_mix - mixing_now
        param_prior = -0.125 * jnp.sum(profile_now * profile_now) - 0.5 * jnp.sum(
            mixing_now * mixing_now
        )
        log_part = log_part + jnp.where(first_cells, param_prior, 0.0)
        return (log_part, grad_field, grad_profile, grad_mixing)

    first = evaluate(factor_field, profile, mixing)
    half_field = factor_mom + 0.5 * step_field * first[1]
    half_profile = profile_mom + 0.5 * step_profile * first[2]
    half_mixing = mixing_mom + 0.5 * step_mixing * first[3]
    new_field = factor_field + step_field * half_field
    new_profile = profile + step_profile * half_profile
    new_mixing = mixing + step_mixing * half_mixing
    second = evaluate(new_field, new_profile, new_mixing)
    new_factor_mom = half_field + 0.5 * step_field * second[1]
    new_profile_mom = half_profile + 0.5 * step_profile * second[2]
    new_mixing_mom = half_mixing + 0.5 * step_mixing * second[3]
    kinetic = 0.5 * jnp.sum(new_factor_mom * new_factor_mom)
    kinetic = kinetic + jnp.where(
        first_cells,
        0.5
        * (jnp.sum(new_profile_mom * new_profile_mom) + jnp.sum(new_mixing_mom * new_mixing_mom)),
        0.0,
    )
    log_total, kinetic_total = lax.psum((second[0], kinetic), ("cells", "comp"))
    cell_count = tile_rows * tile_cols * lax.axis_size("cells")
    hamiltonian = (kinetic_total - log_total) / cell_count
    return (
        new_field,
        new_profile,
        new_mixing,
        new_factor_mom,
        new_profile_mom,
        new_mixing_mom,
        hamiltonian,
    )


STEP_FIELD = 0.05
STEP_PARAM = 0.002
RIDGE = 0.1
LOG2E = math.log2(math.e)
LN2 = math.log(2.0)
LANES = 128
EXTRA = 16
F32 = jnp.float32
BF16 = jnp.bfloat16


def pieces(values, count):
    parts = []
    for _ in range(count):
        part = values.astype(BF16)
        parts.append(part)
        values = values - part.astype(F32)
    return parts


def dot(left, right, dims=((1,), (0,))):
    return lax.dot_general(left, right, (dims, ((), ())), preferred_element_type=F32)


def partner(values, axis, flip):
    count = lax.axis_size(axis)
    return lax.ppermute(values, axis, [(i, i ^ flip) for i in range(count)])


def all_sum(keep, send, near_edge=None, far_edge=None, beside=()):
    pairs, rows, _ = keep.shape
    chunks = keep + partner(send, "cells", 1)
    total = chunks[0]
    for part in [partner(chunks[k], "cells", 2 * k) for k in range(1, pairs)]:
        total = total + part
    total, beside = lax.optimization_barrier((total, beside))
    if near_edge is None:
        parts = [partner(total, "comp", k) for k in range(1, lax.axis_size("comp"))]
        near_got = None
        for part in parts:
            total = total + part
    else:
        first = partner(jnp.concatenate([total, near_edge], axis=0), "comp", 1)
        second = partner(total, "comp", 2)
        third = partner(jnp.concatenate([total, far_edge], axis=0), "comp", 3)
        near_got = first[rows:]
        total = jnp.concatenate([total + first[:rows] + second + third[:rows], third[rows:]], axis=0)
    near = jnp.stack([total] + [partner(total, "cells", 2 * k) for k in range(1, pairs)])
    return near, partner(near, "cells", 1), near_got, beside


def gather_params(pack, cells_rank):
    tiles, ring = lax.axis_size("cells"), lax.axis_size("comp")
    rows = pack.shape[0]
    spread = [(c * ring + z, c * ring + (z ^ (1 + c % 2))) for c in range(tiles) for z in range(ring)]
    one = lax.ppermute(pack, ("cells", "comp"), spread)
    half = lax.dynamic_slice_in_dim(pack, cells_rank % 2 * (rows // 2), rows // 2, 0)
    got = jnp.concatenate([one, partner(half, "comp", 3)], axis=0)
    return got, partner(got, "cells", 1)


def chunk_index(cells_rank, k, other):
    core = cells_rank % 2
    return (((cells_rank // 2) ^ k) * 2) + (1 - core if other else core)


def gather_chunks(flat_ref, near_ref, far_ref, cells_rank, rows):
    for k in range(near_ref.shape[0]):
        for source, other in ((near_ref, False), (far_ref, True)):
            start = pl.multiple_of(chunk_index(cells_rank, k, other) * rows, 8)
            flat_ref[pl.ds(start, rows), :] = source[k, 0:rows, :]


def spread_chunks(flat_ref, keep_ref, send_ref, cells_rank):
    pairs, rows, _ = keep_ref.shape
    for k in range(pairs):
        for target, other in ((keep_ref, False), (send_ref, True)):
            start = pl.multiple_of(chunk_index(cells_rank, k, other) * rows, 8)
            target[k] = flat_ref[pl.ds(start, rows), :]


def load_params(flat_ref, left_ref, mix_ref, load_ref, ncomp, nfac):
    lane = lax.broadcasted_iota(jnp.int32, (LANES, LANES), 1)
    spare = jnp.zeros((LANES - EXTRA - 6 * nfac, LANES), F32)
    for q in range(ncomp // LANES):
        rows = pl.ds(q * LANES, LANES)
        prof = flat_ref[rows, :]
        high, mid, low = pieces(prof * LOG2E, 3)
        left_ref[rows, 0:LANES] = high
        left_ref[rows, 2 * LANES : 3 * LANES] = mid
        left_ref[rows, 3 * LANES : 4 * LANES] = low
        rate = jnp.sum(jnp.exp(prof), axis=1, keepdims=True) * LOG2E
        rate_high, rate_mid, rate_low = [part.astype(F32) for part in pieces(rate, 3)]
        load = flat_ref[pl.ds(ncomp + q * nfac, nfac), :]
        w_high, w_mid, w_low = [part.astype(F32) for part in pieces(load * LOG2E, 3)]
        stack = jnp.concatenate(
            [jnp.zeros((EXTRA, LANES), F32), w_high, w_high, w_high, w_mid, w_mid, w_low, spare], axis=0
        )
        turned = stack.T
        mix_ref[rows, :] = turned.astype(BF16)
        rate_part = jnp.where(
            lane < 3, rate_high, jnp.where(lane < 5, rate_mid, jnp.where(lane == 5, rate_low, 0.0))
        )
        left_ref[rows, LANES : 2 * LANES] = (turned - rate_part).astype(BF16)
        load_high, load_mid = pieces(load, 2)
        load_ref[0:nfac, q * LANES : (q + 1) * LANES] = load_high
        load_ref[nfac : 2 * nfac, q * LANES : (q + 1) * LANES] = load_mid


def load_cells(counts_ref, field_ref, log_exposure, right_ref, wide_ref):
    share, ncat, cols = counts_ref.shape
    nfac = field_ref.shape[1]
    exposure = jnp.exp(log_exposure)
    sub = lax.broadcasted_iota(jnp.int32, (EXTRA, cols), 0)
    spare = jnp.zeros((LANES - EXTRA - 6 * nfac, cols), BF16)
    for r in range(share):
        count = counts_ref[r]
        high, mid, low = pieces(field_ref[r], 3)
        e_high, e_mid, e_low = [part.astype(F32) for part in pieces(exposure[r : r + 1, :], 3)]
        e_rows = jnp.where((sub == 0) | (sub == 3) | (sub == 5), e_high, 0.0)
        e_rows = jnp.where((sub == 1) | (sub == 4), e_mid, e_rows)
        e_rows = jnp.where(sub == 2, e_low, e_rows).astype(BF16)
        extra = jnp.concatenate([e_rows, high, mid, low, high, mid, high, spare], axis=0)
        right_ref[r, 0:ncat, :] = count
        right_ref[r, LANES : 2 * LANES, :] = extra
        right_ref[r, 2 * LANES : 2 * LANES + ncat, :] = count
        right_ref[r, 3 * LANES : 3 * LANES + ncat, :] = count
        for side in range(2):
            wide_ref[r, 0:ncat, side * cols : (side + 1) * cols] = count
            wide_ref[r, LANES : 2 * LANES, side * cols : (side + 1) * cols] = extra


def field_weights(tau_ref, nfac, cols):
    row = lax.broadcasted_iota(jnp.int32, (nfac, cols), 0)
    tau = jnp.zeros((nfac, cols), F32)
    for j in range(nfac):
        tau = jnp.where(row == j, tau_ref[j], tau)
    return tau


def load_prior(rows, lands, tau, prior_ref):
    nfac, cols = tau.shape
    inner = lax.broadcasted_iota(jnp.int32, (nfac, cols), 1) < cols - 1
    energy = jnp.zeros((nfac, cols), F32)
    lands = [jnp.broadcast_to(x, (nfac, cols)) for x in lands]
    for r in range(len(rows) - 2):
        here = rows[r + 1]
        step_right = here - pltpu.roll(here, cols - 1, 1)
        edge_right = jnp.where(inner, lands[r + 1] * pltpu.roll(lands[r + 1], cols - 1, 1), 0.0)
        flux_right = edge_right * step_right
        laplace = flux_right - pltpu.roll(flux_right, 1, 1)
        parts = flux_right * step_right + RIDGE * (here * here)
        if rows[r] is not None:
            laplace = laplace + lands[r] * lands[r + 1] * (here - rows[r])
        if rows[r + 2] is not None:
            step_down = here - rows[r + 2]
            flux_down = lands[r + 1] * lands[r + 2] * step_down
            laplace = laplace + flux_down
            parts = parts + flux_down * step_down
        prior_ref[r] = -tau * (laplace + RIDGE * here)
        energy = energy + 0.5 * tau * parts
    return energy


def pack_edge(edge_ref, field, fresh, land):
    nfac, cols = field.shape
    blocks = cols // LANES
    sub = lax.broadcasted_iota(jnp.int32, (8, LANES), 0)
    lands = jnp.zeros((8, LANES), F32)
    for b in range(blocks):
        lanes = slice(b * LANES, (b + 1) * LANES)
        edge_ref[b * nfac : (b + 1) * nfac, :] = field[:, lanes]
        edge_ref[(blocks + b) * nfac : (blocks + b + 1) * nfac, :] = fresh[:, lanes]
        lands = jnp.where(sub == b, land[:, lanes], lands)
    edge_ref[2 * blocks * nfac :, :] = lands


def unpack_edge(edge, nfac, cols):
    blocks = cols // LANES
    wide = lambda start, size, step: jnp.concatenate(
        [edge[start + b * step : start + b * step + size, :] for b in range(blocks)], axis=1
    )
    return wide(0, nfac, nfac), wide(blocks * nfac, nfac, nfac), wide(2 * blocks * nfac, 1, 1)


def row_scores(r, right_ref, left_ref, mix_ref, score_ref, logit_ref):
    tops = []
    for target, values in (
        (score_ref, dot(left_ref[...], right_ref[r])),
        (logit_ref, dot(mix_ref[...], right_ref[r, LANES : 2 * LANES, :])),
    ):
        target[...] = values
        ncomp, cols = values.shape
        tops.append(jnp.max(jnp.max(values.reshape(ncomp // 8, 8, cols), axis=0), axis=0, keepdims=True))
    return tops


def row_shares(tops, land, score_ref, logit_ref, post_ref, gap_ref):
    ncomp, cols = score_ref.shape
    block = 32
    top_s, top_a = tops
    sum_s = jnp.zeros((8, cols), F32)
    sum_a = jnp.zeros((8, cols), F32)
    for i in range(0, ncomp, block):
        part_s = jnp.exp2(score_ref[i : i + block, :] - top_s)
        part_a = jnp.exp2(logit_ref[i : i + block, :] - top_a)
        score_ref[i : i + block, :] = part_s
        logit_ref[i : i + block, :] = part_a
        sum_s = sum_s + jnp.sum(part_s.reshape(block // 8, 8, cols), axis=0)
        sum_a = sum_a + jnp.sum(part_a.reshape(block // 8, 8, cols), axis=0)
    sum_s = jnp.sum(sum_s, axis=0, keepdims=True)
    sum_a = jnp.sum(sum_a, axis=0, keepdims=True)
    log_s = top_s + jnp.log2(sum_s)
    log_a = top_a + jnp.log2(sum_a)
    inv_s = land / sum_s
    inv_a = land / sum_a
    for i in range(0, ncomp, block):
        post = score_ref[i : i + block, :] * inv_s
        gap = post - logit_ref[i : i + block, :] * inv_a
        for target, values in ((post_ref, post), (gap_ref, gap)):
            high, low = pieces(values, 2)
            target[i : i + block, 0:cols] = high
            target[i : i + block, cols : 2 * cols] = low
    return land * (LN2 * (log_s - log_a))


def row_products(r, wide_ref, load_ref, post_ref, gap_ref, acc_ref, accw_ref, prior_ref):
    nfac = load_ref.shape[0] // 2
    cols = prior_ref.shape[2]
    last = ((1,), (1,))
    start = LANES + EXTRA
    acc = dot(post_ref[...], wide_ref[r], last)
    accw = dot(wide_ref[r, start : start + 3 * nfac, :], gap_ref[...], last)
    if r == 0:
        acc_ref[...] = acc
        accw_ref[...] = accw
    else:
        acc_ref[...] += acc
        accw_ref[...] += accw
    lik = dot(load_ref[...], gap_ref[...])
    lik = lik[0:nfac] + lik[nfac : 2 * nfac]
    prior_ref[r] += lik[:, 0:cols] + lik[:, cols : 2 * cols]


def all_rows(land, right, wide, left, mix, load, scores, logits, posts, gaps, acc, accw, prior):
    share, _, cols = prior.shape
    log_dens = jnp.zeros((1, cols), F32)
    tops = {}
    for r in range(share + 2):
        if r < share:
            tops[r] = row_scores(r, right, left, mix, scores[r % 2], logits[r % 2])
        if 0 <= r - 1 < share:
            p = r - 1
            log_dens = log_dens + row_shares(
                tops[p], land[p : p + 1, :], scores[p % 2], logits[p % 2], posts[p % 2], gaps[p % 2]
            )
        if 0 <= r - 2:
            p = r - 2
            row_products(p, wide, load, posts[p % 2], gaps[p % 2], acc, accw, prior)
    return log_dens


def param_grads(flat_ref, acc_ref, accw_ref, grad_ref, ncomp, nfac):
    lane = lax.broadcasted_iota(jnp.int32, (LANES, LANES), 1)
    for q in range(ncomp // LANES):
        rows = pl.ds(q * LANES, LANES)
        lanes = slice(q * LANES, (q + 1) * LANES)
        mass = jnp.sum(jnp.where(lane < 3, acc_ref[rows, LANES : 2 * LANES], 0.0), axis=1, keepdims=True)
        grad_ref[rows, :] = acc_ref[rows, 0:LANES] - jnp.exp(flat_ref[rows, :]) * mass
        load = accw_ref[:, lanes]
        grad_ref[pl.ds(ncomp + q * nfac, nfac), :] = load[0:nfac] + load[nfac : 2 * nfac] + load[2 * nfac : 3 * nfac]


def first_kernel(
    ncomp, rank_ref, tau_ref, counts_ref, field_ref, mom_ref, land_ref, logexp_ref, pmom_ref, wmom_ref, *refs
):
    (pack_ref, got_ref, others_ref, new_ref, half_ref, near_ref, far_ref, grad_ref, keep_ref, send_ref) = refs[:10]
    (flat, left, mix, load, right, wide, prior, score0, score1, logit0, logit1, post0, post1, gap0, gap1, acc, accw) = (
        refs[10:27]
    )
    (stage,) = refs[27:]
    cells_rank, comp_rank = rank_ref[0], rank_ref[1]
    share, nfac, cols = field_ref.shape
    mine = pmom_ref.shape[0]
    core = cells_rank % 2
    size = mine + nfac
    for source, side in ((got_ref, core), (others_ref, 1 - core)):
        stage[pl.ds(pl.multiple_of(side * (size // 2), 8), size // 2), :] = source[size:, :]
    for source, group in (
        (pack_ref, comp_rank),
        (got_ref, comp_rank ^ (1 + core)),
        (others_ref, comp_rank ^ (2 - core)),
        (stage, comp_rank ^ 3),
    ):
        flat[pl.ds(pl.multiple_of(group * mine, mine), mine), :] = source[0:mine, :]
        flat[pl.ds(pl.multiple_of(ncomp + group * nfac, nfac), nfac), :] = source[mine:size, :]
    here = pl.ds(pl.multiple_of(comp_rank * share, 8), share)
    land = land_ref[here, :].astype(F32)
    load_params(flat, left, mix, load, ncomp, nfac)
    load_cells(counts_ref, field_ref, logexp_ref[here, :], right, wide)
    lands = [land[r : r + 1, :] for r in range(share)]
    tau = field_weights(tau_ref, nfac, cols)
    load_prior([None] + [field_ref[r] for r in range(share)] + [None], lands[:1] + lands + lands[-1:], tau, prior)
    all_rows(
        land, right, wide, left, mix, load, (score0, score1), (logit0, logit1), (post0, post1), (gap0, gap1), acc, accw,
        prior,
    )
    for r in range(share):
        half = mom_ref[r] + 0.5 * STEP_FIELD * prior[r]
        half_ref[r] = half
        new_ref[r] = field_ref[r] + STEP_FIELD * half
    even = comp_rank % 2 == 0
    end = share - 1
    for target, flag in ((near_ref, even), (far_ref, jnp.logical_not(even))):
        pack_edge(
            target,
            jnp.where(flag, field_ref[end], field_ref[0]),
            jnp.where(flag, new_ref[end], new_ref[0]),
            jnp.where(flag, lands[end], lands[0]),
        )
    param_grads(flat, acc, accw, grad_ref, ncomp, nfac)
    nparam = grad_ref.shape[0]
    if flat.shape[0] > nparam:
        flat[nparam:, :] = jnp.zeros((flat.shape[0] - nparam, LANES), F32)
    flat[0:nparam, :] = 0.5 * STEP_PARAM * STEP_PARAM * grad_ref[...]
    own_prof, own_load = pack_ref[0:mine, :], pack_ref[mine:size, :]
    owner = cells_rank == 0
    base_prof = own_prof + STEP_PARAM * (pmom_ref[...] - 0.5 * STEP_PARAM * 0.25 * own_prof)
    base_load = own_load + STEP_PARAM * (wmom_ref[...] - 0.5 * STEP_PARAM * own_load)
    flat[pl.ds(pl.multiple_of(comp_rank * mine, mine), mine), :] += jnp.where(owner, base_prof, 0.0)
    flat[pl.ds(pl.multiple_of(ncomp + comp_rank * nfac, nfac), nfac), :] += jnp.where(owner, base_load, 0.0)
    spread_chunks(flat, keep_ref, send_ref, cells_rank)


def second_kernel(
    ncomp, chunk, ring, tiles, rank_ref, tau_ref, counts_ref, field_ref, half_ref, land_ref, logexp_ref, pmom_ref, wmom_ref,
    old_ref, own_ref, near_ref, far_ref, edge_ref, grad0_ref, new_ref, mom_ref, params_ref,
    keep_ref, send_ref,
    flat, left, mix, load, right, wide, prior, score0, score1, logit0, logit1, post0, post1, gap0, gap1, acc, accw, out,
    grad,
):
    cells_rank, comp_rank = rank_ref[0], rank_ref[1]
    share, nfac, cols = field_ref.shape
    mine = pmom_ref.shape[0]
    nparam = grad0_ref.shape[0]
    gather_chunks(flat, near_ref, far_ref, cells_rank, chunk)
    new_prof = flat[pl.ds(pl.multiple_of(comp_rank * mine, mine), mine), :]
    new_load = flat[pl.ds(pl.multiple_of(ncomp + comp_rank * nfac, nfac), nfac), :]
    params_ref[0:mine, :] = new_prof
    params_ref[mine:, :] = new_load
    here = pl.ds(pl.multiple_of(comp_rank * share, 8), share)
    land = land_ref[here, :].astype(F32)
    lands = [land[r : r + 1, :] for r in range(share)]
    tau = field_weights(tau_ref, nfac, cols)

    source = jnp.where(comp_rank == 0, cells_rank - 1, jnp.where(comp_rank == ring - 1, cells_rank + 1, cells_rank))
    source = jnp.clip(source, 0, tiles - 1)
    slot = (source // 2) ^ (cells_rank // 2)
    relay = jnp.where(source % 2 == cells_rank % 2, near_ref[slot, chunk:, :], far_ref[slot, chunk:, :])
    even = comp_rank % 2 == 0
    direct = edge_ref[...]
    above = unpack_edge(jnp.where(even, relay, direct), nfac, cols)
    below = unpack_edge(jnp.where(even, direct, relay), nfac, cols)
    land_above = jnp.where((comp_rank == 0) & (cells_rank == 0), 0.0, above[2])
    land_below = jnp.where((comp_rank == ring - 1) & (cells_rank == tiles - 1), 0.0, below[2])
    end = share - 1
    pull_up = -tau * (land_above * lands[0]) * (old_ref[0] - above[0])
    pull_down = -tau * (land_below * lands[end]) * (old_ref[end] - below[0])
    move = 0.5 * STEP_FIELD * STEP_FIELD
    for r in range(share):
        fresh = field_ref[r]
        if r == 0:
            fresh = fresh + move * pull_up
        if r == end:
            fresh = fresh + move * pull_down
        new_ref[r] = fresh
    load_params(flat, left, mix, load, ncomp, nfac)
    load_cells(counts_ref, new_ref, logexp_ref[here, :], right, wide)
    rows = [above[1] - move * pull_up] + [new_ref[r] for r in range(share)] + [below[1] - move * pull_down]
    energy = load_prior(rows, [land_above] + lands + [land_below], tau, prior)
    prior[0] += pull_up
    prior[end] += pull_down

    log_dens = all_rows(
        land, right, wide, left, mix, load, (score0, score1), (logit0, logit1), (post0, post1), (gap0, gap1), acc, accw,
        prior,
    )
    for r in range(share):
        fresh = half_ref[r] + 0.5 * STEP_FIELD * prior[r]
        mom_ref[r] = fresh
        energy = energy + 0.5 * (fresh * fresh)
    param_grads(flat, acc, accw, grad, ncomp, nfac)
    first_device = (cells_rank == 0) & (comp_rank == 0)
    prof_all = flat[0:ncomp, :]
    load_all = flat[ncomp:nparam, :]
    param_energy = jnp.sum(0.125 * (prof_all * prof_all)) + jnp.sum(0.5 * (load_all * load_all))
    total = jnp.sum(energy) - jnp.sum(log_dens) + jnp.where(first_device, param_energy, 0.0)
    out[0:nparam, :] = 0.5 * STEP_PARAM * (grad0_ref[...] + grad[...])
    tail = out.shape[0] - nparam
    spot = lax.broadcasted_iota(jnp.int32, (tail, LANES), 0) + lax.broadcasted_iota(jnp.int32, (tail, LANES), 1)
    out[nparam:, :] = jnp.where(spot == 0, total, 0.0)
    owner = cells_rank == 0
    old_prof, old_load = own_ref[0:mine, :], own_ref[mine : mine + nfac, :]
    base_prof = pmom_ref[...] - 0.5 * STEP_PARAM * 0.25 * (old_prof + new_prof)
    base_load = wmom_ref[...] - 0.5 * STEP_PARAM * (old_load + new_load)
    out[pl.ds(pl.multiple_of(comp_rank * mine, mine), mine), :] += jnp.where(owner, base_prof, 0.0)
    out[pl.ds(pl.multiple_of(ncomp + comp_rank * nfac, nfac), nfac), :] += jnp.where(owner, base_load, 0.0)
    spread_chunks(out, keep_ref, send_ref, cells_rank)


def last_kernel(ncomp, nparam, chunk, cells, rank_ref, near_ref, far_ref, prof_ref, mixing_ref, ham_ref, flat):
    cells_rank, comp_rank = rank_ref[0], rank_ref[1]
    mine, nfac = prof_ref.shape[0], mixing_ref.shape[0]
    gather_chunks(flat, near_ref, far_ref, cells_rank, chunk)
    prof_ref[...] = flat[pl.ds(pl.multiple_of(comp_rank * mine, mine), mine), :]
    mixing_ref[...] = flat[pl.ds(pl.multiple_of(ncomp + comp_rank * nfac, nfac), nfac), :]
    momenta = flat[0:nparam, :]
    rest = flat[nparam:, :]
    ham_ref[0, 0] = (0.5 * jnp.sum(momenta * momenta) + jnp.sum(rest)) / cells


def fast_device(
    factor_field, profile, mixing, factor_mom, profile_mom, mixing_mom, field_tau, counts, land_mask, log_exposure
):
    nfac, share, cols = factor_field.shape
    mine, ncat = profile.shape
    tile_rows = land_mask.shape[0]
    ring = lax.axis_size("comp")
    tiles = lax.axis_size("cells")
    ncomp = mine * ring
    nparam = ncomp + nfac * ncomp // LANES
    pairs = tiles // 2
    edge = 2 * nfac * cols // LANES + 8
    round_up = lambda rows: -(-rows // (8 * tiles)) * 8
    chunk_one = round_up(nparam)
    chunk_two = round_up(nparam + 1)
    comp_rank = lax.axis_index("comp")
    cells_rank = lax.axis_index("cells")
    ranks = jnp.stack([cells_rank, comp_rank]).astype(jnp.int32)
    pack = jnp.pad(profile, ((0, nfac), (0, 0))) + jnp.pad(mixing, ((mine, 0), (0, 0)))
    got, others = gather_params(pack, cells_rank)
    count_rows = lax.dynamic_slice_in_dim(counts, comp_rank * share, share, 1).swapaxes(0, 1).astype(BF16)
    field_rows = factor_field.swapaxes(0, 1)
    mom_rows = factor_mom.swapaxes(0, 1)
    vmem = pl.BlockSpec(memory_space=pltpu.VMEM)
    smem = pl.BlockSpec(memory_space=pltpu.SMEM)
    shape = lambda *dims: jax.ShapeDtypeStruct(dims, F32)
    work = [
        pltpu.VMEM((ncomp, 4 * LANES), BF16),
        pltpu.VMEM((ncomp, LANES), BF16),
        pltpu.VMEM((2 * nfac, ncomp), BF16),
        pltpu.VMEM((share, 4 * LANES, cols), BF16),
        pltpu.VMEM((share, 2 * LANES, 2 * cols), BF16),
        pltpu.VMEM((share, nfac, cols), F32),
    ]
    work += [pltpu.VMEM((ncomp, cols), F32)] * 4 + [pltpu.VMEM((ncomp, 2 * cols), BF16)] * 4
    work += [
        pltpu.VMEM((ncomp, 2 * LANES), F32),
        pltpu.VMEM((3 * nfac, ncomp), F32),
    ]
    def call(body, name, smem_count, vmem_count, outs, scratch):
        return pl.pallas_call(
            body,
            name=name,
            in_specs=[smem] * smem_count + [vmem] * vmem_count,
            out_specs=[smem if out.shape == (1, 1) else vmem for out in outs],
            scratch_shapes=scratch,
            out_shape=outs,
            compiler_params=pltpu.CompilerParams(vmem_limit_bytes=40 * 1024 * 1024),
        )

    first = call(
        functools.partial(first_kernel, ncomp),
        "first_gradient",
        2,
        7 + 3,
        [
            shape(share, nfac, cols),
            shape(share, nfac, cols),
            shape(edge, LANES),
            shape(edge, LANES),
            shape(nparam, LANES),
            shape(pairs, chunk_one, LANES),
            shape(pairs, chunk_one, LANES),
        ],
        [pltpu.VMEM((tiles * chunk_one, LANES), F32)] + work + [pltpu.VMEM((mine + nfac, LANES), F32)],
    )
    part_field, half, near_edge, far_edge, grad, keep, send = first(
        ranks, field_tau, count_rows, field_rows, mom_rows, land_mask, log_exposure, profile_mom, mixing_mom, pack, got, others
    )
    near, far, got_edge, _ = all_sum(keep, send, near_edge, far_edge)
    second = call(
        functools.partial(second_kernel, ncomp, chunk_one, ring, tiles),
        "second_gradient",
        2,
        7 + 6,
        [
            shape(share, nfac, cols),
            shape(share, nfac, cols),
            shape(mine + nfac, ncat),
            shape(pairs, chunk_two, LANES),
            shape(pairs, chunk_two, LANES),
        ],
        [pltpu.VMEM((tiles * chunk_one, LANES), F32)]
        + work
        + [pltpu.VMEM((tiles * chunk_two, LANES), F32), pltpu.VMEM((nparam, LANES), F32)],
    )
    new_field, new_mom, new_params, keep, send = second(
        ranks, field_tau, count_rows, part_field, half, land_mask, log_exposure, profile_mom, mixing_mom, field_rows, pack,
        near, far, got_edge, grad,
    )
    done = (new_field.swapaxes(0, 1), new_params[:mine], new_params[mine:], new_mom.swapaxes(0, 1))
    near, far, _, done = all_sum(keep, send, beside=done)
    final = call(
        functools.partial(last_kernel, ncomp, nparam, chunk_two, tile_rows * cols * tiles),
        "momenta",
        1,
        2,
        [shape(mine, ncat), shape(nfac, mine), shape(1, 1)],
        [pltpu.VMEM((tiles * chunk_two, LANES), F32)],
    )
    new_profile_mom, new_mixing_mom, hamiltonian = final(ranks, near, far)
    return (
        *done,
        new_profile_mom,
        new_mixing_mom,
        hamiltonian.reshape(()),
    )


def power_of_two(count):
    return count & (count - 1) == 0


def choose_device(*args):
    factor_field, profile, mixing = args[:3]
    nfac, share, cols = factor_field.shape
    mine, ncat = profile.shape
    tiles, ring = lax.axis_size("cells"), lax.axis_size("comp")
    fits = mine == LANES and ncat == LANES and nfac % 16 == 0 and 6 * nfac + EXTRA <= LANES
    fits = fits and share % 8 == 0 and cols % LANES == 0 and cols <= 8 * LANES
    fits = fits and power_of_two(tiles) and tiles > 1 and ring == 4
    return fast_device(*args) if fits else plain_device(*args)


def solution(mesh):
    in_specs = (
        P(None, ("cells", "comp"), None),
        P("comp", None),
        P(None, "comp"),
        P(None, ("cells", "comp"), None),
        P("comp", None),
        P(None, "comp"),
        P(),
        P(None, "cells", None),
        P("cells", None),
        P("cells", None),
    )
    out_specs = (
        P(None, ("cells", "comp"), None),
        P("comp", None),
        P(None, "comp"),
        P(None, ("cells", "comp"), None),
        P("comp", None),
        P(None, "comp"),
        P(),
    )
    return jax.shard_map(
        choose_device, mesh=mesh, in_specs=in_specs, out_specs=out_specs, check_vma=False
    )
```

```python
import functools
import math

import jax
import jax.numpy as jnp
from jax import lax
from jax.experimental import pallas as pl
from jax.experimental.pallas import tpu as pltpu
from jax.sharding import PartitionSpec as P


def extended(cells, sides, width):
    for axis, dim in sides:
        count = lax.axis_size(axis)
        ends = count - 1
        head = lax.slice_in_dim(cells, 0, width, axis=dim)
        tail = lax.slice_in_dim(cells, cells.shape[dim] - width, cells.shape[dim], axis=dim)
        cells = jnp.concatenate(
            [
                lax.ppermute(tail, axis, [(i, (i + 1) % count) for i in range(ends)]),
                cells,
                lax.ppermute(head, axis, [((i + 1) % count, i) for i in range(ends)]),
            ],
            axis=dim,
        )
    return cells


def field_prior(padded, land_pad, field_tau):
    ridge = 0.1
    step_x = padded[:, 1:, :] - padded[:, :-1, :]
    edge_x = land_pad[1:, :] * land_pad[:-1, :]
    flux_x = edge_x[None, :, :] * step_x
    centre = padded[:, 1:-1, :]
    land_mid = land_pad[1:-1, :]
    step_y = centre[:, :, 1:] - centre[:, :, :-1]
    edge_y = land_mid[:, 1:] * land_mid[:, :-1]
    flux_y = edge_y[None, :, :] * step_y
    lap_x = flux_x[:, :-1, :] - flux_x[:, 1:, :]
    lap_y = jnp.pad(flux_y, ((0, 0), (0, 0), (1, 0))) - jnp.pad(flux_y, ((0, 0), (0, 0), (0, 1)))
    tau_cube = field_tau[:, None, None]
    grad = -tau_cube * (lap_x + lap_y + ridge * centre)
    energy = 0.5 * jnp.sum(tau_cube * (flux_x[:, 1:, :] * step_x[:, 1:, :]))
    energy = energy + 0.5 * jnp.sum(tau_cube * (flux_y * step_y))
    energy = energy + 0.5 * ridge * jnp.sum(tau_cube * (centre * centre))
    return (grad, energy)


def tile_scores(flat_tile, count_rows, exposure, profile, mixing):
    prof_exp = jnp.exp(profile)
    rate_total = jnp.sum(prof_exp, axis=1)
    mix_logit = jnp.dot(mixing.T, flat_tile, precision=lax.Precision.HIGHEST)
    fit_score = (
        jnp.dot(profile, count_rows, precision=lax.Precision.HIGHEST)
        - rate_total[:, None] * exposure[None, :]
    )
    return (mix_logit, mix_logit + fit_score)


def tile_grads(
    flat_tile, count_rows, land_weight, exposure, mixing, mix_logit, joint_score, log_mix, log_joint
):
    prior_share = jnp.exp(mix_logit - log_mix[None, :])
    posterior = jnp.exp(joint_score - log_joint[None, :])
    post_land = posterior * land_weight[None, :]
    gap_weight = (posterior - prior_share) * land_weight[None, :]
    grad_counts = jnp.dot(post_land, count_rows.T, precision=lax.Precision.HIGHEST)
    rate_mass = jnp.sum(post_land * exposure[None, :], axis=1)
    grad_mix = jnp.dot(flat_tile, gap_weight.T, precision=lax.Precision.HIGHEST)
    field_lik = jnp.dot(mixing, gap_weight, precision=lax.Precision.HIGHEST)
    log_dens = jnp.sum(land_weight * (log_joint - log_mix))
    return (grad_counts, rate_mass, grad_mix, field_lik, log_dens)


def log_sum(scores):
    top = jnp.max(scores, axis=0)
    return top + jnp.log(jnp.sum(jnp.exp(scores - top[None, :]), axis=0))


def plain_device(
    factor_field,
    profile,
    mixing,
    factor_mom,
    profile_mom,
    mixing_mom,
    field_tau,
    counts,
    land_mask,
    log_exposure,
):
    step_field = 0.05
    step_profile = 0.002
    step_mixing = 0.002
    tile_rows, tile_cols = land_mask.shape
    ncat = counts.shape[0]
    share_rows = factor_field.shape[1]
    comp_rank = lax.axis_index("comp")
    cells_rank = lax.axis_index("cells")
    first_cells = cells_rank == 0
    land_pad = extended(land_mask, (("cells", 0),), 1).astype(jnp.float32)
    row_start = comp_rank * share_rows
    count_rows = lax.dynamic_slice_in_dim(counts, row_start, share_rows, 1)
    count_rows = count_rows.reshape(ncat, share_rows * tile_cols).astype(jnp.float32)
    land_weight = (
        lax.dynamic_slice_in_dim(land_mask, row_start, share_rows, 0)
        .reshape(-1)
        .astype(jnp.float32)
    )
    exposure = jnp.exp(lax.dynamic_slice_in_dim(log_exposure, row_start, share_rows, 0).reshape(-1))
    land_near = lax.dynamic_slice_in_dim(land_pad, row_start, share_rows + 2, 0)

    def evaluate(share_field, profile_now, mixing_now):
        padded = extended(share_field, ((("cells", "comp"), 1),), 1)
        prior_grad, prior_energy = field_prior(padded, land_near, field_tau)
        profile_all, mixing_all = (
            lax.all_gather(profile_now, "comp", axis=0, tiled=True),
            lax.all_gather(mixing_now, "comp", axis=1, tiled=True),
        )
        flat_tile = share_field.reshape(share_field.shape[0], -1)
        mix_logit, joint_score = tile_scores(
            flat_tile, count_rows, exposure, profile_all, mixing_all
        )
        log_mix = log_sum(mix_logit)
        log_joint = log_sum(joint_score)
        grad_counts, rate_mass, grad_mix, field_lik, log_dens = tile_grads(
            flat_tile,
            count_rows,
            land_weight,
            exposure,
            mixing_all,
            mix_logit,
            joint_score,
            log_mix,
            log_joint,
        )
        grad_counts, rate_mass, mix_rows = (
            lax.psum_scatter(grad_counts, "comp", scatter_dimension=0, tiled=True),
            lax.psum_scatter(rate_mass, "comp", scatter_dimension=0, tiled=True),
            lax.psum_scatter(grad_mix.T, "comp", scatter_dimension=0, tiled=True),
        )
        grad_mix = mix_rows.T
        grad_field = prior_grad + field_lik.reshape(share_field.shape)
        log_part = log_dens - prior_energy
        grad_counts, rate_mass, grad_mix = lax.psum((grad_counts, rate_mass, grad_mix), "cells")
        grad_profile = grad_counts - jnp.exp(profile_now) * rate_mass[:, None] - 0.25 * profile_now
        grad_mixing = grad_mix - mixing_now
        param_prior = -0.125 * jnp.sum(profile_now * profile_now) - 0.5 * jnp.sum(
            mixing_now * mixing_now
        )
        log_part = log_part + jnp.where(first_cells, param_prior, 0.0)
        return (log_part, grad_field, grad_profile, grad_mixing)

    first = evaluate(factor_field, profile, mixing)
    half_field = factor_mom + 0.5 * step_field * first[1]
    half_profile = profile_mom + 0.5 * step_profile * first[2]
    half_mixing = mixing_mom + 0.5 * step_mixing * first[3]
    new_field = factor_field + step_field * half_field
    new_profile = profile + step_profile * half_profile
    new_mixing = mixing + step_mixing * half_mixing
    second = evaluate(new_field, new_profile, new_mixing)
    new_factor_mom = half_field + 0.5 * step_field * second[1]
    new_profile_mom = half_profile + 0.5 * step_profile * second[2]
    new_mixing_mom = half_mixing + 0.5 * step_mixing * second[3]
    kinetic = 0.5 * jnp.sum(new_factor_mom * new_factor_mom)
    kinetic = kinetic + jnp.where(
        first_cells,
        0.5
        * (jnp.sum(new_profile_mom * new_profile_mom) + jnp.sum(new_mixing_mom * new_mixing_mom)),
        0.0,
    )
    log_total, kinetic_total = lax.psum((second[0], kinetic), ("cells", "comp"))
    cell_count = tile_rows * tile_cols * lax.axis_size("cells")
    hamiltonian = (kinetic_total - log_total) / cell_count
    return (
        new_field,
        new_profile,
        new_mixing,
        new_factor_mom,
        new_profile_mom,
        new_mixing_mom,
        hamiltonian,
    )


STEP_FIELD = 0.05
STEP_PARAM = 0.002
RIDGE = 0.1
LOG2E = math.log2(math.e)
LN2 = math.log(2.0)
LANES = 128
EXTRA = 16
F32 = jnp.float32
BF16 = jnp.bfloat16


def pieces(values, count):
    parts = []
    for _ in range(count):
        part = values.astype(BF16)
        parts.append(part)
        values = values - part.astype(F32)
    return parts


def dot(left, right, dims=((1,), (0,))):
    return lax.dot_general(left, right, (dims, ((), ())), preferred_element_type=F32)


def partner(values, axis, flip):
    count = lax.axis_size(axis)
    return lax.ppermute(values, axis, [(i, i ^ flip) for i in range(count)])


def all_sum(keep, send, near_edge=None, far_edge=None, beside=()):
    pairs, rows, _ = keep.shape
    chunks = keep + partner(send, "cells", 1)
    total = chunks[0]
    for part in [partner(chunks[k], "cells", 2 * k) for k in range(1, pairs)]:
        total = total + part
    total, beside = lax.optimization_barrier((total, beside))
    if near_edge is None:
        parts = [partner(total, "comp", k) for k in range(1, lax.axis_size("comp"))]
        near_got = None
        for part in parts:
            total = total + part
    else:
        first = partner(jnp.concatenate([total, near_edge], axis=0), "comp", 1)
        second = partner(total, "comp", 2)
        third = partner(jnp.concatenate([total, far_edge], axis=0), "comp", 3)
        near_got = first[rows:]
        total = jnp.concatenate([total + first[:rows] + second + third[:rows], third[rows:]], axis=0)
    near = jnp.stack([total] + [partner(total, "cells", 2 * k) for k in range(1, pairs)])
    return near, partner(near, "cells", 1), near_got, beside


def gather_params(pack, cells_rank):
    tiles, ring = lax.axis_size("cells"), lax.axis_size("comp")
    rows = pack.shape[0]
    spread = [(c * ring + z, c * ring + (z ^ (1 + c % 2))) for c in range(tiles) for z in range(ring)]
    one = lax.ppermute(pack, ("cells", "comp"), spread)
    half = lax.dynamic_slice_in_dim(pack, cells_rank % 2 * (rows // 2), rows // 2, 0)
    got = jnp.concatenate([one, partner(half, "comp", 3)], axis=0)
    return got, partner(got, "cells", 1)


def chunk_index(cells_rank, k, other):
    core = cells_rank % 2
    return (((cells_rank // 2) ^ k) * 2) + (1 - core if other else core)


def gather_chunks(flat_ref, near_ref, far_ref, cells_rank, rows):
    for k in range(near_ref.shape[0]):
        for source, other in ((near_ref, False), (far_ref, True)):
            start = pl.multiple_of(chunk_index(cells_rank, k, other) * rows, 8)
            flat_ref[pl.ds(start, rows), :] = source[k, 0:rows, :]


def spread_chunks(flat_ref, keep_ref, send_ref, cells_rank):
    pairs, rows, _ = keep_ref.shape
    for k in range(pairs):
        for target, other in ((keep_ref, False), (send_ref, True)):
            start = pl.multiple_of(chunk_index(cells_rank, k, other) * rows, 8)
            target[k] = flat_ref[pl.ds(start, rows), :]


def load_params(flat_ref, left_ref, mix_ref, load_ref, ncomp, nfac):
    lane = lax.broadcasted_iota(jnp.int32, (LANES, LANES), 1)
    spare = jnp.zeros((LANES - EXTRA - 6 * nfac, LANES), F32)
    for q in range(ncomp // LANES):
        rows = pl.ds(q * LANES, LANES)
        prof = flat_ref[rows, :]
        high, mid, low = pieces(prof * LOG2E, 3)
        left_ref[rows, 0:LANES] = high
        left_ref[rows, 2 * LANES : 3 * LANES] = mid
        left_ref[rows, 3 * LANES : 4 * LANES] = low
        rate = jnp.sum(jnp.exp(prof), axis=1, keepdims=True) * LOG2E
        rate_high, rate_mid, rate_low = [part.astype(F32) for part in pieces(rate, 3)]
        load = flat_ref[pl.ds(ncomp + q * nfac, nfac), :]
        w_high, w_mid, w_low = [part.astype(F32) for part in pieces(load * LOG2E, 3)]
        stack = jnp.concatenate(
            [jnp.zeros((EXTRA, LANES), F32), w_high, w_high, w_high, w_mid, w_mid, w_low, spare], axis=0
        )
        turned = stack.T
        mix_ref[rows, :] = turned.astype(BF16)
        rate_part = jnp.where(
            lane < 3, rate_high, jnp.where(lane < 5, rate_mid, jnp.where(lane == 5, rate_low, 0.0))
        )
        left_ref[rows, LANES : 2 * LANES] = (turned - rate_part).astype(BF16)
        load_high, load_mid = pieces(load, 2)
        load_ref[0:nfac, q * LANES : (q + 1) * LANES] = load_high
        load_ref[nfac : 2 * nfac, q * LANES : (q + 1) * LANES] = load_mid


def load_cells(counts_ref, field_ref, log_exposure, right_ref, wide_ref):
    share, ncat, cols = counts_ref.shape
    nfac = field_ref.shape[1]
    exposure = jnp.exp(log_exposure)
    sub = lax.broadcasted_iota(jnp.int32, (EXTRA, cols), 0)
    spare = jnp.zeros((LANES - EXTRA - 6 * nfac, cols), BF16)
    for r in range(share):
        count = counts_ref[r]
        high, mid, low = pieces(field_ref[r], 3)
        e_high, e_mid, e_low = [part.astype(F32) for part in pieces(exposure[r : r + 1, :], 3)]
        e_rows = jnp.where((sub == 0) | (sub == 3) | (sub == 5), e_high, 0.0)
        e_rows = jnp.where((sub == 1) | (sub == 4), e_mid, e_rows)
        e_rows = jnp.where(sub == 2, e_low, e_rows).astype(BF16)
        extra = jnp.concatenate([e_rows, high, mid, low, high, mid, high, spare], axis=0)
        right_ref[r, 0:ncat, :] = count
        right_ref[r, LANES : 2 * LANES, :] = extra
        right_ref[r, 2 * LANES : 2 * LANES + ncat, :] = count
        right_ref[r, 3 * LANES : 3 * LANES + ncat, :] = count
        for side in range(2):
            wide_ref[r, 0:ncat, side * cols : (side + 1) * cols] = count
            wide_ref[r, LANES : 2 * LANES, side * cols : (side + 1) * cols] = extra


def field_weights(tau_ref, nfac, cols):
    row = lax.broadcasted_iota(jnp.int32, (nfac, cols), 0)
    tau = jnp.zeros((nfac, cols), F32)
    for j in range(nfac):
        tau = jnp.where(row == j, tau_ref[j], tau)
    return tau


def load_prior(rows, lands, tau, prior_ref):
    nfac, cols = tau.shape
    inner = lax.broadcasted_iota(jnp.int32, (nfac, cols), 1) < cols - 1
    energy = jnp.zeros((nfac, cols), F32)
    lands = [jnp.broadcast_to(x, (nfac, cols)) for x in lands]
    for r in range(len(rows) - 2):
        here = rows[r + 1]
        step_right = here - pltpu.roll(here, cols - 1, 1)
        edge_right = jnp.where(inner, lands[r + 1] * pltpu.roll(lands[r + 1], cols - 1, 1), 0.0)
        flux_right = edge_right * step_right
        laplace = flux_right - pltpu.roll(flux_right, 1, 1)
        parts = flux_right * step_right + RIDGE * (here * here)
        if rows[r] is not None:
            laplace = laplace + lands[r] * lands[r + 1] * (here - rows[r])
        if rows[r + 2] is not None:
            step_down = here - rows[r + 2]
            flux_down = lands[r + 1] * lands[r + 2] * step_down
            laplace = laplace + flux_down
            parts = parts + flux_down * step_down
        prior_ref[r] = -tau * (laplace + RIDGE * here)
        energy = energy + 0.5 * tau * parts
    return energy


def pack_edge(edge_ref, field, fresh, land):
    nfac, cols = field.shape
    blocks = cols // LANES
    sub = lax.broadcasted_iota(jnp.int32, (8, LANES), 0)
    lands = jnp.zeros((8, LANES), F32)
    for b in range(blocks):
        lanes = slice(b * LANES, (b + 1) * LANES)
        edge_ref[b * nfac : (b + 1) * nfac, :] = field[:, lanes]
        edge_ref[(blocks + b) * nfac : (blocks + b + 1) * nfac, :] = fresh[:, lanes]
        lands = jnp.where(sub == b, land[:, lanes], lands)
    edge_ref[2 * blocks * nfac :, :] = lands


def unpack_edge(edge, nfac, cols):
    blocks = cols // LANES
    wide = lambda start, size, step: jnp.concatenate(
        [edge[start + b * step : start + b * step + size, :] for b in range(blocks)], axis=1
    )
    return wide(0, nfac, nfac), wide(blocks * nfac, nfac, nfac), wide(2 * blocks * nfac, 1, 1)


def row_scores(r, right_ref, left_ref, mix_ref, score_ref, logit_ref):
    tops = []
    for target, values in (
        (score_ref, dot(left_ref[...], right_ref[r])),
        (logit_ref, dot(mix_ref[...], right_ref[r, LANES : 2 * LANES, :])),
    ):
        target[...] = values
        ncomp, cols = values.shape
        tops.append(jnp.max(jnp.max(values.reshape(ncomp // 8, 8, cols), axis=0), axis=0, keepdims=True))
    return tops


def row_shares(tops, land, score_ref, logit_ref, post_ref, gap_ref):
    ncomp, cols = score_ref.shape
    block = 32
    top_s, top_a = tops
    sum_s = jnp.zeros((8, cols), F32)
    sum_a = jnp.zeros((8, cols), F32)
    for i in range(0, ncomp, block):
        part_s = jnp.exp2(score_ref[i : i + block, :] - top_s)
        part_a = jnp.exp2(logit_ref[i : i + block, :] - top_a)
        score_ref[i : i + block, :] = part_s
        logit_ref[i : i + block, :] = part_a
        sum_s = sum_s + jnp.sum(part_s.reshape(block // 8, 8, cols), axis=0)
        sum_a = sum_a + jnp.sum(part_a.reshape(block // 8, 8, cols), axis=0)
    sum_s = jnp.sum(sum_s, axis=0, keepdims=True)
    sum_a = jnp.sum(sum_a, axis=0, keepdims=True)
    log_s = top_s + jnp.log2(sum_s)
    log_a = top_a + jnp.log2(sum_a)
    inv_s = land / sum_s
    inv_a = land / sum_a
    for i in range(0, ncomp, block):
        post = score_ref[i : i + block, :] * inv_s
        gap = post - logit_ref[i : i + block, :] * inv_a
        for target, values in ((post_ref, post), (gap_ref, gap)):
            high, low = pieces(values, 2)
            target[i : i + block, 0:cols] = high
            target[i : i + block, cols : 2 * cols] = low
    return land * (LN2 * (log_s - log_a))


def row_products(r, wide_ref, load_ref, post_ref, gap_ref, acc_ref, accw_ref, prior_ref):
    nfac = load_ref.shape[0] // 2
    cols = prior_ref.shape[2]
    last = ((1,), (1,))
    start = LANES + EXTRA
    acc = dot(post_ref[...], wide_ref[r], last)
    accw = dot(wide_ref[r, start : start + 3 * nfac, :], gap_ref[...], last)
    if r == 0:
        acc_ref[...] = acc
        accw_ref[...] = accw
    else:
        acc_ref[...] += acc
        accw_ref[...] += accw
    lik = dot(load_ref[...], gap_ref[...])
    lik = lik[0:nfac] + lik[nfac : 2 * nfac]
    prior_ref[r] += lik[:, 0:cols] + lik[:, cols : 2 * cols]


def all_rows(land, right, wide, left, mix, load, scores, logits, posts, gaps, acc, accw, prior):
    share, _, cols = prior.shape
    log_dens = jnp.zeros((1, cols), F32)
    tops = {}
    for r in range(share + 2):
        if r < share:
            tops[r] = row_scores(r, right, left, mix, scores[r % 2], logits[r % 2])
        if 0 <= r - 1 < share:
            p = r - 1
            log_dens = log_dens + row_shares(
                tops[p], land[p : p + 1, :], scores[p % 2], logits[p % 2], posts[p % 2], gaps[p % 2]
            )
        if 0 <= r - 2:
            p = r - 2
            row_products(p, wide, load, posts[p % 2], gaps[p % 2], acc, accw, prior)
    return log_dens


def param_grads(flat_ref, acc_ref, accw_ref, grad_ref, ncomp, nfac):
    lane = lax.broadcasted_iota(jnp.int32, (LANES, LANES), 1)
    for q in range(ncomp // LANES):
        rows = pl.ds(q * LANES, LANES)
        lanes = slice(q * LANES, (q + 1) * LANES)
        mass = jnp.sum(jnp.where(lane < 3, acc_ref[rows, LANES : 2 * LANES], 0.0), axis=1, keepdims=True)
        grad_ref[rows, :] = acc_ref[rows, 0:LANES] - jnp.exp(flat_ref[rows, :]) * mass
        load = accw_ref[:, lanes]
        grad_ref[pl.ds(ncomp + q * nfac, nfac), :] = load[0:nfac] + load[nfac : 2 * nfac] + load[2 * nfac : 3 * nfac]


def first_kernel(
    ncomp, rank_ref, tau_ref, counts_ref, field_ref, mom_ref, land_ref, logexp_ref, pmom_ref, wmom_ref, *refs
):
    (pack_ref, got_ref, others_ref, new_ref, half_ref, near_ref, far_ref, grad_ref, keep_ref, send_ref) = refs[:10]
    (flat, left, mix, load, right, wide, prior, score0, score1, logit0, logit1, post0, post1, gap0, gap1, acc, accw) = (
        refs[10:27]
    )
    (stage,) = refs[27:]
    cells_rank, comp_rank = rank_ref[0], rank_ref[1]
    share, nfac, cols = field_ref.shape
    mine = pmom_ref.shape[0]
    core = cells_rank % 2
    size = mine + nfac
    for source, side in ((got_ref, core), (others_ref, 1 - core)):
        stage[pl.ds(pl.multiple_of(side * (size // 2), 8), size // 2), :] = source[size:, :]
    for source, group in (
        (pack_ref, comp_rank),
        (got_ref, comp_rank ^ (1 + core)),
        (others_ref, comp_rank ^ (2 - core)),
        (stage, comp_rank ^ 3),
    ):
        flat[pl.ds(pl.multiple_of(group * mine, mine), mine), :] = source[0:mine, :]
        flat[pl.ds(pl.multiple_of(ncomp + group * nfac, nfac), nfac), :] = source[mine:size, :]
    here = pl.ds(pl.multiple_of(comp_rank * share, 8), share)
    land = land_ref[here, :].astype(F32)
    load_params(flat, left, mix, load, ncomp, nfac)
    load_cells(counts_ref, field_ref, logexp_ref[here, :], right, wide)
    lands = [land[r : r + 1, :] for r in range(share)]
    tau = field_weights(tau_ref, nfac, cols)
    load_prior([None] + [field_ref[r] for r in range(share)] + [None], lands[:1] + lands + lands[-1:], tau, prior)
    all_rows(
        land, right, wide, left, mix, load, (score0, score1), (logit0, logit1), (post0, post1), (gap0, gap1), acc, accw,
        prior,
    )
    for r in range(share):
        half = mom_ref[r] + 0.5 * STEP_FIELD * prior[r]
        half_ref[r] = half
        new_ref[r] = field_ref[r] + STEP_FIELD * half
    even = comp_rank % 2 == 0
    end = share - 1
    for target, flag in ((near_ref, even), (far_ref, jnp.logical_not(even))):
        pack_edge(
            target,
            jnp.where(flag, field_ref[end], field_ref[0]),
            jnp.where(flag, new_ref[end], new_ref[0]),
            jnp.where(flag, lands[end], lands[0]),
        )
    param_grads(flat, acc, accw, grad_ref, ncomp, nfac)
    nparam = grad_ref.shape[0]
    if flat.shape[0] > nparam:
        flat[nparam:, :] = jnp.zeros((flat.shape[0] - nparam, LANES), F32)
    flat[0:nparam, :] = 0.5 * STEP_PARAM * STEP_PARAM * grad_ref[...]
    own_prof, own_load = pack_ref[0:mine, :], pack_ref[mine:size, :]
    owner = cells_rank == 0
    base_prof = own_prof + STEP_PARAM * (pmom_ref[...] - 0.5 * STEP_PARAM * 0.25 * own_prof)
    base_load = own_load + STEP_PARAM * (wmom_ref[...] - 0.5 * STEP_PARAM * own_load)
    flat[pl.ds(pl.multiple_of(comp_rank * mine, mine), mine), :] += jnp.where(owner, base_prof, 0.0)
    flat[pl.ds(pl.multiple_of(ncomp + comp_rank * nfac, nfac), nfac), :] += jnp.where(owner, base_load, 0.0)
    spread_chunks(flat, keep_ref, send_ref, cells_rank)


def second_kernel(
    ncomp, chunk, ring, tiles, rank_ref, tau_ref, counts_ref, field_ref, half_ref, land_ref, logexp_ref, pmom_ref, wmom_ref,
    old_ref, own_ref, near_ref, far_ref, edge_ref, grad0_ref, new_ref, mom_ref, params_ref,
    keep_ref, send_ref,
    flat, left, mix, load, right, wide, prior, score0, score1, logit0, logit1, post0, post1, gap0, gap1, acc, accw, out,
    grad,
):
    cells_rank, comp_rank = rank_ref[0], rank_ref[1]
    share, nfac, cols = field_ref.shape
    mine = pmom_ref.shape[0]
    nparam = grad0_ref.shape[0]
    gather_chunks(flat, near_ref, far_ref, cells_rank, chunk)
    new_prof = flat[pl.ds(pl.multiple_of(comp_rank * mine, mine), mine), :]
    new_load = flat[pl.ds(pl.multiple_of(ncomp + comp_rank * nfac, nfac), nfac), :]
    params_ref[0:mine, :] = new_prof
    params_ref[mine:, :] = new_load
    here = pl.ds(pl.multiple_of(comp_rank * share, 8), share)
    land = land_ref[here, :].astype(F32)
    lands = [land[r : r + 1, :] for r in range(share)]
    tau = field_weights(tau_ref, nfac, cols)

    source = jnp.where(comp_rank == 0, cells_rank - 1, jnp.where(comp_rank == ring - 1, cells_rank + 1, cells_rank))
    source = jnp.clip(source, 0, tiles - 1)
    slot = (source // 2) ^ (cells_rank // 2)
    relay = jnp.where(source % 2 == cells_rank % 2, near_ref[slot, chunk:, :], far_ref[slot, chunk:, :])
    even = comp_rank % 2 == 0
    direct = edge_ref[...]
    above = unpack_edge(jnp.where(even, relay, direct), nfac, cols)
    below = unpack_edge(jnp.where(even, direct, relay), nfac, cols)
    land_above = jnp.where((comp_rank == 0) & (cells_rank == 0), 0.0, above[2])
    land_below = jnp.where((comp_rank == ring - 1) & (cells_rank == tiles - 1), 0.0, below[2])
    end = share - 1
    pull_up = -tau * (land_above * lands[0]) * (old_ref[0] - above[0])
    pull_down = -tau * (land_below * lands[end]) * (old_ref[end] - below[0])
    move = 0.5 * STEP_FIELD * STEP_FIELD
    for r in range(share):
        fresh = field_ref[r]
        if r == 0:
            fresh = fresh + move * pull_up
        if r == end:
            fresh = fresh + move * pull_down
        new_ref[r] = fresh
    load_params(flat, left, mix, load, ncomp, nfac)
    load_cells(counts_ref, new_ref, logexp_ref[here, :], right, wide)
    rows = [above[1] - move * pull_up] + [new_ref[r] for r in range(share)] + [below[1] - move * pull_down]
    energy = load_prior(rows, [land_above] + lands + [land_below], tau, prior)
    prior[0] += pull_up
    prior[end] += pull_down

    log_dens = all_rows(
        land, right, wide, left, mix, load, (score0, score1), (logit0, logit1), (post0, post1), (gap0, gap1), acc, accw,
        prior,
    )
    for r in range(share):
        fresh = half_ref[r] + 0.5 * STEP_FIELD * prior[r]
        mom_ref[r] = fresh
        energy = energy + 0.5 * (fresh * fresh)
    param_grads(flat, acc, accw, grad, ncomp, nfac)
    first_device = (cells_rank == 0) & (comp_rank == 0)
    prof_all = flat[0:ncomp, :]
    load_all = flat[ncomp:nparam, :]
    param_energy = jnp.sum(0.125 * (prof_all * prof_all)) + jnp.sum(0.5 * (load_all * load_all))
    total = jnp.sum(energy) - jnp.sum(log_dens) + jnp.where(first_device, param_energy, 0.0)
    out[0:nparam, :] = 0.5 * STEP_PARAM * (grad0_ref[...] + grad[...])
    tail = out.shape[0] - nparam
    spot = lax.broadcasted_iota(jnp.int32, (tail, LANES), 0) + lax.broadcasted_iota(jnp.int32, (tail, LANES), 1)
    out[nparam:, :] = jnp.where(spot == 0, total, 0.0)
    owner = cells_rank == 0
    old_prof, old_load = own_ref[0:mine, :], own_ref[mine : mine + nfac, :]
    base_prof = pmom_ref[...] - 0.5 * STEP_PARAM * 0.25 * (old_prof + new_prof)
    base_load = wmom_ref[...] - 0.5 * STEP_PARAM * (old_load + new_load)
    out[pl.ds(pl.multiple_of(comp_rank * mine, mine), mine), :] += jnp.where(owner, base_prof, 0.0)
    out[pl.ds(pl.multiple_of(ncomp + comp_rank * nfac, nfac), nfac), :] += jnp.where(owner, base_load, 0.0)
    spread_chunks(out, keep_ref, send_ref, cells_rank)


def last_kernel(ncomp, nparam, chunk, cells, rank_ref, near_ref, far_ref, prof_ref, mixing_ref, ham_ref, flat):
    cells_rank, comp_rank = rank_ref[0], rank_ref[1]
    mine, nfac = prof_ref.shape[0], mixing_ref.shape[0]
    gather_chunks(flat, near_ref, far_ref, cells_rank, chunk)
    prof_ref[...] = flat[pl.ds(pl.multiple_of(comp_rank * mine, mine), mine), :]
    mixing_ref[...] = flat[pl.ds(pl.multiple_of(ncomp + comp_rank * nfac, nfac), nfac), :]
    momenta = flat[0:nparam, :]
    rest = flat[nparam:, :]
    total = jnp.sum(0.5 * (momenta * momenta).reshape(nparam // 8, 8, LANES), axis=0)
    total = total + jnp.sum(rest.reshape(rest.shape[0] // 8, 8, LANES), axis=0)
    total = jnp.sum(jnp.sum(total, axis=0, keepdims=True), axis=1, keepdims=True)
    ham_ref[...] = total / cells


def fast_device(
    factor_field, profile, mixing, factor_mom, profile_mom, mixing_mom, field_tau, counts, land_mask, log_exposure
):
    nfac, share, cols = factor_field.shape
    mine, ncat = profile.shape
    tile_rows = land_mask.shape[0]
    ring = lax.axis_size("comp")
    tiles = lax.axis_size("cells")
    ncomp = mine * ring
    nparam = ncomp + nfac * ncomp // LANES
    pairs = tiles // 2
    edge = 2 * nfac * cols // LANES + 8
    round_up = lambda rows: -(-rows // (8 * tiles)) * 8
    chunk_one = round_up(nparam)
    chunk_two = round_up(nparam + 1)
    comp_rank = lax.axis_index("comp")
    cells_rank = lax.axis_index("cells")
    ranks = jnp.stack([cells_rank, comp_rank]).astype(jnp.int32)
    pack = lax.optimization_barrier(jnp.pad(profile, ((0, nfac), (0, 0))) + jnp.pad(mixing, ((mine, 0), (0, 0))))
    got, others = gather_params(pack, cells_rank)
    count_rows = lax.dynamic_slice_in_dim(counts, comp_rank * share, share, 1).swapaxes(0, 1).astype(BF16)
    field_rows = factor_field.swapaxes(0, 1)
    mom_rows = factor_mom.swapaxes(0, 1)
    vmem = pl.BlockSpec(memory_space=pltpu.VMEM)
    smem = pl.BlockSpec(memory_space=pltpu.SMEM)
    shape = lambda *dims: jax.ShapeDtypeStruct(dims, F32)
    work = [
        pltpu.VMEM((ncomp, 4 * LANES), BF16),
        pltpu.VMEM((ncomp, LANES), BF16),
        pltpu.VMEM((2 * nfac, ncomp), BF16),
        pltpu.VMEM((share, 4 * LANES, cols), BF16),
        pltpu.VMEM((share, 2 * LANES, 2 * cols), BF16),
        pltpu.VMEM((share, nfac, cols), F32),
    ]
    work += [pltpu.VMEM((ncomp, cols), F32)] * 4 + [pltpu.VMEM((ncomp, 2 * cols), BF16)] * 4
    work += [
        pltpu.VMEM((ncomp, 2 * LANES), F32),
        pltpu.VMEM((3 * nfac, ncomp), F32),
    ]
    def call(body, name, smem_count, vmem_count, outs, scratch):
        return pl.pallas_call(
            body,
            name=name,
            in_specs=[smem] * smem_count + [vmem] * vmem_count,
            out_specs=[vmem] * len(outs),
            scratch_shapes=scratch,
            out_shape=outs,
            compiler_params=pltpu.CompilerParams(vmem_limit_bytes=40 * 1024 * 1024),
        )

    first = call(
        functools.partial(first_kernel, ncomp),
        "first_gradient",
        2,
        7 + 3,
        [
            shape(share, nfac, cols),
            shape(share, nfac, cols),
            shape(edge, LANES),
            shape(edge, LANES),
            shape(nparam, LANES),
            shape(pairs, chunk_one, LANES),
            shape(pairs, chunk_one, LANES),
        ],
        [pltpu.VMEM((tiles * chunk_one, LANES), F32)] + work + [pltpu.VMEM((mine + nfac, LANES), F32)],
    )
    part_field, half, near_edge, far_edge, grad, keep, send = first(
        ranks, field_tau, count_rows, field_rows, mom_rows, land_mask, log_exposure, profile_mom, mixing_mom, pack, got, others
    )
    near, far, got_edge, _ = all_sum(keep, send, near_edge, far_edge)
    second = call(
        functools.partial(second_kernel, ncomp, chunk_one, ring, tiles),
        "second_gradient",
        2,
        7 + 6,
        [
            shape(share, nfac, cols),
            shape(share, nfac, cols),
            shape(mine + nfac, ncat),
            shape(pairs, chunk_two, LANES),
            shape(pairs, chunk_two, LANES),
        ],
        [pltpu.VMEM((tiles * chunk_one, LANES), F32)]
        + work
        + [pltpu.VMEM((tiles * chunk_two, LANES), F32), pltpu.VMEM((nparam, LANES), F32)],
    )
    new_field, new_mom, new_params, keep, send = second(
        ranks, field_tau, count_rows, part_field, half, land_mask, log_exposure, profile_mom, mixing_mom, field_rows, pack,
        near, far, got_edge, grad,
    )
    done = (new_field.swapaxes(0, 1), new_params[:mine], new_params[mine:], new_mom.swapaxes(0, 1))
    near, far, _, done = all_sum(keep, send, beside=done)
    final = call(
        functools.partial(last_kernel, ncomp, nparam, chunk_two, tile_rows * cols * tiles),
        "momenta",
        1,
        2,
        [shape(mine, ncat), shape(nfac, mine), shape(1, 1)],
        [pltpu.VMEM((tiles * chunk_two, LANES), F32)],
    )
    new_profile_mom, new_mixing_mom, hamiltonian = final(ranks, near, far)
    return (
        *done,
        new_profile_mom,
        new_mixing_mom,
        hamiltonian.reshape(()),
    )


def power_of_two(count):
    return count & (count - 1) == 0


def choose_device(*args):
    factor_field, profile, mixing = args[:3]
    nfac, share, cols = factor_field.shape
    mine, ncat = profile.shape
    tiles, ring = lax.axis_size("cells"), lax.axis_size("comp")
    fits = mine == LANES and ncat == LANES and nfac % 16 == 0 and 6 * nfac + EXTRA <= LANES
    fits = fits and share % 8 == 0 and cols % LANES == 0 and cols <= 8 * LANES
    fits = fits and power_of_two(tiles) and tiles > 1 and ring == 4
    return fast_device(*args) if fits else plain_device(*args)


def solution(mesh):
    in_specs = (
        P(None, ("cells", "comp"), None),
        P("comp", None),
        P(None, "comp"),
        P(None, ("cells", "comp"), None),
        P("comp", None),
        P(None, "comp"),
        P(),
        P(None, "cells", None),
        P("cells", None),
        P("cells", None),
    )
    out_specs = (
        P(None, ("cells", "comp"), None),
        P("comp", None),
        P(None, "comp"),
        P(None, ("cells", "comp"), None),
        P("comp", None),
        P(None, "comp"),
        P(),
    )
    return jax.shard_map(
        choose_device, mesh=mesh, in_specs=in_specs, out_specs=out_specs, check_vma=False
    )
```

```python
import functools
import math

import jax
import jax.numpy as jnp
from jax import lax
from jax.experimental import pallas as pl
from jax.experimental.pallas import tpu as pltpu
from jax.sharding import PartitionSpec as P


def extended(cells, sides, width):
    for axis, dim in sides:
        count = lax.axis_size(axis)
        ends = count - 1
        head = lax.slice_in_dim(cells, 0, width, axis=dim)
        tail = lax.slice_in_dim(cells, cells.shape[dim] - width, cells.shape[dim], axis=dim)
        cells = jnp.concatenate(
            [
                lax.ppermute(tail, axis, [(i, (i + 1) % count) for i in range(ends)]),
                cells,
                lax.ppermute(head, axis, [((i + 1) % count, i) for i in range(ends)]),
            ],
            axis=dim,
        )
    return cells


def field_prior(padded, land_pad, field_tau):
    ridge = 0.1
    step_x = padded[:, 1:, :] - padded[:, :-1, :]
    edge_x = land_pad[1:, :] * land_pad[:-1, :]
    flux_x = edge_x[None, :, :] * step_x
    centre = padded[:, 1:-1, :]
    land_mid = land_pad[1:-1, :]
    step_y = centre[:, :, 1:] - centre[:, :, :-1]
    edge_y = land_mid[:, 1:] * land_mid[:, :-1]
    flux_y = edge_y[None, :, :] * step_y
    lap_x = flux_x[:, :-1, :] - flux_x[:, 1:, :]
    lap_y = jnp.pad(flux_y, ((0, 0), (0, 0), (1, 0))) - jnp.pad(flux_y, ((0, 0), (0, 0), (0, 1)))
    tau_cube = field_tau[:, None, None]
    grad = -tau_cube * (lap_x + lap_y + ridge * centre)
    energy = 0.5 * jnp.sum(tau_cube * (flux_x[:, 1:, :] * step_x[:, 1:, :]))
    energy = energy + 0.5 * jnp.sum(tau_cube * (flux_y * step_y))
    energy = energy + 0.5 * ridge * jnp.sum(tau_cube * (centre * centre))
    return (grad, energy)


def tile_scores(flat_tile, count_rows, exposure, profile, mixing):
    prof_exp = jnp.exp(profile)
    rate_total = jnp.sum(prof_exp, axis=1)
    mix_logit = jnp.dot(mixing.T, flat_tile, precision=lax.Precision.HIGHEST)
    fit_score = (
        jnp.dot(profile, count_rows, precision=lax.Precision.HIGHEST)
        - rate_total[:, None] * exposure[None, :]
    )
    return (mix_logit, mix_logit + fit_score)


def tile_grads(
    flat_tile, count_rows, land_weight, exposure, mixing, mix_logit, joint_score, log_mix, log_joint
):
    prior_share = jnp.exp(mix_logit - log_mix[None, :])
    posterior = jnp.exp(joint_score - log_joint[None, :])
    post_land = posterior * land_weight[None, :]
    gap_weight = (posterior - prior_share) * land_weight[None, :]
    grad_counts = jnp.dot(post_land, count_rows.T, precision=lax.Precision.HIGHEST)
    rate_mass = jnp.sum(post_land * exposure[None, :], axis=1)
    grad_mix = jnp.dot(flat_tile, gap_weight.T, precision=lax.Precision.HIGHEST)
    field_lik = jnp.dot(mixing, gap_weight, precision=lax.Precision.HIGHEST)
    log_dens = jnp.sum(land_weight * (log_joint - log_mix))
    return (grad_counts, rate_mass, grad_mix, field_lik, log_dens)


def log_sum(scores):
    top = jnp.max(scores, axis=0)
    return top + jnp.log(jnp.sum(jnp.exp(scores - top[None, :]), axis=0))


def plain_device(
    factor_field,
    profile,
    mixing,
    factor_mom,
    profile_mom,
    mixing_mom,
    field_tau,
    counts,
    land_mask,
    log_exposure,
):
    step_field = 0.05
    step_profile = 0.002
    step_mixing = 0.002
    tile_rows, tile_cols = land_mask.shape
    ncat = counts.shape[0]
    share_rows = factor_field.shape[1]
    comp_rank = lax.axis_index("comp")
    cells_rank = lax.axis_index("cells")
    first_cells = cells_rank == 0
    land_pad = extended(land_mask, (("cells", 0),), 1).astype(jnp.float32)
    row_start = comp_rank * share_rows
    count_rows = lax.dynamic_slice_in_dim(counts, row_start, share_rows, 1)
    count_rows = count_rows.reshape(ncat, share_rows * tile_cols).astype(jnp.float32)
    land_weight = (
        lax.dynamic_slice_in_dim(land_mask, row_start, share_rows, 0)
        .reshape(-1)
        .astype(jnp.float32)
    )
    exposure = jnp.exp(lax.dynamic_slice_in_dim(log_exposure, row_start, share_rows, 0).reshape(-1))
    land_near = lax.dynamic_slice_in_dim(land_pad, row_start, share_rows + 2, 0)

    def evaluate(share_field, profile_now, mixing_now):
        padded = extended(share_field, ((("cells", "comp"), 1),), 1)
        prior_grad, prior_energy = field_prior(padded, land_near, field_tau)
        profile_all, mixing_all = (
            lax.all_gather(profile_now, "comp", axis=0, tiled=True),
            lax.all_gather(mixing_now, "comp", axis=1, tiled=True),
        )
        flat_tile = share_field.reshape(share_field.shape[0], -1)
        mix_logit, joint_score = tile_scores(
            flat_tile, count_rows, exposure, profile_all, mixing_all
        )
        log_mix = log_sum(mix_logit)
        log_joint = log_sum(joint_score)
        grad_counts, rate_mass, grad_mix, field_lik, log_dens = tile_grads(
            flat_tile,
            count_rows,
            land_weight,
            exposure,
            mixing_all,
            mix_logit,
            joint_score,
            log_mix,
            log_joint,
        )
        grad_counts, rate_mass, mix_rows = (
            lax.psum_scatter(grad_counts, "comp", scatter_dimension=0, tiled=True),
            lax.psum_scatter(rate_mass, "comp", scatter_dimension=0, tiled=True),
            lax.psum_scatter(grad_mix.T, "comp", scatter_dimension=0, tiled=True),
        )
        grad_mix = mix_rows.T
        grad_field = prior_grad + field_lik.reshape(share_field.shape)
        log_part = log_dens - prior_energy
        grad_counts, rate_mass, grad_mix = lax.psum((grad_counts, rate_mass, grad_mix), "cells")
        grad_profile = grad_counts - jnp.exp(profile_now) * rate_mass[:, None] - 0.25 * profile_now
        grad_mixing = grad_mix - mixing_now
        param_prior = -0.125 * jnp.sum(profile_now * profile_now) - 0.5 * jnp.sum(
            mixing_now * mixing_now
        )
        log_part = log_part + jnp.where(first_cells, param_prior, 0.0)
        return (log_part, grad_field, grad_profile, grad_mixing)

    first = evaluate(factor_field, profile, mixing)
    half_field = factor_mom + 0.5 * step_field * first[1]
    half_profile = profile_mom + 0.5 * step_profile * first[2]
    half_mixing = mixing_mom + 0.5 * step_mixing * first[3]
    new_field = factor_field + step_field * half_field
    new_profile = profile + step_profile * half_profile
    new_mixing = mixing + step_mixing * half_mixing
    second = evaluate(new_field, new_profile, new_mixing)
    new_factor_mom = half_field + 0.5 * step_field * second[1]
    new_profile_mom = half_profile + 0.5 * step_profile * second[2]
    new_mixing_mom = half_mixing + 0.5 * step_mixing * second[3]
    kinetic = 0.5 * jnp.sum(new_factor_mom * new_factor_mom)
    kinetic = kinetic + jnp.where(
        first_cells,
        0.5
        * (jnp.sum(new_profile_mom * new_profile_mom) + jnp.sum(new_mixing_mom * new_mixing_mom)),
        0.0,
    )
    log_total, kinetic_total = lax.psum((second[0], kinetic), ("cells", "comp"))
    cell_count = tile_rows * tile_cols * lax.axis_size("cells")
    hamiltonian = (kinetic_total - log_total) / cell_count
    return (
        new_field,
        new_profile,
        new_mixing,
        new_factor_mom,
        new_profile_mom,
        new_mixing_mom,
        hamiltonian,
    )


STEP_FIELD = 0.05
STEP_PARAM = 0.002
RIDGE = 0.1
LOG2E = math.log2(math.e)
LN2 = math.log(2.0)
LANES = 128
EXTRA = 16
F32 = jnp.float32
BF16 = jnp.bfloat16


def pieces(values, count):
    parts = []
    for _ in range(count):
        part = values.astype(BF16)
        parts.append(part)
        values = values - part.astype(F32)
    return parts


def dot(left, right, dims=((1,), (0,))):
    return lax.dot_general(left, right, (dims, ((), ())), preferred_element_type=F32)


def partner(values, axis, flip):
    count = lax.axis_size(axis)
    return lax.ppermute(values, axis, [(i, i ^ flip) for i in range(count)])


def all_sum(keep, send, near_edge=None, far_edge=None, late=None, beside=()):
    pairs, rows, _ = keep.shape
    chunks = keep + partner(send, "cells", 1)
    total = chunks[0]
    for part in [partner(chunks[k], "cells", 2 * k) for k in range(1, pairs)]:
        total = total + part
    total, beside = lax.optimization_barrier((total, beside))
    if late is not None:
        total = jnp.concatenate([total, late], axis=0)
    if near_edge is None:
        parts = [partner(total, "comp", k) for k in range(1, lax.axis_size("comp"))]
        near_got = None
        for part in parts:
            total = total + part
    else:
        first = partner(jnp.concatenate([total, near_edge], axis=0), "comp", 1)
        second = partner(total, "comp", 2)
        third = partner(jnp.concatenate([total, far_edge], axis=0), "comp", 3)
        near_got = first[rows:]
        total = jnp.concatenate([total + first[:rows] + second + third[:rows], third[rows:]], axis=0)
    near = jnp.stack([total] + [partner(total, "cells", 2 * k) for k in range(1, pairs)])
    return near, partner(near, "cells", 1), near_got, beside


def gather_params(pack, cells_rank):
    tiles, ring = lax.axis_size("cells"), lax.axis_size("comp")
    rows = pack.shape[0]
    spread = [(c * ring + z, c * ring + (z ^ (1 + c % 2))) for c in range(tiles) for z in range(ring)]
    one = lax.ppermute(pack, ("cells", "comp"), spread)
    half = lax.dynamic_slice_in_dim(pack, cells_rank % 2 * (rows // 2), rows // 2, 0)
    got = jnp.concatenate([one, partner(half, "comp", 3)], axis=0)
    return got, partner(got, "cells", 1)


def chunk_index(cells_rank, k, other):
    core = cells_rank % 2
    return (((cells_rank // 2) ^ k) * 2) + (1 - core if other else core)


def gather_chunks(flat_ref, near_ref, far_ref, cells_rank, rows):
    for k in range(near_ref.shape[0]):
        for source, other in ((near_ref, False), (far_ref, True)):
            start = pl.multiple_of(chunk_index(cells_rank, k, other) * rows, 8)
            flat_ref[pl.ds(start, rows), :] = source[k, 0:rows, :]


def spread_chunks(flat_ref, keep_ref, send_ref, cells_rank):
    pairs, rows, _ = keep_ref.shape
    for k in range(pairs):
        for target, other in ((keep_ref, False), (send_ref, True)):
            start = pl.multiple_of(chunk_index(cells_rank, k, other) * rows, 8)
            target[k] = flat_ref[pl.ds(start, rows), :]


def load_params(flat_ref, left_ref, mix_ref, load_ref, ncomp, nfac):
    lane = lax.broadcasted_iota(jnp.int32, (LANES, LANES), 1)
    spare = jnp.zeros((LANES - EXTRA - 6 * nfac, LANES), F32)
    for q in range(ncomp // LANES):
        rows = pl.ds(q * LANES, LANES)
        prof = flat_ref[rows, :]
        high, mid, low = pieces(prof * LOG2E, 3)
        left_ref[rows, 0:LANES] = high
        left_ref[rows, 2 * LANES : 3 * LANES] = mid
        left_ref[rows, 3 * LANES : 4 * LANES] = low
        rate = jnp.sum(jnp.exp(prof), axis=1, keepdims=True) * LOG2E
        rate_high, rate_mid, rate_low = [part.astype(F32) for part in pieces(rate, 3)]
        load = flat_ref[pl.ds(ncomp + q * nfac, nfac), :]
        w_high, w_mid, w_low = [part.astype(F32) for part in pieces(load * LOG2E, 3)]
        stack = jnp.concatenate(
            [jnp.zeros((EXTRA, LANES), F32), w_high, w_high, w_high, w_mid, w_mid, w_low, spare], axis=0
        )
        turned = stack.T
        mix_ref[rows, :] = turned.astype(BF16)
        rate_part = jnp.where(
            lane < 3, rate_high, jnp.where(lane < 5, rate_mid, jnp.where(lane == 5, rate_low, 0.0))
        )
        left_ref[rows, LANES : 2 * LANES] = (turned - rate_part).astype(BF16)
        load_high, load_mid = pieces(load, 2)
        load_ref[0:nfac, q * LANES : (q + 1) * LANES] = load_high
        load_ref[nfac : 2 * nfac, q * LANES : (q + 1) * LANES] = load_mid


def load_cells(counts_ref, field_ref, log_exposure, right_ref, wide_ref):
    share, ncat, cols = counts_ref.shape
    nfac = field_ref.shape[1]
    exposure = jnp.exp(log_exposure)
    sub = lax.broadcasted_iota(jnp.int32, (EXTRA, cols), 0)
    spare = jnp.zeros((LANES - EXTRA - 6 * nfac, cols), BF16)
    for r in range(share):
        count = counts_ref[r]
        high, mid, low = pieces(field_ref[r], 3)
        e_high, e_mid, e_low = [part.astype(F32) for part in pieces(exposure[r : r + 1, :], 3)]
        e_rows = jnp.where((sub == 0) | (sub == 3) | (sub == 5), e_high, 0.0)
        e_rows = jnp.where((sub == 1) | (sub == 4), e_mid, e_rows)
        e_rows = jnp.where(sub == 2, e_low, e_rows).astype(BF16)
        extra = jnp.concatenate([e_rows, high, mid, low, high, mid, high, spare], axis=0)
        right_ref[r, 0:ncat, :] = count
        right_ref[r, LANES : 2 * LANES, :] = extra
        right_ref[r, 2 * LANES : 2 * LANES + ncat, :] = count
        right_ref[r, 3 * LANES : 3 * LANES + ncat, :] = count
        for side in range(2):
            wide_ref[r, 0:ncat, side * cols : (side + 1) * cols] = count
            wide_ref[r, LANES : 2 * LANES, side * cols : (side + 1) * cols] = extra


def field_weights(tau_ref, nfac, cols):
    row = lax.broadcasted_iota(jnp.int32, (nfac, cols), 0)
    tau = jnp.zeros((nfac, cols), F32)
    for j in range(nfac):
        tau = jnp.where(row == j, tau_ref[j], tau)
    return tau


def load_prior(rows, lands, tau, prior_ref):
    nfac, cols = tau.shape
    inner = lax.broadcasted_iota(jnp.int32, (nfac, cols), 1) < cols - 1
    energy = jnp.zeros((nfac, cols), F32)
    lands = [jnp.broadcast_to(x, (nfac, cols)) for x in lands]
    for r in range(len(rows) - 2):
        here = rows[r + 1]
        step_right = here - pltpu.roll(here, cols - 1, 1)
        edge_right = jnp.where(inner, lands[r + 1] * pltpu.roll(lands[r + 1], cols - 1, 1), 0.0)
        flux_right = edge_right * step_right
        laplace = flux_right - pltpu.roll(flux_right, 1, 1)
        parts = flux_right * step_right + RIDGE * (here * here)
        if rows[r] is not None:
            laplace = laplace + lands[r] * lands[r + 1] * (here - rows[r])
        if rows[r + 2] is not None:
            step_down = here - rows[r + 2]
            flux_down = lands[r + 1] * lands[r + 2] * step_down
            laplace = laplace + flux_down
            parts = parts + flux_down * step_down
        prior_ref[r] = -tau * (laplace + RIDGE * here)
        energy = energy + 0.5 * tau * parts
    return energy


def pack_edge(edge_ref, field, fresh, land):
    nfac, cols = field.shape
    blocks = cols // LANES
    sub = lax.broadcasted_iota(jnp.int32, (8, LANES), 0)
    lands = jnp.zeros((8, LANES), F32)
    for b in range(blocks):
        lanes = slice(b * LANES, (b + 1) * LANES)
        edge_ref[b * nfac : (b + 1) * nfac, :] = field[:, lanes]
        edge_ref[(blocks + b) * nfac : (blocks + b + 1) * nfac, :] = fresh[:, lanes]
        lands = jnp.where(sub == b, land[:, lanes], lands)
    edge_ref[2 * blocks * nfac :, :] = lands


def unpack_edge(edge, nfac, cols):
    blocks = cols // LANES
    wide = lambda start, size, step: jnp.concatenate(
        [edge[start + b * step : start + b * step + size, :] for b in range(blocks)], axis=1
    )
    return wide(0, nfac, nfac), wide(blocks * nfac, nfac, nfac), wide(2 * blocks * nfac, 1, 1)


def row_scores(r, right_ref, left_ref, mix_ref, score_ref, logit_ref):
    tops = []
    for target, values in (
        (score_ref, dot(left_ref[...], right_ref[r])),
        (logit_ref, dot(mix_ref[...], right_ref[r, LANES : 2 * LANES, :])),
    ):
        target[...] = values
        ncomp, cols = values.shape
        tops.append(jnp.max(jnp.max(values.reshape(ncomp // 8, 8, cols), axis=0), axis=0, keepdims=True))
    return tops


def row_shares(tops, land, score_ref, logit_ref, post_ref, gap_ref, kept_ref):
    ncomp, cols = score_ref.shape
    block = 32
    top_s, top_a = tops
    sum_s = jnp.zeros((8, cols), F32)
    sum_a = jnp.zeros((8, cols), F32)
    for i in range(0, ncomp, block):
        part_s = jnp.exp2(score_ref[i : i + block, :] - top_s)
        part_a = jnp.exp2(logit_ref[i : i + block, :] - top_a)
        score_ref[i : i + block, :] = part_s
        logit_ref[i : i + block, :] = part_a
        sum_s = sum_s + jnp.sum(part_s.reshape(block // 8, 8, cols), axis=0)
        sum_a = sum_a + jnp.sum(part_a.reshape(block // 8, 8, cols), axis=0)
    sum_s = jnp.sum(sum_s, axis=0, keepdims=True)
    sum_a = jnp.sum(sum_a, axis=0, keepdims=True)
    log_s = top_s + jnp.log2(sum_s)
    log_a = top_a + jnp.log2(sum_a)
    inv_s = land / sum_s
    inv_a = land / sum_a
    for i in range(0, ncomp, block):
        post = score_ref[i : i + block, :] * inv_s
        gap = post - logit_ref[i : i + block, :] * inv_a
        for targets, values in (((post_ref,), post), ((gap_ref, kept_ref), gap)):
            high, low = pieces(values, 2)
            for target in targets:
                target[i : i + block, 0:cols] = high
                target[i : i + block, cols : 2 * cols] = low
    return land * (LN2 * (log_s - log_a))


def row_products(r, wide_ref, post_ref, gap_ref, acc_ref, accw_ref):
    nfac = accw_ref.shape[0] // 3
    last = ((1,), (1,))
    start = LANES + EXTRA
    acc = dot(post_ref[...], wide_ref[r], last)
    accw = dot(wide_ref[r, start : start + 3 * nfac, :], gap_ref[...], last)
    if r == 0:
        acc_ref[...] = acc
        accw_ref[...] = accw
    else:
        acc_ref[...] += acc
        accw_ref[...] += accw


def field_grads(load_ref, gap_refs, prior_ref):
    share, nfac, cols = prior_ref.shape
    for r in range(share):
        lik = dot(load_ref[...], gap_refs[r][...])
        lik = lik[0:nfac] + lik[nfac : 2 * nfac]
        prior_ref[r] += lik[:, 0:cols] + lik[:, cols : 2 * cols]


def all_rows(land, right, wide, left, mix, scores, logits, posts, gaps, kept, acc, accw):
    share, _, cols = right.shape
    log_dens = jnp.zeros((1, cols), F32)
    tops = {}
    for r in range(share + 2):
        if r < share:
            tops[r] = row_scores(r, right, left, mix, scores[r % 2], logits[r % 2])
        if 0 <= r - 1 < share:
            p = r - 1
            log_dens = log_dens + row_shares(
                tops[p], land[p : p + 1, :], scores[p % 2], logits[p % 2], posts[p % 2], gaps[p % 2], kept[p]
            )
        if 0 <= r - 2:
            p = r - 2
            row_products(p, wide, posts[p % 2], gaps[p % 2], acc, accw)
    return log_dens


def param_grads(flat_ref, acc_ref, accw_ref, grad_ref, ncomp, nfac):
    lane = lax.broadcasted_iota(jnp.int32, (LANES, LANES), 1)
    for q in range(ncomp // LANES):
        rows = pl.ds(q * LANES, LANES)
        lanes = slice(q * LANES, (q + 1) * LANES)
        mass = jnp.sum(jnp.where(lane < 3, acc_ref[rows, LANES : 2 * LANES], 0.0), axis=1, keepdims=True)
        grad_ref[rows, :] = acc_ref[rows, 0:LANES] - jnp.exp(flat_ref[rows, :]) * mass
        load = accw_ref[:, lanes]
        grad_ref[pl.ds(ncomp + q * nfac, nfac), :] = load[0:nfac] + load[nfac : 2 * nfac] + load[2 * nfac : 3 * nfac]


def first_kernel(
    ncomp, rank_ref, counts_ref, field_ref, land_ref, logexp_ref, pmom_ref, wmom_ref, pack_ref, got_ref, others_ref, *refs
):
    gaps, refs = refs[: counts_ref.shape[0]], refs[counts_ref.shape[0] :]
    load, grad_ref, keep_ref, send_ref, flat, left, mix, right, wide, score0, score1, logit0, logit1, *refs = refs
    post0, post1, gap0, gap1, acc, accw, stage = refs
    cells_rank, comp_rank = rank_ref[0], rank_ref[1]
    share, nfac, cols = field_ref.shape
    mine = pmom_ref.shape[0]
    core = cells_rank % 2
    size = mine + nfac
    for source, side in ((got_ref, core), (others_ref, 1 - core)):
        stage[pl.ds(pl.multiple_of(side * (size // 2), 8), size // 2), :] = source[size:, :]
    for source, group in (
        (pack_ref, comp_rank),
        (got_ref, comp_rank ^ (1 + core)),
        (others_ref, comp_rank ^ (2 - core)),
        (stage, comp_rank ^ 3),
    ):
        flat[pl.ds(pl.multiple_of(group * mine, mine), mine), :] = source[0:mine, :]
        flat[pl.ds(pl.multiple_of(ncomp + group * nfac, nfac), nfac), :] = source[mine:size, :]
    here = pl.ds(pl.multiple_of(comp_rank * share, 8), share)
    land = land_ref[here, :].astype(F32)
    load_params(flat, left, mix, load, ncomp, nfac)
    load_cells(counts_ref, field_ref, logexp_ref[here, :], right, wide)
    all_rows(land, right, wide, left, mix, (score0, score1), (logit0, logit1), (post0, post1), (gap0, gap1), gaps, acc, accw)
    param_grads(flat, acc, accw, grad_ref, ncomp, nfac)
    nparam = grad_ref.shape[0]
    if flat.shape[0] > nparam:
        flat[nparam:, :] = jnp.zeros((flat.shape[0] - nparam, LANES), F32)
    flat[0:nparam, :] = 0.5 * STEP_PARAM * STEP_PARAM * grad_ref[...]
    own_prof, own_load = pack_ref[0:mine, :], pack_ref[mine:size, :]
    owner = cells_rank == 0
    base_prof = own_prof + STEP_PARAM * (pmom_ref[...] - 0.5 * STEP_PARAM * 0.25 * own_prof)
    base_load = own_load + STEP_PARAM * (wmom_ref[...] - 0.5 * STEP_PARAM * own_load)
    flat[pl.ds(pl.multiple_of(comp_rank * mine, mine), mine), :] += jnp.where(owner, base_prof, 0.0)
    flat[pl.ds(pl.multiple_of(ncomp + comp_rank * nfac, nfac), nfac), :] += jnp.where(owner, base_load, 0.0)
    spread_chunks(flat, keep_ref, send_ref, cells_rank)


def first_field(rank_ref, tau_ref, field_ref, mom_ref, land_ref, load_ref, *refs):
    gap_refs, refs = refs[: field_ref.shape[0]], refs[field_ref.shape[0] :]
    new_ref, half_ref, near_ref, far_ref, prior = refs
    comp_rank = rank_ref[1]
    share, nfac, cols = field_ref.shape
    land = land_ref[pl.ds(pl.multiple_of(comp_rank * share, 8), share), :].astype(F32)
    lands = [land[r : r + 1, :] for r in range(share)]
    tau = field_weights(tau_ref, nfac, cols)
    load_prior([None] + [field_ref[r] for r in range(share)] + [None], lands[:1] + lands + lands[-1:], tau, prior)
    field_grads(load_ref, gap_refs, prior)
    for r in range(share):
        half = mom_ref[r] + 0.5 * STEP_FIELD * prior[r]
        half_ref[r] = half
        new_ref[r] = field_ref[r] + STEP_FIELD * half
    even = comp_rank % 2 == 0
    end = share - 1
    for target, flag in ((near_ref, even), (far_ref, jnp.logical_not(even))):
        pack_edge(
            target,
            jnp.where(flag, field_ref[end], field_ref[0]),
            jnp.where(flag, new_ref[end], new_ref[0]),
            jnp.where(flag, lands[end], lands[0]),
        )


def edge_terms(chunk, ring, tiles, rank_ref, tau, lands, old_ref, near_ref, far_ref, edge_ref):
    cells_rank, comp_rank = rank_ref[0], rank_ref[1]
    nfac, cols = tau.shape
    source = jnp.where(comp_rank == 0, cells_rank - 1, jnp.where(comp_rank == ring - 1, cells_rank + 1, cells_rank))
    source = jnp.clip(source, 0, tiles - 1)
    slot = (source // 2) ^ (cells_rank // 2)
    relay = jnp.where(source % 2 == cells_rank % 2, near_ref[slot, chunk:, :], far_ref[slot, chunk:, :])
    even = comp_rank % 2 == 0
    direct = edge_ref[...]
    above = unpack_edge(jnp.where(even, relay, direct), nfac, cols)
    below = unpack_edge(jnp.where(even, direct, relay), nfac, cols)
    land_above = jnp.where((comp_rank == 0) & (cells_rank == 0), 0.0, above[2])
    land_below = jnp.where((comp_rank == ring - 1) & (cells_rank == tiles - 1), 0.0, below[2])
    pull_up = -tau * (land_above * lands[0]) * (old_ref[0] - above[0])
    pull_down = -tau * (land_below * lands[-1]) * (old_ref[old_ref.shape[0] - 1] - below[0])
    return (above[1], below[1]), (land_above, land_below), (pull_up, pull_down)


def second_kernel(
    ncomp, chunk, ring, tiles, rank_ref, tau_ref, counts_ref, field_ref, land_ref, logexp_ref, pmom_ref, wmom_ref, old_ref,
    own_ref, near_ref, far_ref, edge_ref, grad0_ref, *refs
):
    gaps, refs = refs[: counts_ref.shape[0]], refs[counts_ref.shape[0] :]
    load, new_ref, params_ref, stats_ref, keep_ref, send_ref, flat, left, mix, right, wide, *refs = refs
    score0, score1, logit0, logit1, post0, post1, gap0, gap1, acc, accw, out, grad = refs
    cells_rank, comp_rank = rank_ref[0], rank_ref[1]
    share, nfac, cols = field_ref.shape
    mine = pmom_ref.shape[0]
    nparam = grad0_ref.shape[0]
    gather_chunks(flat, near_ref, far_ref, cells_rank, chunk)
    new_prof = flat[pl.ds(pl.multiple_of(comp_rank * mine, mine), mine), :]
    new_load = flat[pl.ds(pl.multiple_of(ncomp + comp_rank * nfac, nfac), nfac), :]
    params_ref[0:mine, :] = new_prof
    params_ref[mine:, :] = new_load
    here = pl.ds(pl.multiple_of(comp_rank * share, 8), share)
    land = land_ref[here, :].astype(F32)
    lands = [land[r : r + 1, :] for r in range(share)]
    tau = field_weights(tau_ref, nfac, cols)
    _, _, pulls = edge_terms(chunk, ring, tiles, rank_ref, tau, lands, old_ref, near_ref, far_ref, edge_ref)
    move = 0.5 * STEP_FIELD * STEP_FIELD
    for r in range(share):
        fresh = field_ref[r]
        if r == 0:
            fresh = fresh + move * pulls[0]
        if r == share - 1:
            fresh = fresh + move * pulls[1]
        new_ref[r] = fresh
    load_params(flat, left, mix, load, ncomp, nfac)
    load_cells(counts_ref, new_ref, logexp_ref[here, :], right, wide)
    log_dens = all_rows(land, right, wide, left, mix, (score0, score1), (logit0, logit1), (post0, post1), (gap0, gap1), gaps, acc, accw)
    param_grads(flat, acc, accw, grad, ncomp, nfac)
    first_device = (cells_rank == 0) & (comp_rank == 0)
    prof_all = flat[0:ncomp, :]
    load_all = flat[ncomp:nparam, :]
    param_energy = jnp.sum(0.125 * (prof_all * prof_all).reshape(ncomp // 8, 8, LANES), axis=0)
    param_energy = param_energy + jnp.sum(
        0.5 * (load_all * load_all).reshape((nparam - ncomp) // 8, 8, LANES), axis=0
    )
    stats_ref[0:8, :] = jnp.where(first_device, param_energy, 0.0)
    sub = lax.broadcasted_iota(jnp.int32, (8, LANES), 0)
    dens = jnp.zeros((8, LANES), F32)
    for b in range(cols // LANES):
        dens = jnp.where(sub == b, -log_dens[:, b * LANES : (b + 1) * LANES], dens)
    stats_ref[8:16, :] = dens
    if out.shape[0] > nparam:
        out[nparam:, :] = jnp.zeros((out.shape[0] - nparam, LANES), F32)
    out[0:nparam, :] = 0.5 * STEP_PARAM * (grad0_ref[...] + grad[...])
    owner = cells_rank == 0
    old_prof, old_load = own_ref[0:mine, :], own_ref[mine : mine + nfac, :]
    base_prof = pmom_ref[...] - 0.5 * STEP_PARAM * 0.25 * (old_prof + new_prof)
    base_load = wmom_ref[...] - 0.5 * STEP_PARAM * (old_load + new_load)
    out[pl.ds(pl.multiple_of(comp_rank * mine, mine), mine), :] += jnp.where(owner, base_prof, 0.0)
    out[pl.ds(pl.multiple_of(ncomp + comp_rank * nfac, nfac), nfac), :] += jnp.where(owner, base_load, 0.0)
    spread_chunks(out, keep_ref, send_ref, cells_rank)


def second_field(
    chunk, ring, tiles, rank_ref, tau_ref, new_ref, half_ref, old_ref, land_ref, load_ref, stats_ref, near_ref, far_ref,
    edge_ref, *refs
):
    gap_refs, (mom_ref, energy_ref, prior) = refs[: new_ref.shape[0]], refs[new_ref.shape[0] :]
    comp_rank = rank_ref[1]
    share, nfac, cols = new_ref.shape
    land = land_ref[pl.ds(pl.multiple_of(comp_rank * share, 8), share), :].astype(F32)
    lands = [land[r : r + 1, :] for r in range(share)]
    tau = field_weights(tau_ref, nfac, cols)
    (above, below), (land_above, land_below), (pull_up, pull_down) = edge_terms(
        chunk, ring, tiles, rank_ref, tau, lands, old_ref, near_ref, far_ref, edge_ref
    )
    move = 0.5 * STEP_FIELD * STEP_FIELD
    rows = [above - move * pull_up] + [new_ref[r] for r in range(share)] + [below - move * pull_down]
    energy = load_prior(rows, [land_above] + lands + [land_below], tau, prior)
    prior[0] += pull_up
    prior[share - 1] += pull_down
    field_grads(load_ref, gap_refs, prior)
    for r in range(share):
        fresh = half_ref[r] + 0.5 * STEP_FIELD * prior[r]
        mom_ref[r] = fresh
        energy = energy + 0.5 * (fresh * fresh)
    tiles_sum = stats_ref[0:8, :] + stats_ref[8:16, :]
    for i in range(0, nfac, 8):
        for b in range(0, cols, LANES):
            tiles_sum = tiles_sum + energy[i : i + 8, b : b + LANES]
    energy_ref[...] = tiles_sum


def last_kernel(ncomp, nparam, chunk, cells, rank_ref, near_ref, far_ref, prof_ref, mixing_ref, ham_ref, flat):
    cells_rank, comp_rank = rank_ref[0], rank_ref[1]
    mine, nfac = prof_ref.shape[0], mixing_ref.shape[0]
    gather_chunks(flat, near_ref, far_ref, cells_rank, chunk)
    prof_ref[...] = flat[pl.ds(pl.multiple_of(comp_rank * mine, mine), mine), :]
    mixing_ref[...] = flat[pl.ds(pl.multiple_of(ncomp + comp_rank * nfac, nfac), nfac), :]
    momenta = flat[0:nparam, :]
    total = jnp.sum(0.5 * (momenta * momenta).reshape(nparam // 8, 8, LANES), axis=0)
    for source in (near_ref, far_ref):
        total = total + jnp.sum(source[:, chunk:, :], axis=0)
    total = jnp.sum(jnp.sum(total, axis=0, keepdims=True), axis=1, keepdims=True)
    ham_ref[...] = total / cells


def fast_device(
    factor_field, profile, mixing, factor_mom, profile_mom, mixing_mom, field_tau, counts, land_mask, log_exposure
):
    nfac, share, cols = factor_field.shape
    mine, ncat = profile.shape
    tile_rows = land_mask.shape[0]
    ring = lax.axis_size("comp")
    tiles = lax.axis_size("cells")
    ncomp = mine * ring
    nparam = ncomp + nfac * ncomp // LANES
    pairs = tiles // 2
    edge = 2 * nfac * cols // LANES + 8
    round_up = lambda rows: -(-rows // (8 * tiles)) * 8
    chunk = round_up(nparam)
    comp_rank = lax.axis_index("comp")
    cells_rank = lax.axis_index("cells")
    ranks = jnp.stack([cells_rank, comp_rank]).astype(jnp.int32)
    pack = lax.optimization_barrier(jnp.pad(profile, ((0, nfac), (0, 0))) + jnp.pad(mixing, ((mine, 0), (0, 0))))
    got, others = gather_params(pack, cells_rank)
    count_rows = lax.dynamic_slice_in_dim(counts, comp_rank * share, share, 1).swapaxes(0, 1).astype(BF16)
    field_rows = factor_field.swapaxes(0, 1)
    mom_rows = factor_mom.swapaxes(0, 1)
    vmem = pl.BlockSpec(memory_space=pltpu.VMEM)
    smem = pl.BlockSpec(memory_space=pltpu.SMEM)
    shape = lambda *dims: jax.ShapeDtypeStruct(dims, F32)
    work = [
        pltpu.VMEM((tiles * chunk, LANES), F32),
        pltpu.VMEM((ncomp, 4 * LANES), BF16),
        pltpu.VMEM((ncomp, LANES), BF16),
        pltpu.VMEM((share, 4 * LANES, cols), BF16),
        pltpu.VMEM((share, 2 * LANES, 2 * cols), BF16),
    ]
    work += [pltpu.VMEM((ncomp, cols), F32)] * 4 + [pltpu.VMEM((ncomp, 2 * cols), BF16)] * 4
    work += [
        pltpu.VMEM((ncomp, 2 * LANES), F32),
        pltpu.VMEM((3 * nfac, ncomp), F32),
    ]
    field_shape = shape(share, nfac, cols)
    chunk_shape = shape(pairs, chunk, LANES)
    gap_shapes = [jax.ShapeDtypeStruct((ncomp, 2 * cols), BF16)] * share
    load_shape = jax.ShapeDtypeStruct((2 * nfac, ncomp), BF16)
    field_flops = 2 * 2 * nfac * ncomp * 2 * cols * share
    field_cost = pl.CostEstimate(flops=field_flops, bytes_accessed=4 * share * ncomp * cols, transcendentals=0)

    def call(body, name, smem_count, vmem_count, outs, scratch, cost=None):
        return pl.pallas_call(
            body,
            name=name,
            in_specs=[smem] * smem_count + [vmem] * vmem_count,
            out_specs=[vmem] * len(outs),
            scratch_shapes=scratch,
            out_shape=outs,
            cost_estimate=cost,
            compiler_params=pltpu.CompilerParams(vmem_limit_bytes=40 * 1024 * 1024),
        )

    prior = [pltpu.VMEM((share, nfac, cols), F32)]
    first = call(
        functools.partial(first_kernel, ncomp),
        "first_gradient",
        1,
        9,
        gap_shapes + [load_shape, shape(nparam, LANES), chunk_shape, chunk_shape],
        work + [pltpu.VMEM((mine + nfac, LANES), F32)],
    )
    *gaps, load, grad, keep, send = first(
        ranks, count_rows, field_rows, land_mask, log_exposure, profile_mom, mixing_mom, pack, got, others
    )
    edge_shape = shape(edge, LANES)
    part_field, half, near_edge, far_edge = call(
        first_field, "first_field", 2, 4 + share, [field_shape, field_shape, edge_shape, edge_shape], prior, field_cost
    )(ranks, field_tau, field_rows, mom_rows, land_mask, load, *gaps)
    near, far, got_edge, _ = all_sum(keep, send, near_edge, far_edge)
    second = call(
        functools.partial(second_kernel, ncomp, chunk, ring, tiles),
        "second_gradient",
        2,
        12,
        gap_shapes
        + [
            load_shape,
            field_shape,
            shape(mine + nfac, ncat),
            shape(16, LANES),
            chunk_shape,
            chunk_shape,
        ],
        work + [pltpu.VMEM((tiles * chunk, LANES), F32), pltpu.VMEM((nparam, LANES), F32)],
    )
    *gaps, load, new_field, new_params, stats, keep, send = second(
        ranks, field_tau, count_rows, part_field, land_mask, log_exposure, profile_mom, mixing_mom, field_rows, pack, near,
        far, got_edge, grad,
    )
    new_mom, energy = call(
        functools.partial(second_field, chunk, ring, tiles), "second_field", 2, 9 + share, [field_shape, shape(8, LANES)], prior, field_cost
    )(ranks, field_tau, new_field, half, field_rows, land_mask, load, stats, near, far, got_edge, *gaps)
    done = (new_field.swapaxes(0, 1), new_params[:mine], new_params[mine:], new_mom.swapaxes(0, 1))
    near, far, _, done = all_sum(keep, send, late=energy, beside=done)
    final = call(
        functools.partial(last_kernel, ncomp, nparam, chunk, tile_rows * cols * tiles),
        "momenta",
        1,
        2,
        [shape(mine, ncat), shape(nfac, mine), shape(1, 1)],
        [pltpu.VMEM((tiles * chunk, LANES), F32)],
    )
    new_profile_mom, new_mixing_mom, hamiltonian = final(ranks, near, far)
    return (
        *done,
        new_profile_mom,
        new_mixing_mom,
        hamiltonian.reshape(()),
    )


def power_of_two(count):
    return count & (count - 1) == 0


def choose_device(*args):
    factor_field, profile, mixing = args[:3]
    nfac, share, cols = factor_field.shape
    mine, ncat = profile.shape
    tiles, ring = lax.axis_size("cells"), lax.axis_size("comp")
    fits = mine == LANES and ncat == LANES and nfac % 16 == 0 and 6 * nfac + EXTRA <= LANES
    fits = fits and share % 8 == 0 and cols % LANES == 0 and cols <= 8 * LANES
    fits = fits and power_of_two(tiles) and tiles > 1 and ring == 4
    return fast_device(*args) if fits else plain_device(*args)


def solution(mesh):
    in_specs = (
        P(None, ("cells", "comp"), None),
        P("comp", None),
        P(None, "comp"),
        P(None, ("cells", "comp"), None),
        P("comp", None),
        P(None, "comp"),
        P(),
        P(None, "cells", None),
        P("cells", None),
        P("cells", None),
    )
    out_specs = (
        P(None, ("cells", "comp"), None),
        P("comp", None),
        P(None, "comp"),
        P(None, ("cells", "comp"), None),
        P("comp", None),
        P(None, "comp"),
        P(),
    )
    return jax.shard_map(
        choose_device, mesh=mesh, in_specs=in_specs, out_specs=out_specs, check_vma=False
    )
```

```python
import functools
import math

import jax
import jax.numpy as jnp
from jax import lax
from jax.experimental import pallas as pl
from jax.experimental.pallas import tpu as pltpu
from jax.sharding import PartitionSpec as P


def extended(cells, sides, width):
    for axis, dim in sides:
        count = lax.axis_size(axis)
        ends = count - 1
        head = lax.slice_in_dim(cells, 0, width, axis=dim)
        tail = lax.slice_in_dim(cells, cells.shape[dim] - width, cells.shape[dim], axis=dim)
        cells = jnp.concatenate(
            [
                lax.ppermute(tail, axis, [(i, (i + 1) % count) for i in range(ends)]),
                cells,
                lax.ppermute(head, axis, [((i + 1) % count, i) for i in range(ends)]),
            ],
            axis=dim,
        )
    return cells


def field_prior(padded, land_pad, field_tau):
    ridge = 0.1
    step_x = padded[:, 1:, :] - padded[:, :-1, :]
    edge_x = land_pad[1:, :] * land_pad[:-1, :]
    flux_x = edge_x[None, :, :] * step_x
    centre = padded[:, 1:-1, :]
    land_mid = land_pad[1:-1, :]
    step_y = centre[:, :, 1:] - centre[:, :, :-1]
    edge_y = land_mid[:, 1:] * land_mid[:, :-1]
    flux_y = edge_y[None, :, :] * step_y
    lap_x = flux_x[:, :-1, :] - flux_x[:, 1:, :]
    lap_y = jnp.pad(flux_y, ((0, 0), (0, 0), (1, 0))) - jnp.pad(flux_y, ((0, 0), (0, 0), (0, 1)))
    tau_cube = field_tau[:, None, None]
    grad = -tau_cube * (lap_x + lap_y + ridge * centre)
    energy = 0.5 * jnp.sum(tau_cube * (flux_x[:, 1:, :] * step_x[:, 1:, :]))
    energy = energy + 0.5 * jnp.sum(tau_cube * (flux_y * step_y))
    energy = energy + 0.5 * ridge * jnp.sum(tau_cube * (centre * centre))
    return (grad, energy)


def tile_scores(flat_tile, count_rows, exposure, profile, mixing):
    prof_exp = jnp.exp(profile)
    rate_total = jnp.sum(prof_exp, axis=1)
    mix_logit = jnp.dot(mixing.T, flat_tile, precision=lax.Precision.HIGHEST)
    fit_score = (
        jnp.dot(profile, count_rows, precision=lax.Precision.HIGHEST)
        - rate_total[:, None] * exposure[None, :]
    )
    return (mix_logit, mix_logit + fit_score)


def tile_grads(
    flat_tile, count_rows, land_weight, exposure, mixing, mix_logit, joint_score, log_mix, log_joint
):
    prior_share = jnp.exp(mix_logit - log_mix[None, :])
    posterior = jnp.exp(joint_score - log_joint[None, :])
    post_land = posterior * land_weight[None, :]
    gap_weight = (posterior - prior_share) * land_weight[None, :]
    grad_counts = jnp.dot(post_land, count_rows.T, precision=lax.Precision.HIGHEST)
    rate_mass = jnp.sum(post_land * exposure[None, :], axis=1)
    grad_mix = jnp.dot(flat_tile, gap_weight.T, precision=lax.Precision.HIGHEST)
    field_lik = jnp.dot(mixing, gap_weight, precision=lax.Precision.HIGHEST)
    log_dens = jnp.sum(land_weight * (log_joint - log_mix))
    return (grad_counts, rate_mass, grad_mix, field_lik, log_dens)


def log_sum(scores):
    top = jnp.max(scores, axis=0)
    return top + jnp.log(jnp.sum(jnp.exp(scores - top[None, :]), axis=0))


def plain_device(
    factor_field,
    profile,
    mixing,
    factor_mom,
    profile_mom,
    mixing_mom,
    field_tau,
    counts,
    land_mask,
    log_exposure,
):
    step_field = 0.05
    step_profile = 0.002
    step_mixing = 0.002
    tile_rows, tile_cols = land_mask.shape
    ncat = counts.shape[0]
    share_rows = factor_field.shape[1]
    comp_rank = lax.axis_index("comp")
    cells_rank = lax.axis_index("cells")
    first_cells = cells_rank == 0
    land_pad = extended(land_mask, (("cells", 0),), 1).astype(jnp.float32)
    row_start = comp_rank * share_rows
    count_rows = lax.dynamic_slice_in_dim(counts, row_start, share_rows, 1)
    count_rows = count_rows.reshape(ncat, share_rows * tile_cols).astype(jnp.float32)
    land_weight = (
        lax.dynamic_slice_in_dim(land_mask, row_start, share_rows, 0)
        .reshape(-1)
        .astype(jnp.float32)
    )
    exposure = jnp.exp(lax.dynamic_slice_in_dim(log_exposure, row_start, share_rows, 0).reshape(-1))
    land_near = lax.dynamic_slice_in_dim(land_pad, row_start, share_rows + 2, 0)

    def evaluate(share_field, profile_now, mixing_now):
        padded = extended(share_field, ((("cells", "comp"), 1),), 1)
        prior_grad, prior_energy = field_prior(padded, land_near, field_tau)
        profile_all, mixing_all = (
            lax.all_gather(profile_now, "comp", axis=0, tiled=True),
            lax.all_gather(mixing_now, "comp", axis=1, tiled=True),
        )
        flat_tile = share_field.reshape(share_field.shape[0], -1)
        mix_logit, joint_score = tile_scores(
            flat_tile, count_rows, exposure, profile_all, mixing_all
        )
        log_mix = log_sum(mix_logit)
        log_joint = log_sum(joint_score)
        grad_counts, rate_mass, grad_mix, field_lik, log_dens = tile_grads(
            flat_tile,
            count_rows,
            land_weight,
            exposure,
            mixing_all,
            mix_logit,
            joint_score,
            log_mix,
            log_joint,
        )
        grad_counts, rate_mass, mix_rows = (
            lax.psum_scatter(grad_counts, "comp", scatter_dimension=0, tiled=True),
            lax.psum_scatter(rate_mass, "comp", scatter_dimension=0, tiled=True),
            lax.psum_scatter(grad_mix.T, "comp", scatter_dimension=0, tiled=True),
        )
        grad_mix = mix_rows.T
        grad_field = prior_grad + field_lik.reshape(share_field.shape)
        log_part = log_dens - prior_energy
        grad_counts, rate_mass, grad_mix = lax.psum((grad_counts, rate_mass, grad_mix), "cells")
        grad_profile = grad_counts - jnp.exp(profile_now) * rate_mass[:, None] - 0.25 * profile_now
        grad_mixing = grad_mix - mixing_now
        param_prior = -0.125 * jnp.sum(profile_now * profile_now) - 0.5 * jnp.sum(
            mixing_now * mixing_now
        )
        log_part = log_part + jnp.where(first_cells, param_prior, 0.0)
        return (log_part, grad_field, grad_profile, grad_mixing)

    first = evaluate(factor_field, profile, mixing)
    half_field = factor_mom + 0.5 * step_field * first[1]
    half_profile = profile_mom + 0.5 * step_profile * first[2]
    half_mixing = mixing_mom + 0.5 * step_mixing * first[3]
    new_field = factor_field + step_field * half_field
    new_profile = profile + step_profile * half_profile
    new_mixing = mixing + step_mixing * half_mixing
    second = evaluate(new_field, new_profile, new_mixing)
    new_factor_mom = half_field + 0.5 * step_field * second[1]
    new_profile_mom = half_profile + 0.5 * step_profile * second[2]
    new_mixing_mom = half_mixing + 0.5 * step_mixing * second[3]
    kinetic = 0.5 * jnp.sum(new_factor_mom * new_factor_mom)
    kinetic = kinetic + jnp.where(
        first_cells,
        0.5
        * (jnp.sum(new_profile_mom * new_profile_mom) + jnp.sum(new_mixing_mom * new_mixing_mom)),
        0.0,
    )
    log_total, kinetic_total = lax.psum((second[0], kinetic), ("cells", "comp"))
    cell_count = tile_rows * tile_cols * lax.axis_size("cells")
    hamiltonian = (kinetic_total - log_total) / cell_count
    return (
        new_field,
        new_profile,
        new_mixing,
        new_factor_mom,
        new_profile_mom,
        new_mixing_mom,
        hamiltonian,
    )


STEP_FIELD = 0.05
STEP_PARAM = 0.002
RIDGE = 0.1
LOG2E = math.log2(math.e)
LN2 = math.log(2.0)
LANES = 128
EXTRA = 16
F32 = jnp.float32
BF16 = jnp.bfloat16


def pieces(values, count):
    parts = []
    for _ in range(count):
        part = values.astype(BF16)
        parts.append(part)
        values = values - part.astype(F32)
    return parts


def dot(left, right, dims=((1,), (0,))):
    return lax.dot_general(left, right, (dims, ((), ())), preferred_element_type=F32)


def partner(values, axis, flip):
    count = lax.axis_size(axis)
    return lax.ppermute(values, axis, [(i, i ^ flip) for i in range(count)])


def all_sum(keep, send, near_edge, far_edge):
    pairs, rows, _ = keep.shape
    chunks = keep + partner(send, "cells", 1)
    total = chunks[0]
    for part in [partner(chunks[k], "cells", 2 * k) for k in range(1, pairs)]:
        total = total + part
    first = partner(jnp.concatenate([total, near_edge], axis=0), "comp", 1)
    second = partner(total, "comp", 2)
    third = partner(jnp.concatenate([total, far_edge], axis=0), "comp", 3)
    total = jnp.concatenate([total + first[:rows] + second + third[:rows], third[rows:]], axis=0)
    near = jnp.stack([total] + [partner(total, "cells", 2 * k) for k in range(1, pairs)])
    return near, partner(near, "cells", 1), first[rows:]


def group_sum(keep, send, energy, beside):
    ring, rows, _ = keep.shape
    pairs = lax.axis_size("cells") // 2
    halves = keep + partner(send, "cells", 1)
    total = halves[0]
    for part in [partner(halves[k], "comp", k) for k in range(1, ring)]:
        total = total + part
    total, beside = lax.optimization_barrier((total, beside))
    total = jnp.concatenate([total, energy], axis=0)
    for part in [partner(total, "cells", 2 * k) for k in range(1, pairs)]:
        total = total + part
    other = partner(total, "cells", 1)
    upper = lax.axis_index("cells") % 2 == 1
    low = jnp.where(upper, other, total)[:rows]
    high = jnp.where(upper, total, other)[:rows]
    return jnp.concatenate([low, high], axis=0), total[rows:] + other[rows:], beside


def gather_params(pack, cells_rank):
    tiles, ring = lax.axis_size("cells"), lax.axis_size("comp")
    rows = pack.shape[0]
    spread = [(c * ring + z, c * ring + (z ^ (1 + c % 2))) for c in range(tiles) for z in range(ring)]
    one = lax.ppermute(pack, ("cells", "comp"), spread)
    half = lax.dynamic_slice_in_dim(pack, cells_rank % 2 * (rows // 2), rows // 2, 0)
    got = jnp.concatenate([one, partner(half, "comp", 3)], axis=0)
    return got, partner(got, "cells", 1)


def chunk_index(cells_rank, k, other):
    core = cells_rank % 2
    return (((cells_rank // 2) ^ k) * 2) + (1 - core if other else core)


def gather_chunks(flat_ref, near_ref, far_ref, cells_rank, rows):
    for k in range(near_ref.shape[0]):
        for source, other in ((near_ref, False), (far_ref, True)):
            start = pl.multiple_of(chunk_index(cells_rank, k, other) * rows, 8)
            flat_ref[pl.ds(start, rows), :] = source[k, 0:rows, :]


def spread_chunks(flat_ref, keep_ref, send_ref, cells_rank):
    pairs, rows, _ = keep_ref.shape
    for k in range(pairs):
        for target, other in ((keep_ref, False), (send_ref, True)):
            start = pl.multiple_of(chunk_index(cells_rank, k, other) * rows, 8)
            target[k] = flat_ref[pl.ds(start, rows), :]


def load_params(flat_ref, left_ref, mix_ref, load_ref, ncomp, nfac):
    lane = lax.broadcasted_iota(jnp.int32, (LANES, LANES), 1)
    spare = jnp.zeros((LANES - EXTRA - 6 * nfac, LANES), F32)
    for q in range(ncomp // LANES):
        rows = pl.ds(q * LANES, LANES)
        prof = flat_ref[rows, :]
        high, mid, low = pieces(prof * LOG2E, 3)
        left_ref[rows, 0:LANES] = high
        left_ref[rows, 2 * LANES : 3 * LANES] = mid
        left_ref[rows, 3 * LANES : 4 * LANES] = low
        rate = jnp.sum(jnp.exp(prof), axis=1, keepdims=True) * LOG2E
        rate_high, rate_mid, rate_low = [part.astype(F32) for part in pieces(rate, 3)]
        load = flat_ref[pl.ds(ncomp + q * nfac, nfac), :]
        w_high, w_mid, w_low = [part.astype(F32) for part in pieces(load * LOG2E, 3)]
        stack = jnp.concatenate(
            [jnp.zeros((EXTRA, LANES), F32), w_high, w_high, w_high, w_mid, w_mid, w_low, spare], axis=0
        )
        turned = stack.T
        mix_ref[rows, :] = turned.astype(BF16)
        rate_part = jnp.where(
            lane < 3, rate_high, jnp.where(lane < 5, rate_mid, jnp.where(lane == 5, rate_low, 0.0))
        )
        left_ref[rows, LANES : 2 * LANES] = (turned - rate_part).astype(BF16)
        load_high, load_mid = pieces(load, 2)
        load_ref[0:nfac, q * LANES : (q + 1) * LANES] = load_high
        load_ref[nfac : 2 * nfac, q * LANES : (q + 1) * LANES] = load_mid


def load_cells(counts_ref, field_ref, log_exposure, right_ref, wide_ref):
    share, ncat, cols = counts_ref.shape
    nfac = field_ref.shape[1]
    exposure = jnp.exp(log_exposure)
    sub = lax.broadcasted_iota(jnp.int32, (EXTRA, cols), 0)
    spare = jnp.zeros((LANES - EXTRA - 6 * nfac, cols), BF16)
    for r in range(share):
        count = counts_ref[r]
        high, mid, low = pieces(field_ref[r], 3)
        e_high, e_mid, e_low = [part.astype(F32) for part in pieces(exposure[r : r + 1, :], 3)]
        e_rows = jnp.where((sub == 0) | (sub == 3) | (sub == 5), e_high, 0.0)
        e_rows = jnp.where((sub == 1) | (sub == 4), e_mid, e_rows)
        e_rows = jnp.where(sub == 2, e_low, e_rows).astype(BF16)
        extra = jnp.concatenate([e_rows, high, mid, low, high, mid, high, spare], axis=0)
        right_ref[r, 0:ncat, :] = count
        right_ref[r, LANES : 2 * LANES, :] = extra
        right_ref[r, 2 * LANES : 2 * LANES + ncat, :] = count
        right_ref[r, 3 * LANES : 3 * LANES + ncat, :] = count
        for side in range(2):
            wide_ref[r, 0:ncat, side * cols : (side + 1) * cols] = count
            wide_ref[r, LANES : 2 * LANES, side * cols : (side + 1) * cols] = extra


def field_weights(tau_ref, nfac, cols):
    row = lax.broadcasted_iota(jnp.int32, (nfac, cols), 0)
    tau = jnp.zeros((nfac, cols), F32)
    for j in range(nfac):
        tau = jnp.where(row == j, tau_ref[j], tau)
    return tau


def load_prior(rows, lands, tau, prior_ref):
    nfac, cols = tau.shape
    inner = lax.broadcasted_iota(jnp.int32, (nfac, cols), 1) < cols - 1
    energy = jnp.zeros((nfac, cols), F32)
    lands = [jnp.broadcast_to(x, (nfac, cols)) for x in lands]
    for r in range(len(rows) - 2):
        here = rows[r + 1]
        step_right = here - pltpu.roll(here, cols - 1, 1)
        edge_right = jnp.where(inner, lands[r + 1] * pltpu.roll(lands[r + 1], cols - 1, 1), 0.0)
        flux_right = edge_right * step_right
        laplace = flux_right - pltpu.roll(flux_right, 1, 1)
        parts = flux_right * step_right + RIDGE * (here * here)
        if rows[r] is not None:
            laplace = laplace + lands[r] * lands[r + 1] * (here - rows[r])
        if rows[r + 2] is not None:
            step_down = here - rows[r + 2]
            flux_down = lands[r + 1] * lands[r + 2] * step_down
            laplace = laplace + flux_down
            parts = parts + flux_down * step_down
        prior_ref[r] = -tau * (laplace + RIDGE * here)
        energy = energy + 0.5 * tau * parts
    return energy


def pack_edge(edge_ref, field, fresh, land):
    nfac, cols = field.shape
    blocks = cols // LANES
    sub = lax.broadcasted_iota(jnp.int32, (8, LANES), 0)
    lands = jnp.zeros((8, LANES), F32)
    for b in range(blocks):
        lanes = slice(b * LANES, (b + 1) * LANES)
        edge_ref[b * nfac : (b + 1) * nfac, :] = field[:, lanes]
        edge_ref[(blocks + b) * nfac : (blocks + b + 1) * nfac, :] = fresh[:, lanes]
        lands = jnp.where(sub == b, land[:, lanes], lands)
    edge_ref[2 * blocks * nfac :, :] = lands


def unpack_edge(edge, nfac, cols):
    blocks = cols // LANES
    wide = lambda start, size, step: jnp.concatenate(
        [edge[start + b * step : start + b * step + size, :] for b in range(blocks)], axis=1
    )
    return wide(0, nfac, nfac), wide(blocks * nfac, nfac, nfac), wide(2 * blocks * nfac, 1, 1)


def row_scores(r, right_ref, left_ref, mix_ref, score_ref, logit_ref):
    tops = []
    for target, values in (
        (score_ref, dot(left_ref[...], right_ref[r])),
        (logit_ref, dot(mix_ref[...], right_ref[r, LANES : 2 * LANES, :])),
    ):
        target[...] = values
        ncomp, cols = values.shape
        tops.append(jnp.max(jnp.max(values.reshape(ncomp // 8, 8, cols), axis=0), axis=0, keepdims=True))
    return tops


def row_shares(tops, land, score_ref, logit_ref, post_ref, gap_ref, kept_ref):
    ncomp, cols = score_ref.shape
    block = 32
    top_s, top_a = tops
    sum_s = jnp.zeros((8, cols), F32)
    sum_a = jnp.zeros((8, cols), F32)
    for i in range(0, ncomp, block):
        part_s = jnp.exp2(score_ref[i : i + block, :] - top_s)
        part_a = jnp.exp2(logit_ref[i : i + block, :] - top_a)
        score_ref[i : i + block, :] = part_s
        logit_ref[i : i + block, :] = part_a
        sum_s = sum_s + jnp.sum(part_s.reshape(block // 8, 8, cols), axis=0)
        sum_a = sum_a + jnp.sum(part_a.reshape(block // 8, 8, cols), axis=0)
    sum_s = jnp.sum(sum_s, axis=0, keepdims=True)
    sum_a = jnp.sum(sum_a, axis=0, keepdims=True)
    log_s = top_s + jnp.log2(sum_s)
    log_a = top_a + jnp.log2(sum_a)
    inv_s = land / sum_s
    inv_a = land / sum_a
    for i in range(0, ncomp, block):
        post = score_ref[i : i + block, :] * inv_s
        gap = post - logit_ref[i : i + block, :] * inv_a
        for targets, values in (((post_ref,), post), ((gap_ref, kept_ref), gap)):
            high, low = pieces(values, 2)
            for target in targets:
                target[i : i + block, 0:cols] = high
                target[i : i + block, cols : 2 * cols] = low
    return land * (LN2 * (log_s - log_a))


def row_products(r, wide_ref, post_ref, gap_ref, acc_ref, accw_ref):
    nfac = accw_ref.shape[0] // 3
    last = ((1,), (1,))
    start = LANES + EXTRA
    acc = dot(post_ref[...], wide_ref[r], last)
    accw = dot(wide_ref[r, start : start + 3 * nfac, :], gap_ref[...], last)
    if r == 0:
        acc_ref[...] = acc
        accw_ref[...] = accw
    else:
        acc_ref[...] += acc
        accw_ref[...] += accw


def field_grads(load_ref, gap_refs, prior_ref):
    share, nfac, cols = prior_ref.shape
    for r in range(share):
        lik = dot(load_ref[...], gap_refs[r][...])
        lik = lik[0:nfac] + lik[nfac : 2 * nfac]
        prior_ref[r] += lik[:, 0:cols] + lik[:, cols : 2 * cols]


def all_rows(land, right, wide, left, mix, scores, logits, posts, gaps, kept, acc, accw):
    share, _, cols = right.shape
    log_dens = jnp.zeros((1, cols), F32)
    tops = {}
    for r in range(share + 2):
        if r < share:
            tops[r] = row_scores(r, right, left, mix, scores[r % 2], logits[r % 2])
        if 0 <= r - 1 < share:
            p = r - 1
            log_dens = log_dens + row_shares(
                tops[p], land[p : p + 1, :], scores[p % 2], logits[p % 2], posts[p % 2], gaps[p % 2], kept[p]
            )
        if 0 <= r - 2:
            p = r - 2
            row_products(p, wide, posts[p % 2], gaps[p % 2], acc, accw)
    return log_dens


def param_grads(flat_ref, acc_ref, accw_ref, grad_ref, ncomp, nfac):
    lane = lax.broadcasted_iota(jnp.int32, (LANES, LANES), 1)
    for q in range(ncomp // LANES):
        rows = pl.ds(q * LANES, LANES)
        lanes = slice(q * LANES, (q + 1) * LANES)
        mass = jnp.sum(jnp.where(lane < 3, acc_ref[rows, LANES : 2 * LANES], 0.0), axis=1, keepdims=True)
        grad_ref[rows, :] = acc_ref[rows, 0:LANES] - jnp.exp(flat_ref[rows, :]) * mass
        load = accw_ref[:, lanes]
        grad_ref[pl.ds(ncomp + q * nfac, nfac), :] = load[0:nfac] + load[nfac : 2 * nfac] + load[2 * nfac : 3 * nfac]


def first_kernel(
    ncomp, rank_ref, counts_ref, field_ref, land_ref, logexp_ref, pmom_ref, wmom_ref, pack_ref, got_ref, others_ref, *refs
):
    gaps, refs = refs[: counts_ref.shape[0]], refs[counts_ref.shape[0] :]
    load, grad_ref, keep_ref, send_ref, flat, left, mix, right, wide, score0, score1, logit0, logit1, *refs = refs
    post0, post1, gap0, gap1, acc, accw, stage = refs
    cells_rank, comp_rank = rank_ref[0], rank_ref[1]
    share, nfac, cols = field_ref.shape
    mine = pmom_ref.shape[0]
    core = cells_rank % 2
    size = mine + nfac
    for source, side in ((got_ref, core), (others_ref, 1 - core)):
        stage[pl.ds(pl.multiple_of(side * (size // 2), 8), size // 2), :] = source[size:, :]
    for source, group in (
        (pack_ref, comp_rank),
        (got_ref, comp_rank ^ (1 + core)),
        (others_ref, comp_rank ^ (2 - core)),
        (stage, comp_rank ^ 3),
    ):
        flat[pl.ds(pl.multiple_of(group * mine, mine), mine), :] = source[0:mine, :]
        flat[pl.ds(pl.multiple_of(ncomp + group * nfac, nfac), nfac), :] = source[mine:size, :]
    here = pl.ds(pl.multiple_of(comp_rank * share, 8), share)
    land = land_ref[here, :].astype(F32)
    load_params(flat, left, mix, load, ncomp, nfac)
    load_cells(counts_ref, field_ref, logexp_ref[here, :], right, wide)
    all_rows(land, right, wide, left, mix, (score0, score1), (logit0, logit1), (post0, post1), (gap0, gap1), gaps, acc, accw)
    param_grads(flat, acc, accw, grad_ref, ncomp, nfac)
    nparam = grad_ref.shape[0]
    if flat.shape[0] > nparam:
        flat[nparam:, :] = jnp.zeros((flat.shape[0] - nparam, LANES), F32)
    flat[0:nparam, :] = 0.5 * STEP_PARAM * STEP_PARAM * grad_ref[...]
    own_prof, own_load = pack_ref[0:mine, :], pack_ref[mine:size, :]
    owner = cells_rank == 0
    base_prof = own_prof + STEP_PARAM * (pmom_ref[...] - 0.5 * STEP_PARAM * 0.25 * own_prof)
    base_load = own_load + STEP_PARAM * (wmom_ref[...] - 0.5 * STEP_PARAM * own_load)
    flat[pl.ds(pl.multiple_of(comp_rank * mine, mine), mine), :] += jnp.where(owner, base_prof, 0.0)
    flat[pl.ds(pl.multiple_of(ncomp + comp_rank * nfac, nfac), nfac), :] += jnp.where(owner, base_load, 0.0)
    spread_chunks(flat, keep_ref, send_ref, cells_rank)


def first_field(rank_ref, tau_ref, field_ref, mom_ref, land_ref, load_ref, *refs):
    gap_refs, refs = refs[: field_ref.shape[0]], refs[field_ref.shape[0] :]
    new_ref, half_ref, near_ref, far_ref, prior = refs
    comp_rank = rank_ref[1]
    share, nfac, cols = field_ref.shape
    land = land_ref[pl.ds(pl.multiple_of(comp_rank * share, 8), share), :].astype(F32)
    lands = [land[r : r + 1, :] for r in range(share)]
    tau = field_weights(tau_ref, nfac, cols)
    load_prior([None] + [field_ref[r] for r in range(share)] + [None], lands[:1] + lands + lands[-1:], tau, prior)
    field_grads(load_ref, gap_refs, prior)
    for r in range(share):
        half = mom_ref[r] + 0.5 * STEP_FIELD * prior[r]
        half_ref[r] = half
        new_ref[r] = field_ref[r] + STEP_FIELD * half
    even = comp_rank % 2 == 0
    end = share - 1
    for target, flag in ((near_ref, even), (far_ref, jnp.logical_not(even))):
        pack_edge(
            target,
            jnp.where(flag, field_ref[end], field_ref[0]),
            jnp.where(flag, new_ref[end], new_ref[0]),
            jnp.where(flag, lands[end], lands[0]),
        )


def edge_terms(chunk, ring, tiles, rank_ref, tau, lands, old_ref, near_ref, far_ref, edge_ref):
    cells_rank, comp_rank = rank_ref[0], rank_ref[1]
    nfac, cols = tau.shape
    source = jnp.where(comp_rank == 0, cells_rank - 1, jnp.where(comp_rank == ring - 1, cells_rank + 1, cells_rank))
    source = jnp.clip(source, 0, tiles - 1)
    slot = (source // 2) ^ (cells_rank // 2)
    relay = jnp.where(source % 2 == cells_rank % 2, near_ref[slot, chunk:, :], far_ref[slot, chunk:, :])
    even = comp_rank % 2 == 0
    direct = edge_ref[...]
    above = unpack_edge(jnp.where(even, relay, direct), nfac, cols)
    below = unpack_edge(jnp.where(even, direct, relay), nfac, cols)
    land_above = jnp.where((comp_rank == 0) & (cells_rank == 0), 0.0, above[2])
    land_below = jnp.where((comp_rank == ring - 1) & (cells_rank == tiles - 1), 0.0, below[2])
    pull_up = -tau * (land_above * lands[0]) * (old_ref[0] - above[0])
    pull_down = -tau * (land_below * lands[-1]) * (old_ref[old_ref.shape[0] - 1] - below[0])
    return (above[1], below[1]), (land_above, land_below), (pull_up, pull_down)


def second_kernel(
    ncomp, chunk, ring, tiles, rank_ref, tau_ref, counts_ref, field_ref, land_ref, logexp_ref, pmom_ref, wmom_ref, old_ref,
    own_ref, near_ref, far_ref, edge_ref, grad0_ref, *refs
):
    gaps, refs = refs[: counts_ref.shape[0]], refs[counts_ref.shape[0] :]
    load, new_ref, params_ref, stats_ref, keep_ref, send_ref, flat, left, mix, right, wide, *refs = refs
    score0, score1, logit0, logit1, post0, post1, gap0, gap1, acc, accw, out, grad = refs
    cells_rank, comp_rank = rank_ref[0], rank_ref[1]
    share, nfac, cols = field_ref.shape
    mine = pmom_ref.shape[0]
    nparam = grad0_ref.shape[0]
    gather_chunks(flat, near_ref, far_ref, cells_rank, chunk)
    new_prof = flat[pl.ds(pl.multiple_of(comp_rank * mine, mine), mine), :]
    new_load = flat[pl.ds(pl.multiple_of(ncomp + comp_rank * nfac, nfac), nfac), :]
    params_ref[0:mine, :] = new_prof
    params_ref[mine:, :] = new_load
    here = pl.ds(pl.multiple_of(comp_rank * share, 8), share)
    land = land_ref[here, :].astype(F32)
    lands = [land[r : r + 1, :] for r in range(share)]
    tau = field_weights(tau_ref, nfac, cols)
    _, _, pulls = edge_terms(chunk, ring, tiles, rank_ref, tau, lands, old_ref, near_ref, far_ref, edge_ref)
    move = 0.5 * STEP_FIELD * STEP_FIELD
    for r in range(share):
        fresh = field_ref[r]
        if r == 0:
            fresh = fresh + move * pulls[0]
        if r == share - 1:
            fresh = fresh + move * pulls[1]
        new_ref[r] = fresh
    load_params(flat, left, mix, load, ncomp, nfac)
    load_cells(counts_ref, new_ref, logexp_ref[here, :], right, wide)
    log_dens = all_rows(land, right, wide, left, mix, (score0, score1), (logit0, logit1), (post0, post1), (gap0, gap1), gaps, acc, accw)
    param_grads(flat, acc, accw, grad, ncomp, nfac)
    first_device = (cells_rank == 0) & (comp_rank == 0)
    prof_all = flat[0:ncomp, :]
    load_all = flat[ncomp:nparam, :]
    param_energy = jnp.sum(0.125 * (prof_all * prof_all).reshape(ncomp // 8, 8, LANES), axis=0)
    param_energy = param_energy + jnp.sum(
        0.5 * (load_all * load_all).reshape((nparam - ncomp) // 8, 8, LANES), axis=0
    )
    stats_ref[0:8, :] = jnp.where(first_device, param_energy, 0.0)
    sub = lax.broadcasted_iota(jnp.int32, (8, LANES), 0)
    dens = jnp.zeros((8, LANES), F32)
    for b in range(cols // LANES):
        dens = jnp.where(sub == b, -log_dens[:, b * LANES : (b + 1) * LANES], dens)
    stats_ref[8:16, :] = dens
    out[...] = 0.5 * STEP_PARAM * (grad0_ref[...] + grad[...])
    owner = cells_rank == 0
    old_prof, old_load = own_ref[0:mine, :], own_ref[mine : mine + nfac, :]
    base_prof = pmom_ref[...] - 0.5 * STEP_PARAM * 0.25 * (old_prof + new_prof)
    base_load = wmom_ref[...] - 0.5 * STEP_PARAM * (old_load + new_load)
    out[pl.ds(pl.multiple_of(comp_rank * mine, mine), mine), :] += jnp.where(owner, base_prof, 0.0)
    out[pl.ds(pl.multiple_of(ncomp + comp_rank * nfac, nfac), nfac), :] += jnp.where(owner, base_load, 0.0)
    ring, rows, _ = keep_ref.shape
    upper = cells_rank % 2 == 1
    for k in range(ring):
        group = comp_rank ^ k
        start = pl.multiple_of(group * mine, mine)
        low = out[pl.ds(start, rows), :]
        tail = out[pl.ds(pl.multiple_of(ncomp + group * nfac, nfac), nfac), :]
        high = jnp.concatenate([out[pl.ds(start + rows, mine - rows), :], tail], axis=0)
        keep_ref[k] = jnp.where(upper, high, low)
        send_ref[k] = jnp.where(upper, low, high)


def second_field(
    chunk, ring, tiles, rank_ref, tau_ref, new_ref, half_ref, old_ref, land_ref, load_ref, stats_ref, near_ref, far_ref,
    edge_ref, *refs
):
    gap_refs, (mom_ref, energy_ref, prior) = refs[: new_ref.shape[0]], refs[new_ref.shape[0] :]
    comp_rank = rank_ref[1]
    share, nfac, cols = new_ref.shape
    land = land_ref[pl.ds(pl.multiple_of(comp_rank * share, 8), share), :].astype(F32)
    lands = [land[r : r + 1, :] for r in range(share)]
    tau = field_weights(tau_ref, nfac, cols)
    (above, below), (land_above, land_below), (pull_up, pull_down) = edge_terms(
        chunk, ring, tiles, rank_ref, tau, lands, old_ref, near_ref, far_ref, edge_ref
    )
    move = 0.5 * STEP_FIELD * STEP_FIELD
    rows = [above - move * pull_up] + [new_ref[r] for r in range(share)] + [below - move * pull_down]
    energy = load_prior(rows, [land_above] + lands + [land_below], tau, prior)
    prior[0] += pull_up
    prior[share - 1] += pull_down
    field_grads(load_ref, gap_refs, prior)
    for r in range(share):
        fresh = half_ref[r] + 0.5 * STEP_FIELD * prior[r]
        mom_ref[r] = fresh
        energy = energy + 0.5 * (fresh * fresh)
    tiles_sum = stats_ref[0:8, :] + stats_ref[8:16, :]
    for i in range(0, nfac, 8):
        for b in range(0, cols, LANES):
            tiles_sum = tiles_sum + energy[i : i + 8, b : b + LANES]
    energy_ref[...] = tiles_sum


def last_kernel(cells, *refs):
    total = refs[0][...]
    for part in refs[1:-1]:
        total = total + part[...]
    total = jnp.sum(jnp.sum(total, axis=0, keepdims=True), axis=1, keepdims=True)
    refs[-1][...] = total / cells


def fast_device(
    factor_field, profile, mixing, factor_mom, profile_mom, mixing_mom, field_tau, counts, land_mask, log_exposure
):
    nfac, share, cols = factor_field.shape
    mine, ncat = profile.shape
    tile_rows = land_mask.shape[0]
    ring = lax.axis_size("comp")
    tiles = lax.axis_size("cells")
    ncomp = mine * ring
    nparam = ncomp + nfac * ncomp // LANES
    pairs = tiles // 2
    edge = 2 * nfac * cols // LANES + 8
    round_up = lambda rows: -(-rows // (8 * tiles)) * 8
    chunk = round_up(nparam)
    comp_rank = lax.axis_index("comp")
    cells_rank = lax.axis_index("cells")
    ranks = jnp.stack([cells_rank, comp_rank]).astype(jnp.int32)
    pack = lax.optimization_barrier(jnp.pad(profile, ((0, nfac), (0, 0))) + jnp.pad(mixing, ((mine, 0), (0, 0))))
    got, others = gather_params(pack, cells_rank)
    count_rows = lax.dynamic_slice_in_dim(counts, comp_rank * share, share, 1).swapaxes(0, 1).astype(BF16)
    field_rows = factor_field.swapaxes(0, 1)
    mom_rows = factor_mom.swapaxes(0, 1)
    vmem = pl.BlockSpec(memory_space=pltpu.VMEM)
    smem = pl.BlockSpec(memory_space=pltpu.SMEM)
    shape = lambda *dims: jax.ShapeDtypeStruct(dims, F32)
    work = [
        pltpu.VMEM((tiles * chunk, LANES), F32),
        pltpu.VMEM((ncomp, 4 * LANES), BF16),
        pltpu.VMEM((ncomp, LANES), BF16),
        pltpu.VMEM((share, 4 * LANES, cols), BF16),
        pltpu.VMEM((share, 2 * LANES, 2 * cols), BF16),
    ]
    work += [pltpu.VMEM((ncomp, cols), F32)] * 4 + [pltpu.VMEM((ncomp, 2 * cols), BF16)] * 4
    work += [
        pltpu.VMEM((ncomp, 2 * LANES), F32),
        pltpu.VMEM((3 * nfac, ncomp), F32),
    ]
    field_shape = shape(share, nfac, cols)
    chunk_shape = shape(pairs, chunk, LANES)
    half_shape = shape(ring, (mine + nfac) // 2, LANES)
    gap_shapes = [jax.ShapeDtypeStruct((ncomp, 2 * cols), BF16)] * share
    load_shape = jax.ShapeDtypeStruct((2 * nfac, ncomp), BF16)
    field_flops = 2 * 2 * nfac * ncomp * 2 * cols * share
    field_cost = pl.CostEstimate(flops=field_flops, bytes_accessed=4 * share * ncomp * cols, transcendentals=0)

    def call(body, name, smem_count, vmem_count, outs, scratch, cost=None):
        return pl.pallas_call(
            body,
            name=name,
            in_specs=[smem] * smem_count + [vmem] * vmem_count,
            out_specs=[vmem] * len(outs),
            scratch_shapes=scratch,
            out_shape=outs,
            cost_estimate=cost,
            compiler_params=pltpu.CompilerParams(vmem_limit_bytes=40 * 1024 * 1024),
        )

    prior = [pltpu.VMEM((share, nfac, cols), F32)]
    first = call(
        functools.partial(first_kernel, ncomp),
        "first_gradient",
        1,
        9,
        gap_shapes + [load_shape, shape(nparam, LANES), chunk_shape, chunk_shape],
        work + [pltpu.VMEM((mine + nfac, LANES), F32)],
    )
    *gaps, load, grad, keep, send = first(
        ranks, count_rows, field_rows, land_mask, log_exposure, profile_mom, mixing_mom, pack, got, others
    )
    edge_shape = shape(edge, LANES)
    part_field, half, near_edge, far_edge = call(
        first_field, "first_field", 2, 4 + share, [field_shape, field_shape, edge_shape, edge_shape], prior, field_cost
    )(ranks, field_tau, field_rows, mom_rows, land_mask, load, *gaps)
    near, far, got_edge = all_sum(keep, send, near_edge, far_edge)
    second = call(
        functools.partial(second_kernel, ncomp, chunk, ring, tiles),
        "second_gradient",
        2,
        12,
        gap_shapes
        + [
            load_shape,
            field_shape,
            shape(mine + nfac, ncat),
            shape(16, LANES),
            half_shape,
            half_shape,
        ],
        work + [pltpu.VMEM((nparam, LANES), F32)] * 2,
    )
    *gaps, load, new_field, new_params, stats, keep, send = second(
        ranks, field_tau, count_rows, part_field, land_mask, log_exposure, profile_mom, mixing_mom, field_rows, pack, near,
        far, got_edge, grad,
    )
    new_mom, energy = call(
        functools.partial(second_field, chunk, ring, tiles), "second_field", 2, 9 + share, [field_shape, shape(8, LANES)], prior, field_cost
    )(ranks, field_tau, new_field, half, field_rows, land_mask, load, stats, near, far, got_edge, *gaps)
    done = (new_field.swapaxes(0, 1), new_params[:mine], new_params[mine:], new_mom.swapaxes(0, 1))
    momenta, energy, done = group_sum(keep, send, energy, done)
    kinetic = jnp.sum(0.5 * (momenta * momenta).reshape(-1, 8, LANES), axis=0)
    total = energy + kinetic
    parts = [total] + [partner(total, "comp", k) for k in range(1, ring)]
    cells = tile_rows * cols * tiles
    (hamiltonian,) = call(functools.partial(last_kernel, cells), "total_energy", 0, ring, [shape(1, 1)], [])(*parts)
    return (
        *done,
        momenta[:mine],
        momenta[mine:],
        hamiltonian.reshape(()),
    )


def power_of_two(count):
    return count & (count - 1) == 0


def choose_device(*args):
    factor_field, profile, mixing = args[:3]
    nfac, share, cols = factor_field.shape
    mine, ncat = profile.shape
    tiles, ring = lax.axis_size("cells"), lax.axis_size("comp")
    fits = mine == LANES and ncat == LANES and nfac % 16 == 0 and 6 * nfac + EXTRA <= LANES
    fits = fits and (mine + nfac) % 16 == 0 and mine >= nfac and share % 8 == 0 and cols % LANES == 0 and cols <= 8 * LANES
    fits = fits and power_of_two(tiles) and tiles > 1 and ring == 4
    return fast_device(*args) if fits else plain_device(*args)


def solution(mesh):
    in_specs = (
        P(None, ("cells", "comp"), None),
        P("comp", None),
        P(None, "comp"),
        P(None, ("cells", "comp"), None),
        P("comp", None),
        P(None, "comp"),
        P(),
        P(None, "cells", None),
        P("cells", None),
        P("cells", None),
    )
    out_specs = (
        P(None, ("cells", "comp"), None),
        P("comp", None),
        P(None, "comp"),
        P(None, ("cells", "comp"), None),
        P("comp", None),
        P(None, "comp"),
        P(),
    )
    return jax.shard_map(
        choose_device, mesh=mesh, in_specs=in_specs, out_specs=out_specs, check_vma=False
    )
```

```python
import functools
import math

import jax
import jax.numpy as jnp
from jax import lax
from jax.experimental import pallas as pl
from jax.experimental.pallas import tpu as pltpu
from jax.sharding import PartitionSpec as P


def extended(cells, sides, width):
    for axis, dim in sides:
        count = lax.axis_size(axis)
        ends = count - 1
        head = lax.slice_in_dim(cells, 0, width, axis=dim)
        tail = lax.slice_in_dim(cells, cells.shape[dim] - width, cells.shape[dim], axis=dim)
        cells = jnp.concatenate(
            [
                lax.ppermute(tail, axis, [(i, (i + 1) % count) for i in range(ends)]),
                cells,
                lax.ppermute(head, axis, [((i + 1) % count, i) for i in range(ends)]),
            ],
            axis=dim,
        )
    return cells


def field_prior(padded, land_pad, field_tau):
    ridge = 0.1
    step_x = padded[:, 1:, :] - padded[:, :-1, :]
    edge_x = land_pad[1:, :] * land_pad[:-1, :]
    flux_x = edge_x[None, :, :] * step_x
    centre = padded[:, 1:-1, :]
    land_mid = land_pad[1:-1, :]
    step_y = centre[:, :, 1:] - centre[:, :, :-1]
    edge_y = land_mid[:, 1:] * land_mid[:, :-1]
    flux_y = edge_y[None, :, :] * step_y
    lap_x = flux_x[:, :-1, :] - flux_x[:, 1:, :]
    lap_y = jnp.pad(flux_y, ((0, 0), (0, 0), (1, 0))) - jnp.pad(flux_y, ((0, 0), (0, 0), (0, 1)))
    tau_cube = field_tau[:, None, None]
    grad = -tau_cube * (lap_x + lap_y + ridge * centre)
    energy = 0.5 * jnp.sum(tau_cube * (flux_x[:, 1:, :] * step_x[:, 1:, :]))
    energy = energy + 0.5 * jnp.sum(tau_cube * (flux_y * step_y))
    energy = energy + 0.5 * ridge * jnp.sum(tau_cube * (centre * centre))
    return (grad, energy)


def tile_scores(flat_tile, count_rows, exposure, profile, mixing):
    prof_exp = jnp.exp(profile)
    rate_total = jnp.sum(prof_exp, axis=1)
    mix_logit = jnp.dot(mixing.T, flat_tile, precision=lax.Precision.HIGHEST)
    fit_score = (
        jnp.dot(profile, count_rows, precision=lax.Precision.HIGHEST)
        - rate_total[:, None] * exposure[None, :]
    )
    return (mix_logit, mix_logit + fit_score)


def tile_grads(
    flat_tile, count_rows, land_weight, exposure, mixing, mix_logit, joint_score, log_mix, log_joint
):
    prior_share = jnp.exp(mix_logit - log_mix[None, :])
    posterior = jnp.exp(joint_score - log_joint[None, :])
    post_land = posterior * land_weight[None, :]
    gap_weight = (posterior - prior_share) * land_weight[None, :]
    grad_counts = jnp.dot(post_land, count_rows.T, precision=lax.Precision.HIGHEST)
    rate_mass = jnp.sum(post_land * exposure[None, :], axis=1)
    grad_mix = jnp.dot(flat_tile, gap_weight.T, precision=lax.Precision.HIGHEST)
    field_lik = jnp.dot(mixing, gap_weight, precision=lax.Precision.HIGHEST)
    log_dens = jnp.sum(land_weight * (log_joint - log_mix))
    return (grad_counts, rate_mass, grad_mix, field_lik, log_dens)


def log_sum(scores):
    top = jnp.max(scores, axis=0)
    return top + jnp.log(jnp.sum(jnp.exp(scores - top[None, :]), axis=0))


def plain_device(
    factor_field,
    profile,
    mixing,
    factor_mom,
    profile_mom,
    mixing_mom,
    field_tau,
    counts,
    land_mask,
    log_exposure,
):
    step_field = 0.05
    step_profile = 0.002
    step_mixing = 0.002
    tile_rows, tile_cols = land_mask.shape
    ncat = counts.shape[0]
    share_rows = factor_field.shape[1]
    comp_rank = lax.axis_index("comp")
    cells_rank = lax.axis_index("cells")
    first_cells = cells_rank == 0
    land_pad = extended(land_mask, (("cells", 0),), 1).astype(jnp.float32)
    row_start = comp_rank * share_rows
    count_rows = lax.dynamic_slice_in_dim(counts, row_start, share_rows, 1)
    count_rows = count_rows.reshape(ncat, share_rows * tile_cols).astype(jnp.float32)
    land_weight = (
        lax.dynamic_slice_in_dim(land_mask, row_start, share_rows, 0)
        .reshape(-1)
        .astype(jnp.float32)
    )
    exposure = jnp.exp(lax.dynamic_slice_in_dim(log_exposure, row_start, share_rows, 0).reshape(-1))
    land_near = lax.dynamic_slice_in_dim(land_pad, row_start, share_rows + 2, 0)

    def evaluate(share_field, profile_now, mixing_now):
        padded = extended(share_field, ((("cells", "comp"), 1),), 1)
        prior_grad, prior_energy = field_prior(padded, land_near, field_tau)
        profile_all, mixing_all = (
            lax.all_gather(profile_now, "comp", axis=0, tiled=True),
            lax.all_gather(mixing_now, "comp", axis=1, tiled=True),
        )
        flat_tile = share_field.reshape(share_field.shape[0], -1)
        mix_logit, joint_score = tile_scores(
            flat_tile, count_rows, exposure, profile_all, mixing_all
        )
        log_mix = log_sum(mix_logit)
        log_joint = log_sum(joint_score)
        grad_counts, rate_mass, grad_mix, field_lik, log_dens = tile_grads(
            flat_tile,
            count_rows,
            land_weight,
            exposure,
            mixing_all,
            mix_logit,
            joint_score,
            log_mix,
            log_joint,
        )
        grad_counts, rate_mass, mix_rows = (
            lax.psum_scatter(grad_counts, "comp", scatter_dimension=0, tiled=True),
            lax.psum_scatter(rate_mass, "comp", scatter_dimension=0, tiled=True),
            lax.psum_scatter(grad_mix.T, "comp", scatter_dimension=0, tiled=True),
        )
        grad_mix = mix_rows.T
        grad_field = prior_grad + field_lik.reshape(share_field.shape)
        log_part = log_dens - prior_energy
        grad_counts, rate_mass, grad_mix = lax.psum((grad_counts, rate_mass, grad_mix), "cells")
        grad_profile = grad_counts - jnp.exp(profile_now) * rate_mass[:, None] - 0.25 * profile_now
        grad_mixing = grad_mix - mixing_now
        param_prior = -0.125 * jnp.sum(profile_now * profile_now) - 0.5 * jnp.sum(
            mixing_now * mixing_now
        )
        log_part = log_part + jnp.where(first_cells, param_prior, 0.0)
        return (log_part, grad_field, grad_profile, grad_mixing)

    first = evaluate(factor_field, profile, mixing)
    half_field = factor_mom + 0.5 * step_field * first[1]
    half_profile = profile_mom + 0.5 * step_profile * first[2]
    half_mixing = mixing_mom + 0.5 * step_mixing * first[3]
    new_field = factor_field + step_field * half_field
    new_profile = profile + step_profile * half_profile
    new_mixing = mixing + step_mixing * half_mixing
    second = evaluate(new_field, new_profile, new_mixing)
    new_factor_mom = half_field + 0.5 * step_field * second[1]
    new_profile_mom = half_profile + 0.5 * step_profile * second[2]
    new_mixing_mom = half_mixing + 0.5 * step_mixing * second[3]
    kinetic = 0.5 * jnp.sum(new_factor_mom * new_factor_mom)
    kinetic = kinetic + jnp.where(
        first_cells,
        0.5
        * (jnp.sum(new_profile_mom * new_profile_mom) + jnp.sum(new_mixing_mom * new_mixing_mom)),
        0.0,
    )
    log_total, kinetic_total = lax.psum((second[0], kinetic), ("cells", "comp"))
    cell_count = tile_rows * tile_cols * lax.axis_size("cells")
    hamiltonian = (kinetic_total - log_total) / cell_count
    return (
        new_field,
        new_profile,
        new_mixing,
        new_factor_mom,
        new_profile_mom,
        new_mixing_mom,
        hamiltonian,
    )


STEP_FIELD = 0.05
STEP_PARAM = 0.002
RIDGE = 0.1
LOG2E = math.log2(math.e)
LN2 = math.log(2.0)
LANES = 128
EXTRA = 16
F32 = jnp.float32
BF16 = jnp.bfloat16


def pieces(values, count):
    parts = []
    for _ in range(count):
        part = values.astype(BF16)
        parts.append(part)
        values = values - part.astype(F32)
    return parts


def dot(left, right, dims=((1,), (0,))):
    return lax.dot_general(left, right, (dims, ((), ())), preferred_element_type=F32)


def partner(values, axis, flip):
    count = lax.axis_size(axis)
    return lax.ppermute(values, axis, [(i, i ^ flip) for i in range(count)])


def all_sum(keep, send, near_edge, far_edge):
    pairs, rows, _ = keep.shape
    comp_rank, cells_rank = lax.axis_index("comp"), lax.axis_index("cells")
    chip, core = cells_rank // 2, cells_rank % 2
    chunks = keep + partner(send, "cells", 1)
    total = chunks[0]
    for part in [partner(chunks[k], "cells", 2 * k) for k in range(1, pairs)]:
        total = total + part
    first = partner(jnp.concatenate([total, near_edge], axis=0), "comp", 1)
    second = partner(total, "comp", 2)
    third = partner(jnp.concatenate([total, far_edge], axis=0), "comp", 3)
    total = total + first[:rows] + second + third[:rows]
    crossed = third[rows:]
    message = jnp.concatenate([total, crossed], axis=0)
    parts = [partner(message if k & (k + 1) == 0 else total, "cells", 2 * k) for k in range(1, pairs)]
    near = jnp.concatenate([total] + [part[:rows] for part in parts], axis=0)
    neighbour = chip ^ jnp.where(core == 0, chip + 1, chip - 1)
    passed = crossed
    for k in range(1, pairs):
        if k & (k + 1) == 0:
            passed = jnp.where(neighbour == k, parts[k - 1][rows:], passed)
    passed = jnp.where((comp_rank == 0) == (core == 0), crossed, passed)
    far = partner(jnp.concatenate([near, passed], axis=0), "cells", 1)
    at_end = (comp_rank == 0) | (comp_rank == lax.axis_size("comp") - 1)
    return near, far, first[rows:], jnp.where(at_end, far[pairs * rows :], crossed)


def group_sum(keep, send, energy, beside):
    ring, rows, _ = keep.shape
    pairs = lax.axis_size("cells") // 2
    halves = keep + partner(send, "cells", 1)
    total = halves[0]
    for part in [partner(halves[k], "comp", k) for k in range(1, ring)]:
        total = total + part
    total, beside = lax.optimization_barrier((total, beside))
    total = jnp.concatenate([total, energy], axis=0)
    for part in [partner(total, "cells", 2 * k) for k in range(1, pairs)]:
        total = total + part
    other = partner(total, "cells", 1)
    upper = lax.axis_index("cells") % 2 == 1
    low = jnp.where(upper, other, total)[:rows]
    high = jnp.where(upper, total, other)[:rows]
    return jnp.concatenate([low, high], axis=0), total[rows:] + other[rows:], beside


def gather_params(pack, cells_rank):
    tiles, ring = lax.axis_size("cells"), lax.axis_size("comp")
    rows = pack.shape[0]
    spread = [(c * ring + z, c * ring + (z ^ (1 + c % 2))) for c in range(tiles) for z in range(ring)]
    one = lax.ppermute(pack, ("cells", "comp"), spread)
    half = lax.dynamic_slice_in_dim(pack, cells_rank % 2 * (rows // 2), rows // 2, 0)
    got = jnp.concatenate([one, partner(half, "comp", 3)], axis=0)
    return got, partner(got, "cells", 1)


def chunk_index(cells_rank, k, other):
    core = cells_rank % 2
    return (((cells_rank // 2) ^ k) * 2) + (1 - core if other else core)


def gather_chunks(flat_ref, near_ref, far_ref, cells_rank, rows):
    for k in range(near_ref.shape[0] // rows):
        for source, other in ((near_ref, False), (far_ref, True)):
            start = pl.multiple_of(chunk_index(cells_rank, k, other) * rows, 8)
            flat_ref[pl.ds(start, rows), :] = source[k * rows : (k + 1) * rows, :]


def spread_chunks(flat_ref, keep_ref, send_ref, cells_rank):
    pairs, rows, _ = keep_ref.shape
    for k in range(pairs):
        for target, other in ((keep_ref, False), (send_ref, True)):
            start = pl.multiple_of(chunk_index(cells_rank, k, other) * rows, 8)
            target[k] = flat_ref[pl.ds(start, rows), :]


def load_params(flat_ref, left_ref, mix_ref, load_ref, ncomp, nfac):
    lane = lax.broadcasted_iota(jnp.int32, (LANES, LANES), 1)
    spare = jnp.zeros((LANES - EXTRA - 6 * nfac, LANES), F32)
    for q in range(ncomp // LANES):
        rows = pl.ds(q * LANES, LANES)
        prof = flat_ref[rows, :]
        high, mid, low = pieces(prof * LOG2E, 3)
        left_ref[rows, 0:LANES] = high
        left_ref[rows, 2 * LANES : 3 * LANES] = mid
        left_ref[rows, 3 * LANES : 4 * LANES] = low
        rate = jnp.sum(jnp.exp(prof), axis=1, keepdims=True) * LOG2E
        rate_high, rate_mid, rate_low = [part.astype(F32) for part in pieces(rate, 3)]
        load = flat_ref[pl.ds(ncomp + q * nfac, nfac), :]
        w_high, w_mid, w_low = [part.astype(F32) for part in pieces(load * LOG2E, 3)]
        stack = jnp.concatenate(
            [jnp.zeros((EXTRA, LANES), F32), w_high, w_high, w_high, w_mid, w_mid, w_low, spare], axis=0
        )
        turned = stack.T
        mix_ref[rows, :] = turned.astype(BF16)
        rate_part = jnp.where(
            lane < 3, rate_high, jnp.where(lane < 5, rate_mid, jnp.where(lane == 5, rate_low, 0.0))
        )
        left_ref[rows, LANES : 2 * LANES] = (turned - rate_part).astype(BF16)
        load_high, load_mid = pieces(load, 2)
        load_ref[0:nfac, q * LANES : (q + 1) * LANES] = load_high
        load_ref[nfac : 2 * nfac, q * LANES : (q + 1) * LANES] = load_mid


def load_cells(counts_ref, field_ref, log_exposure, right_ref, wide_ref):
    share, ncat, cols = counts_ref.shape
    nfac = field_ref.shape[1]
    exposure = jnp.exp(log_exposure)
    sub = lax.broadcasted_iota(jnp.int32, (EXTRA, cols), 0)
    spare = jnp.zeros((LANES - EXTRA - 6 * nfac, cols), BF16)
    for r in range(share):
        count = counts_ref[r]
        high, mid, low = pieces(field_ref[r], 3)
        e_high, e_mid, e_low = [part.astype(F32) for part in pieces(exposure[r : r + 1, :], 3)]
        e_rows = jnp.where((sub == 0) | (sub == 3) | (sub == 5), e_high, 0.0)
        e_rows = jnp.where((sub == 1) | (sub == 4), e_mid, e_rows)
        e_rows = jnp.where(sub == 2, e_low, e_rows).astype(BF16)
        extra = jnp.concatenate([e_rows, high, mid, low, high, mid, high, spare], axis=0)
        right_ref[r, 0:ncat, :] = count
        right_ref[r, LANES : 2 * LANES, :] = extra
        right_ref[r, 2 * LANES : 2 * LANES + ncat, :] = count
        right_ref[r, 3 * LANES : 3 * LANES + ncat, :] = count
        for side in range(2):
            wide_ref[r, 0:ncat, side * cols : (side + 1) * cols] = count
            wide_ref[r, LANES : 2 * LANES, side * cols : (side + 1) * cols] = extra


def field_weights(tau_ref, nfac, cols):
    row = lax.broadcasted_iota(jnp.int32, (nfac, cols), 0)
    tau = jnp.zeros((nfac, cols), F32)
    for j in range(nfac):
        tau = jnp.where(row == j, tau_ref[j], tau)
    return tau


def load_prior(rows, lands, tau, prior_ref):
    nfac, cols = tau.shape
    inner = lax.broadcasted_iota(jnp.int32, (nfac, cols), 1) < cols - 1
    energy = jnp.zeros((nfac, cols), F32)
    lands = [jnp.broadcast_to(x, (nfac, cols)) for x in lands]
    for r in range(len(rows) - 2):
        here = rows[r + 1]
        step_right = here - pltpu.roll(here, cols - 1, 1)
        edge_right = jnp.where(inner, lands[r + 1] * pltpu.roll(lands[r + 1], cols - 1, 1), 0.0)
        flux_right = edge_right * step_right
        laplace = flux_right - pltpu.roll(flux_right, 1, 1)
        parts = flux_right * step_right + RIDGE * (here * here)
        if rows[r] is not None:
            laplace = laplace + lands[r] * lands[r + 1] * (here - rows[r])
        if rows[r + 2] is not None:
            step_down = here - rows[r + 2]
            flux_down = lands[r + 1] * lands[r + 2] * step_down
            laplace = laplace + flux_down
            parts = parts + flux_down * step_down
        prior_ref[r] = -tau * (laplace + RIDGE * here)
        energy = energy + 0.5 * tau * parts
    return energy


def pack_edge(edge_ref, field, fresh, land):
    nfac, cols = field.shape
    blocks = cols // LANES
    sub = lax.broadcasted_iota(jnp.int32, (8, LANES), 0)
    lands = jnp.zeros((8, LANES), F32)
    for b in range(blocks):
        lanes = slice(b * LANES, (b + 1) * LANES)
        edge_ref[b * nfac : (b + 1) * nfac, :] = field[:, lanes]
        edge_ref[(blocks + b) * nfac : (blocks + b + 1) * nfac, :] = fresh[:, lanes]
        lands = jnp.where(sub == b, land[:, lanes], lands)
    edge_ref[2 * blocks * nfac :, :] = lands


def unpack_edge(edge, nfac, cols):
    blocks = cols // LANES
    wide = lambda start, size, step: jnp.concatenate(
        [edge[start + b * step : start + b * step + size, :] for b in range(blocks)], axis=1
    )
    return wide(0, nfac, nfac), wide(blocks * nfac, nfac, nfac), wide(2 * blocks * nfac, 1, 1)


def row_scores(r, right_ref, left_ref, mix_ref, score_ref, logit_ref):
    tops = []
    for target, values in (
        (score_ref, dot(left_ref[...], right_ref[r])),
        (logit_ref, dot(mix_ref[...], right_ref[r, LANES : 2 * LANES, :])),
    ):
        target[...] = values
        ncomp, cols = values.shape
        tops.append(jnp.max(jnp.max(values.reshape(ncomp // 8, 8, cols), axis=0), axis=0, keepdims=True))
    return tops


def row_shares(tops, land, score_ref, logit_ref, post_ref, gap_ref, kept_ref):
    ncomp, cols = score_ref.shape
    block = 32
    top_s, top_a = tops
    sum_s = jnp.zeros((8, cols), F32)
    sum_a = jnp.zeros((8, cols), F32)
    for i in range(0, ncomp, block):
        part_s = jnp.exp2(score_ref[i : i + block, :] - top_s)
        part_a = jnp.exp2(logit_ref[i : i + block, :] - top_a)
        score_ref[i : i + block, :] = part_s
        logit_ref[i : i + block, :] = part_a
        sum_s = sum_s + jnp.sum(part_s.reshape(block // 8, 8, cols), axis=0)
        sum_a = sum_a + jnp.sum(part_a.reshape(block // 8, 8, cols), axis=0)
    sum_s = jnp.sum(sum_s, axis=0, keepdims=True)
    sum_a = jnp.sum(sum_a, axis=0, keepdims=True)
    log_s = top_s + jnp.log2(sum_s)
    log_a = top_a + jnp.log2(sum_a)
    inv_s = land / sum_s
    inv_a = land / sum_a
    for i in range(0, ncomp, block):
        post = score_ref[i : i + block, :] * inv_s
        gap = post - logit_ref[i : i + block, :] * inv_a
        for targets, values in (((post_ref,), post), ((gap_ref, kept_ref), gap)):
            high, low = pieces(values, 2)
            for target in targets:
                target[i : i + block, 0:cols] = high
                target[i : i + block, cols : 2 * cols] = low
    return land * (LN2 * (log_s - log_a))


def row_products(r, wide_ref, post_ref, gap_ref, acc_ref, accw_ref):
    nfac = accw_ref.shape[0] // 3
    last = ((1,), (1,))
    start = LANES + EXTRA
    acc = dot(post_ref[...], wide_ref[r], last)
    accw = dot(wide_ref[r, start : start + 3 * nfac, :], gap_ref[...], last)
    if r == 0:
        acc_ref[...] = acc
        accw_ref[...] = accw
    else:
        acc_ref[...] += acc
        accw_ref[...] += accw


def field_grads(load_ref, gap_refs, prior_ref):
    share, nfac, cols = prior_ref.shape
    for r in range(share):
        lik = dot(load_ref[...], gap_refs[r][...])
        lik = lik[0:nfac] + lik[nfac : 2 * nfac]
        prior_ref[r] += lik[:, 0:cols] + lik[:, cols : 2 * cols]


def all_rows(land, right, wide, left, mix, scores, logits, posts, gaps, kept, acc, accw):
    share, _, cols = right.shape
    log_dens = jnp.zeros((1, cols), F32)
    tops = {}
    for r in range(share + 2):
        if r < share:
            tops[r] = row_scores(r, right, left, mix, scores[r % 2], logits[r % 2])
        if 0 <= r - 1 < share:
            p = r - 1
            log_dens = log_dens + row_shares(
                tops[p], land[p : p + 1, :], scores[p % 2], logits[p % 2], posts[p % 2], gaps[p % 2], kept[p]
            )
        if 0 <= r - 2:
            p = r - 2
            row_products(p, wide, posts[p % 2], gaps[p % 2], acc, accw)
    return log_dens


def param_grads(flat_ref, acc_ref, accw_ref, grad_ref, ncomp, nfac, flip=0):
    lane = lax.broadcasted_iota(jnp.int32, (LANES, LANES), 1)
    for q in range(ncomp // LANES):
        rows = pl.ds(q * LANES, LANES)
        lanes = slice(q * LANES, (q + 1) * LANES)
        mass = jnp.sum(jnp.where(lane < 3, acc_ref[rows, LANES : 2 * LANES], 0.0), axis=1, keepdims=True)
        group = flip ^ q
        grad_ref[pl.ds(pl.multiple_of(group * LANES, LANES), LANES), :] = acc_ref[rows, 0:LANES] - jnp.exp(flat_ref[rows, :]) * mass
        load = accw_ref[:, lanes]
        grad_ref[pl.ds(pl.multiple_of(ncomp + group * nfac, nfac), nfac), :] = load[0:nfac] + load[nfac : 2 * nfac] + load[2 * nfac : 3 * nfac]


def first_kernel(
    ncomp, rank_ref, counts_ref, field_ref, land_ref, logexp_ref, pmom_ref, wmom_ref, pack_ref, got_ref, others_ref, *refs
):
    gaps, refs = refs[: counts_ref.shape[0]], refs[counts_ref.shape[0] :]
    load, grad_ref, keep_ref, send_ref, flat, left, mix, right, wide, score0, score1, logit0, logit1, *refs = refs
    post0, post1, gap0, gap1, acc, accw = refs
    cells_rank, comp_rank = rank_ref[0], rank_ref[1]
    share, nfac, cols = field_ref.shape
    mine = pmom_ref.shape[0]
    size = mine + nfac
    middle = size // 2
    swap = cells_rank % 2 == 1
    lower, upper = got_ref[...], others_ref[...]
    one, two = jnp.where(swap, upper, lower), jnp.where(swap, lower, upper)
    three = jnp.concatenate([one[size : size + middle], two[size : size + middle]], axis=0)
    for k, source in enumerate((pack_ref[...], one, two, three)):
        flat[k * mine : (k + 1) * mine, :] = source[0:mine]
        flat[ncomp + k * nfac : ncomp + (k + 1) * nfac, :] = source[mine:size]
    here = pl.ds(pl.multiple_of(comp_rank * share, 8), share)
    land = land_ref[here, :].astype(F32)
    load_params(flat, left, mix, load, ncomp, nfac)
    load_cells(counts_ref, field_ref, logexp_ref[here, :], right, wide)
    all_rows(land, right, wide, left, mix, (score0, score1), (logit0, logit1), (post0, post1), (gap0, gap1), gaps, acc, accw)
    param_grads(flat, acc, accw, grad_ref, ncomp, nfac, comp_rank)
    nparam = grad_ref.shape[0]
    if flat.shape[0] > nparam:
        flat[nparam:, :] = jnp.zeros((flat.shape[0] - nparam, LANES), F32)
    flat[0:nparam, :] = 0.5 * STEP_PARAM * STEP_PARAM * grad_ref[...]
    own_prof, own_load = pack_ref[0:mine, :], pack_ref[mine:size, :]
    owner = cells_rank == 0
    base_prof = own_prof + STEP_PARAM * (pmom_ref[...] - 0.5 * STEP_PARAM * 0.25 * own_prof)
    base_load = own_load + STEP_PARAM * (wmom_ref[...] - 0.5 * STEP_PARAM * own_load)
    flat[pl.ds(pl.multiple_of(comp_rank * mine, mine), mine), :] += jnp.where(owner, base_prof, 0.0)
    flat[pl.ds(pl.multiple_of(ncomp + comp_rank * nfac, nfac), nfac), :] += jnp.where(owner, base_load, 0.0)
    spread_chunks(flat, keep_ref, send_ref, cells_rank)


def first_field(rank_ref, tau_ref, field_ref, mom_ref, land_ref, load_ref, *refs):
    gap_refs, refs = refs[: field_ref.shape[0]], refs[field_ref.shape[0] :]
    new_ref, half_ref, near_ref, far_ref, prior = refs
    comp_rank = rank_ref[1]
    share, nfac, cols = field_ref.shape
    land = land_ref[pl.ds(pl.multiple_of(comp_rank * share, 8), share), :].astype(F32)
    lands = [land[r : r + 1, :] for r in range(share)]
    tau = field_weights(tau_ref, nfac, cols)
    load_prior([None] + [field_ref[r] for r in range(share)] + [None], lands[:1] + lands + lands[-1:], tau, prior)
    field_grads(load_ref, gap_refs, prior)
    for r in range(share):
        half = mom_ref[r] + 0.5 * STEP_FIELD * prior[r]
        half_ref[r] = half
        new_ref[r] = field_ref[r] + STEP_FIELD * half
    even = comp_rank % 2 == 0
    end = share - 1
    for target, flag in ((near_ref, even), (far_ref, jnp.logical_not(even))):
        pack_edge(
            target,
            jnp.where(flag, field_ref[end], field_ref[0]),
            jnp.where(flag, new_ref[end], new_ref[0]),
            jnp.where(flag, lands[end], lands[0]),
        )


def edge_terms(ring, tiles, rank_ref, tau, lands, old_ref, edge_ref, other_ref):
    cells_rank, comp_rank = rank_ref[0], rank_ref[1]
    nfac, cols = tau.shape
    even = comp_rank % 2 == 0
    direct, relay = edge_ref[...], other_ref[...]
    above = unpack_edge(jnp.where(even, relay, direct), nfac, cols)
    below = unpack_edge(jnp.where(even, direct, relay), nfac, cols)
    land_above = jnp.where((comp_rank == 0) & (cells_rank == 0), 0.0, above[2])
    land_below = jnp.where((comp_rank == ring - 1) & (cells_rank == tiles - 1), 0.0, below[2])
    pull_up = -tau * (land_above * lands[0]) * (old_ref[0] - above[0])
    pull_down = -tau * (land_below * lands[-1]) * (old_ref[old_ref.shape[0] - 1] - below[0])
    return (above[1], below[1]), (land_above, land_below), (pull_up, pull_down)


def second_kernel(
    ncomp, chunk, ring, tiles, rank_ref, tau_ref, counts_ref, field_ref, land_ref, logexp_ref, pmom_ref, wmom_ref, old_ref,
    own_ref, near_ref, far_ref, edge_ref, other_ref, grad0_ref, *refs
):
    gaps, refs = refs[: counts_ref.shape[0]], refs[counts_ref.shape[0] :]
    load, new_ref, params_ref, stats_ref, keep_ref, send_ref, flat, left, mix, right, wide, *refs = refs
    score0, score1, logit0, logit1, post0, post1, gap0, gap1, acc, accw, out, grad = refs
    cells_rank, comp_rank = rank_ref[0], rank_ref[1]
    share, nfac, cols = field_ref.shape
    mine = pmom_ref.shape[0]
    nparam = grad0_ref.shape[0]
    gather_chunks(flat, near_ref, far_ref, cells_rank, chunk)
    new_prof = flat[pl.ds(pl.multiple_of(comp_rank * mine, mine), mine), :]
    new_load = flat[pl.ds(pl.multiple_of(ncomp + comp_rank * nfac, nfac), nfac), :]
    params_ref[0:mine, :] = new_prof
    params_ref[mine:, :] = new_load
    here = pl.ds(pl.multiple_of(comp_rank * share, 8), share)
    land = land_ref[here, :].astype(F32)
    lands = [land[r : r + 1, :] for r in range(share)]
    tau = field_weights(tau_ref, nfac, cols)
    _, _, pulls = edge_terms(ring, tiles, rank_ref, tau, lands, old_ref, edge_ref, other_ref)
    move = 0.5 * STEP_FIELD * STEP_FIELD
    for r in range(share):
        fresh = field_ref[r]
        if r == 0:
            fresh = fresh + move * pulls[0]
        if r == share - 1:
            fresh = fresh + move * pulls[1]
        new_ref[r] = fresh
    load_params(flat, left, mix, load, ncomp, nfac)
    load_cells(counts_ref, new_ref, logexp_ref[here, :], right, wide)
    log_dens = all_rows(land, right, wide, left, mix, (score0, score1), (logit0, logit1), (post0, post1), (gap0, gap1), gaps, acc, accw)
    param_grads(flat, acc, accw, grad, ncomp, nfac)
    first_device = (cells_rank == 0) & (comp_rank == 0)
    prof_all = flat[0:ncomp, :]
    load_all = flat[ncomp:nparam, :]
    param_energy = jnp.sum(0.125 * (prof_all * prof_all).reshape(ncomp // 8, 8, LANES), axis=0)
    param_energy = param_energy + jnp.sum(
        0.5 * (load_all * load_all).reshape((nparam - ncomp) // 8, 8, LANES), axis=0
    )
    stats_ref[0:8, :] = jnp.where(first_device, param_energy, 0.0)
    sub = lax.broadcasted_iota(jnp.int32, (8, LANES), 0)
    dens = jnp.zeros((8, LANES), F32)
    for b in range(cols // LANES):
        dens = jnp.where(sub == b, -log_dens[:, b * LANES : (b + 1) * LANES], dens)
    stats_ref[8:16, :] = dens
    out[...] = 0.5 * STEP_PARAM * (grad0_ref[...] + grad[...])
    owner = cells_rank == 0
    old_prof, old_load = own_ref[0:mine, :], own_ref[mine : mine + nfac, :]
    base_prof = pmom_ref[...] - 0.5 * STEP_PARAM * 0.25 * (old_prof + new_prof)
    base_load = wmom_ref[...] - 0.5 * STEP_PARAM * (old_load + new_load)
    out[pl.ds(pl.multiple_of(comp_rank * mine, mine), mine), :] += jnp.where(owner, base_prof, 0.0)
    out[pl.ds(pl.multiple_of(ncomp + comp_rank * nfac, nfac), nfac), :] += jnp.where(owner, base_load, 0.0)
    ring, rows, _ = keep_ref.shape
    upper = cells_rank % 2 == 1
    for k in range(ring):
        group = comp_rank ^ k
        start = pl.multiple_of(group * mine, mine)
        low = out[pl.ds(start, rows), :]
        tail = out[pl.ds(pl.multiple_of(ncomp + group * nfac, nfac), nfac), :]
        high = jnp.concatenate([out[pl.ds(start + rows, mine - rows), :], tail], axis=0)
        keep_ref[k] = jnp.where(upper, high, low)
        send_ref[k] = jnp.where(upper, low, high)


def second_field(
    ring, tiles, rank_ref, tau_ref, new_ref, half_ref, old_ref, land_ref, load_ref, stats_ref, edge_ref, other_ref, *refs
):
    gap_refs, (mom_ref, energy_ref, prior) = refs[: new_ref.shape[0]], refs[new_ref.shape[0] :]
    comp_rank = rank_ref[1]
    share, nfac, cols = new_ref.shape
    land = land_ref[pl.ds(pl.multiple_of(comp_rank * share, 8), share), :].astype(F32)
    lands = [land[r : r + 1, :] for r in range(share)]
    tau = field_weights(tau_ref, nfac, cols)
    (above, below), (land_above, land_below), (pull_up, pull_down) = edge_terms(
        ring, tiles, rank_ref, tau, lands, old_ref, edge_ref, other_ref
    )
    move = 0.5 * STEP_FIELD * STEP_FIELD
    rows = [above - move * pull_up] + [new_ref[r] for r in range(share)] + [below - move * pull_down]
    energy = load_prior(rows, [land_above] + lands + [land_below], tau, prior)
    prior[0] += pull_up
    prior[share - 1] += pull_down
    field_grads(load_ref, gap_refs, prior)
    for r in range(share):
        fresh = half_ref[r] + 0.5 * STEP_FIELD * prior[r]
        mom_ref[r] = fresh
        energy = energy + 0.5 * (fresh * fresh)
    tiles_sum = stats_ref[0:8, :] + stats_ref[8:16, :]
    for i in range(0, nfac, 8):
        for b in range(0, cols, LANES):
            tiles_sum = tiles_sum + energy[i : i + 8, b : b + LANES]
    energy_ref[...] = tiles_sum


def last_kernel(cells, *refs):
    total = refs[0][...]
    for part in refs[1:-1]:
        total = total + part[...]
    total = jnp.sum(jnp.sum(total, axis=0, keepdims=True), axis=1, keepdims=True)
    refs[-1][...] = total / cells


def fast_device(
    factor_field, profile, mixing, factor_mom, profile_mom, mixing_mom, field_tau, counts, land_mask, log_exposure
):
    nfac, share, cols = factor_field.shape
    mine, ncat = profile.shape
    tile_rows = land_mask.shape[0]
    ring = lax.axis_size("comp")
    tiles = lax.axis_size("cells")
    ncomp = mine * ring
    nparam = ncomp + nfac * ncomp // LANES
    pairs = tiles // 2
    edge = 2 * nfac * cols // LANES + 8
    round_up = lambda rows: -(-rows // (8 * tiles)) * 8
    chunk = round_up(nparam)
    comp_rank = lax.axis_index("comp")
    cells_rank = lax.axis_index("cells")
    ranks = jnp.stack([cells_rank, comp_rank]).astype(jnp.int32)
    pack = lax.optimization_barrier(jnp.pad(profile, ((0, nfac), (0, 0))) + jnp.pad(mixing, ((mine, 0), (0, 0))))
    got, others = gather_params(pack, cells_rank)
    count_rows = lax.dynamic_slice_in_dim(counts, comp_rank * share, share, 1).swapaxes(0, 1).astype(BF16)
    field_rows = factor_field.swapaxes(0, 1)
    mom_rows = factor_mom.swapaxes(0, 1)
    vmem = pl.BlockSpec(memory_space=pltpu.VMEM)
    smem = pl.BlockSpec(memory_space=pltpu.SMEM)
    shape = lambda *dims: jax.ShapeDtypeStruct(dims, F32)
    work = [
        pltpu.VMEM((tiles * chunk, LANES), F32),
        pltpu.VMEM((ncomp, 4 * LANES), BF16),
        pltpu.VMEM((ncomp, LANES), BF16),
        pltpu.VMEM((share, 4 * LANES, cols), BF16),
        pltpu.VMEM((share, 2 * LANES, 2 * cols), BF16),
    ]
    work += [pltpu.VMEM((ncomp, cols), F32)] * 4 + [pltpu.VMEM((ncomp, 2 * cols), BF16)] * 4
    work += [
        pltpu.VMEM((ncomp, 2 * LANES), F32),
        pltpu.VMEM((3 * nfac, ncomp), F32),
    ]
    field_shape = shape(share, nfac, cols)
    chunk_shape = shape(pairs, chunk, LANES)
    half_shape = shape(ring, (mine + nfac) // 2, LANES)
    gap_shapes = [jax.ShapeDtypeStruct((ncomp, 2 * cols), BF16)] * share
    load_shape = jax.ShapeDtypeStruct((2 * nfac, ncomp), BF16)
    field_flops = 2 * 2 * nfac * ncomp * 2 * cols * share
    field_cost = pl.CostEstimate(flops=field_flops, bytes_accessed=4 * share * ncomp * cols, transcendentals=0)

    def call(body, name, smem_count, vmem_count, outs, scratch, cost=None):
        return pl.pallas_call(
            body,
            name=name,
            in_specs=[smem] * smem_count + [vmem] * vmem_count,
            out_specs=[vmem] * len(outs),
            scratch_shapes=scratch,
            out_shape=outs,
            cost_estimate=cost,
            compiler_params=pltpu.CompilerParams(vmem_limit_bytes=40 * 1024 * 1024),
        )

    prior = [pltpu.VMEM((share, nfac, cols), F32)]
    first = call(
        functools.partial(first_kernel, ncomp),
        "first_gradient",
        1,
        9,
        gap_shapes + [load_shape, shape(nparam, LANES), chunk_shape, chunk_shape],
        work,
    )
    *gaps, load, grad, keep, send = first(
        ranks, count_rows, field_rows, land_mask, log_exposure, profile_mom, mixing_mom, pack, got, others
    )
    edge_shape = shape(edge, LANES)
    part_field, half, near_edge, far_edge = call(
        first_field, "first_field", 2, 4 + share, [field_shape, field_shape, edge_shape, edge_shape], prior, field_cost
    )(ranks, field_tau, field_rows, mom_rows, land_mask, load, *gaps)
    near, far, *edges = all_sum(keep, send, near_edge, far_edge)
    second = call(
        functools.partial(second_kernel, ncomp, chunk, ring, tiles),
        "second_gradient",
        2,
        13,
        gap_shapes
        + [
            load_shape,
            field_shape,
            shape(mine + nfac, ncat),
            shape(16, LANES),
            half_shape,
            half_shape,
        ],
        work + [pltpu.VMEM((nparam, LANES), F32)] * 2,
    )
    *gaps, load, new_field, new_params, stats, keep, send = second(
        ranks, field_tau, count_rows, part_field, land_mask, log_exposure, profile_mom, mixing_mom, field_rows, pack, near,
        far, *edges, grad,
    )
    new_mom, energy = call(
        functools.partial(second_field, ring, tiles), "second_field", 2, 8 + share, [field_shape, shape(8, LANES)], prior, field_cost
    )(ranks, field_tau, new_field, half, field_rows, land_mask, load, stats, *edges, *gaps)
    done = (new_field.swapaxes(0, 1), new_params[:mine], new_params[mine:], new_mom.swapaxes(0, 1))
    momenta, energy, done = group_sum(keep, send, energy, done)
    kinetic = jnp.sum(0.5 * (momenta * momenta).reshape(-1, 8, LANES), axis=0)
    total = energy + kinetic
    parts = [total] + [partner(total, "comp", k) for k in range(1, ring)]
    cells = tile_rows * cols * tiles
    (hamiltonian,) = call(functools.partial(last_kernel, cells), "total_energy", 0, ring, [shape(1, 1)], [])(*parts)
    return (
        *done,
        momenta[:mine],
        momenta[mine:],
        hamiltonian.reshape(()),
    )


def power_of_two(count):
    return count & (count - 1) == 0


def choose_device(*args):
    factor_field, profile, mixing = args[:3]
    nfac, share, cols = factor_field.shape
    mine, ncat = profile.shape
    tiles, ring = lax.axis_size("cells"), lax.axis_size("comp")
    fits = mine == LANES and ncat == LANES and nfac % 16 == 0 and 6 * nfac + EXTRA <= LANES
    fits = fits and (mine + nfac) % 16 == 0 and mine >= nfac and share % 8 == 0 and cols % LANES == 0 and cols <= 8 * LANES
    fits = fits and power_of_two(tiles) and tiles > 1 and ring == 4
    return fast_device(*args) if fits else plain_device(*args)


def solution(mesh):
    in_specs = (
        P(None, ("cells", "comp"), None),
        P("comp", None),
        P(None, "comp"),
        P(None, ("cells", "comp"), None),
        P("comp", None),
        P(None, "comp"),
        P(),
        P(None, "cells", None),
        P("cells", None),
        P("cells", None),
    )
    out_specs = (
        P(None, ("cells", "comp"), None),
        P("comp", None),
        P(None, "comp"),
        P(None, ("cells", "comp"), None),
        P("comp", None),
        P(None, "comp"),
        P(),
    )
    return jax.shard_map(
        choose_device, mesh=mesh, in_specs=in_specs, out_specs=out_specs, check_vma=False
    )
```

```python
import functools
import math

import jax
import jax.numpy as jnp
from jax import lax
from jax.experimental import pallas as pl
from jax.experimental.pallas import tpu as pltpu
from jax.sharding import PartitionSpec as P


def extended(cells, sides, width):
    for axis, dim in sides:
        count = lax.axis_size(axis)
        ends = count - 1
        head = lax.slice_in_dim(cells, 0, width, axis=dim)
        tail = lax.slice_in_dim(cells, cells.shape[dim] - width, cells.shape[dim], axis=dim)
        cells = jnp.concatenate(
            [
                lax.ppermute(tail, axis, [(i, (i + 1) % count) for i in range(ends)]),
                cells,
                lax.ppermute(head, axis, [((i + 1) % count, i) for i in range(ends)]),
            ],
            axis=dim,
        )
    return cells


def field_prior(padded, land_pad, field_tau):
    ridge = 0.1
    step_x = padded[:, 1:, :] - padded[:, :-1, :]
    edge_x = land_pad[1:, :] * land_pad[:-1, :]
    flux_x = edge_x[None, :, :] * step_x
    centre = padded[:, 1:-1, :]
    land_mid = land_pad[1:-1, :]
    step_y = centre[:, :, 1:] - centre[:, :, :-1]
    edge_y = land_mid[:, 1:] * land_mid[:, :-1]
    flux_y = edge_y[None, :, :] * step_y
    lap_x = flux_x[:, :-1, :] - flux_x[:, 1:, :]
    lap_y = jnp.pad(flux_y, ((0, 0), (0, 0), (1, 0))) - jnp.pad(flux_y, ((0, 0), (0, 0), (0, 1)))
    tau_cube = field_tau[:, None, None]
    grad = -tau_cube * (lap_x + lap_y + ridge * centre)
    energy = 0.5 * jnp.sum(tau_cube * (flux_x[:, 1:, :] * step_x[:, 1:, :]))
    energy = energy + 0.5 * jnp.sum(tau_cube * (flux_y * step_y))
    energy = energy + 0.5 * ridge * jnp.sum(tau_cube * (centre * centre))
    return (grad, energy)


def tile_scores(flat_tile, count_rows, exposure, profile, mixing):
    prof_exp = jnp.exp(profile)
    rate_total = jnp.sum(prof_exp, axis=1)
    mix_logit = jnp.dot(mixing.T, flat_tile, precision=lax.Precision.HIGHEST)
    fit_score = (
        jnp.dot(profile, count_rows, precision=lax.Precision.HIGHEST)
        - rate_total[:, None] * exposure[None, :]
    )
    return (mix_logit, mix_logit + fit_score)


def tile_grads(
    flat_tile, count_rows, land_weight, exposure, mixing, mix_logit, joint_score, log_mix, log_joint
):
    prior_share = jnp.exp(mix_logit - log_mix[None, :])
    posterior = jnp.exp(joint_score - log_joint[None, :])
    post_land = posterior * land_weight[None, :]
    gap_weight = (posterior - prior_share) * land_weight[None, :]
    grad_counts = jnp.dot(post_land, count_rows.T, precision=lax.Precision.HIGHEST)
    rate_mass = jnp.sum(post_land * exposure[None, :], axis=1)
    grad_mix = jnp.dot(flat_tile, gap_weight.T, precision=lax.Precision.HIGHEST)
    field_lik = jnp.dot(mixing, gap_weight, precision=lax.Precision.HIGHEST)
    log_dens = jnp.sum(land_weight * (log_joint - log_mix))
    return (grad_counts, rate_mass, grad_mix, field_lik, log_dens)


def log_sum(scores):
    top = jnp.max(scores, axis=0)
    return top + jnp.log(jnp.sum(jnp.exp(scores - top[None, :]), axis=0))


def plain_device(
    factor_field,
    profile,
    mixing,
    factor_mom,
    profile_mom,
    mixing_mom,
    field_tau,
    counts,
    land_mask,
    log_exposure,
):
    step_field = 0.05
    step_profile = 0.002
    step_mixing = 0.002
    tile_rows, tile_cols = land_mask.shape
    ncat = counts.shape[0]
    share_rows = factor_field.shape[1]
    comp_rank = lax.axis_index("comp")
    cells_rank = lax.axis_index("cells")
    first_cells = cells_rank == 0
    land_pad = extended(land_mask, (("cells", 0),), 1).astype(jnp.float32)
    row_start = comp_rank * share_rows
    count_rows = lax.dynamic_slice_in_dim(counts, row_start, share_rows, 1)
    count_rows = count_rows.reshape(ncat, share_rows * tile_cols).astype(jnp.float32)
    land_weight = (
        lax.dynamic_slice_in_dim(land_mask, row_start, share_rows, 0)
        .reshape(-1)
        .astype(jnp.float32)
    )
    exposure = jnp.exp(lax.dynamic_slice_in_dim(log_exposure, row_start, share_rows, 0).reshape(-1))
    land_near = lax.dynamic_slice_in_dim(land_pad, row_start, share_rows + 2, 0)

    def evaluate(share_field, profile_now, mixing_now):
        padded = extended(share_field, ((("cells", "comp"), 1),), 1)
        prior_grad, prior_energy = field_prior(padded, land_near, field_tau)
        profile_all, mixing_all = (
            lax.all_gather(profile_now, "comp", axis=0, tiled=True),
            lax.all_gather(mixing_now, "comp", axis=1, tiled=True),
        )
        flat_tile = share_field.reshape(share_field.shape[0], -1)
        mix_logit, joint_score = tile_scores(
            flat_tile, count_rows, exposure, profile_all, mixing_all
        )
        log_mix = log_sum(mix_logit)
        log_joint = log_sum(joint_score)
        grad_counts, rate_mass, grad_mix, field_lik, log_dens = tile_grads(
            flat_tile,
            count_rows,
            land_weight,
            exposure,
            mixing_all,
            mix_logit,
            joint_score,
            log_mix,
            log_joint,
        )
        grad_counts, rate_mass, mix_rows = (
            lax.psum_scatter(grad_counts, "comp", scatter_dimension=0, tiled=True),
            lax.psum_scatter(rate_mass, "comp", scatter_dimension=0, tiled=True),
            lax.psum_scatter(grad_mix.T, "comp", scatter_dimension=0, tiled=True),
        )
        grad_mix = mix_rows.T
        grad_field = prior_grad + field_lik.reshape(share_field.shape)
        log_part = log_dens - prior_energy
        grad_counts, rate_mass, grad_mix = lax.psum((grad_counts, rate_mass, grad_mix), "cells")
        grad_profile = grad_counts - jnp.exp(profile_now) * rate_mass[:, None] - 0.25 * profile_now
        grad_mixing = grad_mix - mixing_now
        param_prior = -0.125 * jnp.sum(profile_now * profile_now) - 0.5 * jnp.sum(
            mixing_now * mixing_now
        )
        log_part = log_part + jnp.where(first_cells, param_prior, 0.0)
        return (log_part, grad_field, grad_profile, grad_mixing)

    first = evaluate(factor_field, profile, mixing)
    half_field = factor_mom + 0.5 * step_field * first[1]
    half_profile = profile_mom + 0.5 * step_profile * first[2]
    half_mixing = mixing_mom + 0.5 * step_mixing * first[3]
    new_field = factor_field + step_field * half_field
    new_profile = profile + step_profile * half_profile
    new_mixing = mixing + step_mixing * half_mixing
    second = evaluate(new_field, new_profile, new_mixing)
    new_factor_mom = half_field + 0.5 * step_field * second[1]
    new_profile_mom = half_profile + 0.5 * step_profile * second[2]
    new_mixing_mom = half_mixing + 0.5 * step_mixing * second[3]
    kinetic = 0.5 * jnp.sum(new_factor_mom * new_factor_mom)
    kinetic = kinetic + jnp.where(
        first_cells,
        0.5
        * (jnp.sum(new_profile_mom * new_profile_mom) + jnp.sum(new_mixing_mom * new_mixing_mom)),
        0.0,
    )
    log_total, kinetic_total = lax.psum((second[0], kinetic), ("cells", "comp"))
    cell_count = tile_rows * tile_cols * lax.axis_size("cells")
    hamiltonian = (kinetic_total - log_total) / cell_count
    return (
        new_field,
        new_profile,
        new_mixing,
        new_factor_mom,
        new_profile_mom,
        new_mixing_mom,
        hamiltonian,
    )


STEP_FIELD = 0.05
STEP_PARAM = 0.002
RIDGE = 0.1
LOG2E = math.log2(math.e)
LN2 = math.log(2.0)
LANES = 128
EXTRA = 16
F32 = jnp.float32
BF16 = jnp.bfloat16


def pieces(values, count):
    parts = []
    for _ in range(count):
        part = values.astype(BF16)
        parts.append(part)
        values = values - part.astype(F32)
    return parts


def dot(left, right, dims=((1,), (0,))):
    return lax.dot_general(left, right, (dims, ((), ())), preferred_element_type=F32)


def partner(values, axis, flip):
    count = lax.axis_size(axis)
    return lax.ppermute(values, axis, [(i, i ^ flip) for i in range(count)])


def all_sum(keep, send, near_edge, far_edge):
    pairs, rows, _ = keep.shape
    comp_rank, cells_rank = lax.axis_index("comp"), lax.axis_index("cells")
    chip, core = cells_rank // 2, cells_rank % 2
    chunks = keep + partner(send, "cells", 1)
    total = chunks[0]
    for part in [partner(chunks[k], "cells", 2 * k) for k in range(1, pairs)]:
        total = total + part
    first = partner(jnp.concatenate([total, near_edge], axis=0), "comp", 1)
    second = partner(total, "comp", 2)
    third = partner(jnp.concatenate([total, far_edge], axis=0), "comp", 3)
    total = total + first[:rows] + second + third[:rows]
    crossed = third[rows:]
    message = jnp.concatenate([total, crossed], axis=0)
    parts = [partner(message if k & (k + 1) == 0 else total, "cells", 2 * k) for k in range(1, pairs)]
    near = jnp.concatenate([total] + [part[:rows] for part in parts], axis=0)
    neighbour = chip ^ jnp.where(core == 0, chip + 1, chip - 1)
    passed = crossed
    for k in range(1, pairs):
        if k & (k + 1) == 0:
            passed = jnp.where(neighbour == k, parts[k - 1][rows:], passed)
    passed = jnp.where((comp_rank == 0) == (core == 0), crossed, passed)
    far = partner(jnp.concatenate([near, passed], axis=0), "cells", 1)
    at_end = (comp_rank == 0) | (comp_rank == lax.axis_size("comp") - 1)
    return near, far, first[rows:], jnp.where(at_end, far[pairs * rows :], crossed)


def group_sum(keep, send, energy, beside):
    ring, rows, _ = keep.shape
    pairs = lax.axis_size("cells") // 2
    halves = keep + partner(send, "cells", 1)
    total = halves[0]
    for part in [partner(halves[k], "comp", k) for k in range(1, ring)]:
        total = total + part
    total, beside = lax.optimization_barrier((total, beside))
    total = jnp.concatenate([total, energy], axis=0)
    for part in [partner(total, "cells", 2 * k) for k in range(1, pairs)]:
        total = total + part
    other = partner(total, "cells", 1)
    upper = lax.axis_index("cells") % 2 == 1
    low = jnp.where(upper, other, total)[:rows]
    high = jnp.where(upper, total, other)[:rows]
    return jnp.concatenate([low, high], axis=0), total[rows:] + other[rows:], beside


def gather_params(pack, cells_rank):
    tiles, ring = lax.axis_size("cells"), lax.axis_size("comp")
    rows = pack.shape[0]
    spread = [(c * ring + z, c * ring + (z ^ (1 + c % 2))) for c in range(tiles) for z in range(ring)]
    one = lax.ppermute(pack, ("cells", "comp"), spread)
    half = lax.dynamic_slice_in_dim(pack, cells_rank % 2 * (rows // 2), rows // 2, 0)
    got = jnp.concatenate([one, partner(half, "comp", 3)], axis=0)
    return got, partner(got, "cells", 1)


def chunk_index(cells_rank, k, other):
    core = cells_rank % 2
    return (((cells_rank // 2) ^ k) * 2) + (1 - core if other else core)


def gather_chunks(flat_ref, near_ref, far_ref, cells_rank, rows):
    for k in range(near_ref.shape[0] // rows):
        for source, other in ((near_ref, False), (far_ref, True)):
            start = pl.multiple_of(chunk_index(cells_rank, k, other) * rows, 8)
            flat_ref[pl.ds(start, rows), :] = source[k * rows : (k + 1) * rows, :]


def spread_chunks(flat_ref, keep_ref, send_ref, cells_rank):
    pairs, rows, _ = keep_ref.shape
    for k in range(pairs):
        for target, other in ((keep_ref, False), (send_ref, True)):
            start = pl.multiple_of(chunk_index(cells_rank, k, other) * rows, 8)
            target[k] = flat_ref[pl.ds(start, rows), :]


def load_params(flat_ref, left_ref, mix_ref, load_ref, ncomp, nfac):
    lane = lax.broadcasted_iota(jnp.int32, (LANES, LANES), 1)
    spare = jnp.zeros((LANES - EXTRA - 6 * nfac, LANES), F32)
    for q in range(ncomp // LANES):
        rows = pl.ds(q * LANES, LANES)
        prof = flat_ref[rows, :]
        high, mid, low = pieces(prof * LOG2E, 3)
        left_ref[rows, 0:LANES] = high
        left_ref[rows, 2 * LANES : 3 * LANES] = mid
        left_ref[rows, 3 * LANES : 4 * LANES] = low
        rate = jnp.sum(jnp.exp(prof), axis=1, keepdims=True) * LOG2E
        rate_high, rate_mid, rate_low = [part.astype(F32) for part in pieces(rate, 3)]
        load = flat_ref[pl.ds(ncomp + q * nfac, nfac), :]
        w_high, w_mid, w_low = [part.astype(F32) for part in pieces(load * LOG2E, 3)]
        stack = jnp.concatenate(
            [jnp.zeros((EXTRA, LANES), F32), w_high, w_high, w_high, w_mid, w_mid, w_low, spare], axis=0
        )
        turned = stack.T
        mix_ref[rows, :] = turned.astype(BF16)
        rate_part = jnp.where(
            lane < 3, rate_high, jnp.where(lane < 5, rate_mid, jnp.where(lane == 5, rate_low, 0.0))
        )
        left_ref[rows, LANES : 2 * LANES] = (turned - rate_part).astype(BF16)
        load_high, load_mid = pieces(load, 2)
        load_ref[0:nfac, q * LANES : (q + 1) * LANES] = load_high
        load_ref[nfac : 2 * nfac, q * LANES : (q + 1) * LANES] = load_mid


def load_cells(counts_ref, field_ref, log_exposure, right_ref, wide_ref):
    share, ncat, cols = counts_ref.shape
    nfac = field_ref.shape[1]
    exposure = jnp.exp(log_exposure)
    sub = lax.broadcasted_iota(jnp.int32, (EXTRA, cols), 0)
    spare = jnp.zeros((LANES - EXTRA - 6 * nfac, cols), BF16)
    for r in range(share):
        count = counts_ref[r]
        high, mid, low = pieces(field_ref[r], 3)
        e_high, e_mid, e_low = [part.astype(F32) for part in pieces(exposure[r : r + 1, :], 3)]
        e_rows = jnp.where((sub == 0) | (sub == 3) | (sub == 5), e_high, 0.0)
        e_rows = jnp.where((sub == 1) | (sub == 4), e_mid, e_rows)
        e_rows = jnp.where(sub == 2, e_low, e_rows).astype(BF16)
        extra = jnp.concatenate([e_rows, high, mid, low, high, mid, high, spare], axis=0)
        right_ref[r, 0:ncat, :] = count
        right_ref[r, LANES : 2 * LANES, :] = extra
        right_ref[r, 2 * LANES : 2 * LANES + ncat, :] = count
        right_ref[r, 3 * LANES : 3 * LANES + ncat, :] = count
        for side in range(2):
            wide_ref[r, 0:ncat, side * cols : (side + 1) * cols] = count
            wide_ref[r, LANES : 2 * LANES, side * cols : (side + 1) * cols] = extra


def field_weights(tau_ref, nfac, cols):
    row = lax.broadcasted_iota(jnp.int32, (nfac, cols), 0)
    tau = jnp.zeros((nfac, cols), F32)
    for j in range(nfac):
        tau = jnp.where(row == j, tau_ref[j], tau)
    return tau


def load_prior(rows, lands, tau, prior_ref):
    nfac, cols = tau.shape
    inner = lax.broadcasted_iota(jnp.int32, (nfac, cols), 1) < cols - 1
    energy = jnp.zeros((nfac, cols), F32)
    lands = [jnp.broadcast_to(x, (nfac, cols)) for x in lands]
    for r in range(len(rows) - 2):
        here = rows[r + 1]
        step_right = here - pltpu.roll(here, cols - 1, 1)
        edge_right = jnp.where(inner, lands[r + 1] * pltpu.roll(lands[r + 1], cols - 1, 1), 0.0)
        flux_right = edge_right * step_right
        laplace = flux_right - pltpu.roll(flux_right, 1, 1)
        parts = flux_right * step_right + RIDGE * (here * here)
        if rows[r] is not None:
            laplace = laplace + lands[r] * lands[r + 1] * (here - rows[r])
        if rows[r + 2] is not None:
            step_down = here - rows[r + 2]
            flux_down = lands[r + 1] * lands[r + 2] * step_down
            laplace = laplace + flux_down
            parts = parts + flux_down * step_down
        prior_ref[r] = -tau * (laplace + RIDGE * here)
        energy = energy + 0.5 * tau * parts
    return energy


def pack_edge(edge_ref, field, fresh, land):
    nfac, cols = field.shape
    blocks = cols // LANES
    sub = lax.broadcasted_iota(jnp.int32, (8, LANES), 0)
    lands = jnp.zeros((8, LANES), F32)
    for b in range(blocks):
        lanes = slice(b * LANES, (b + 1) * LANES)
        edge_ref[b * nfac : (b + 1) * nfac, :] = field[:, lanes]
        edge_ref[(blocks + b) * nfac : (blocks + b + 1) * nfac, :] = fresh[:, lanes]
        lands = jnp.where(sub == b, land[:, lanes], lands)
    edge_ref[2 * blocks * nfac :, :] = lands


def unpack_edge(edge, nfac, cols):
    blocks = cols // LANES
    wide = lambda start, size, step: jnp.concatenate(
        [edge[start + b * step : start + b * step + size, :] for b in range(blocks)], axis=1
    )
    return wide(0, nfac, nfac), wide(blocks * nfac, nfac, nfac), wide(2 * blocks * nfac, 1, 1)


def row_scores(r, right_ref, left_ref, mix_ref, score_ref, logit_ref):
    tops = []
    for target, values in (
        (score_ref, dot(left_ref[...], right_ref[r])),
        (logit_ref, dot(mix_ref[...], right_ref[r, LANES : 2 * LANES, :])),
    ):
        target[...] = values
        ncomp, cols = values.shape
        tops.append(jnp.max(jnp.max(values.reshape(ncomp // 8, 8, cols), axis=0), axis=0, keepdims=True))
    return tops


def row_shares(tops, land, score_ref, logit_ref, post_ref, gap_ref, kept_ref):
    ncomp, cols = score_ref.shape
    block = 32
    top_s, top_a = tops
    sum_s = jnp.zeros((8, cols), F32)
    sum_a = jnp.zeros((8, cols), F32)
    for i in range(0, ncomp, block):
        part_s = jnp.exp2(score_ref[i : i + block, :] - top_s)
        part_a = jnp.exp2(logit_ref[i : i + block, :] - top_a)
        score_ref[i : i + block, :] = part_s
        logit_ref[i : i + block, :] = part_a
        sum_s = sum_s + jnp.sum(part_s.reshape(block // 8, 8, cols), axis=0)
        sum_a = sum_a + jnp.sum(part_a.reshape(block // 8, 8, cols), axis=0)
    sum_s = jnp.sum(sum_s, axis=0, keepdims=True)
    sum_a = jnp.sum(sum_a, axis=0, keepdims=True)
    log_s = top_s + jnp.log2(sum_s)
    log_a = top_a + jnp.log2(sum_a)
    inv_s = land / sum_s
    inv_a = land / sum_a
    for i in range(0, ncomp, block):
        post = score_ref[i : i + block, :] * inv_s
        gap = post - logit_ref[i : i + block, :] * inv_a
        for targets, values in (((post_ref,), post), ((gap_ref, kept_ref), gap)):
            high, low = pieces(values, 2)
            for target in targets:
                target[i : i + block, 0:cols] = high
                target[i : i + block, cols : 2 * cols] = low
    return land * (LN2 * (log_s - log_a))


def row_products(r, wide_ref, post_ref, gap_ref, acc_ref, accw_ref):
    nfac = accw_ref.shape[0] // 3
    last = ((1,), (1,))
    start = LANES + EXTRA
    acc = dot(post_ref[...], wide_ref[r], last)
    accw = dot(wide_ref[r, start : start + 3 * nfac, :], gap_ref[...], last)
    if r == 0:
        acc_ref[...] = acc
        accw_ref[...] = accw
    else:
        acc_ref[...] += acc
        accw_ref[...] += accw


def field_grads(load_ref, gap_refs, prior_ref):
    share, nfac, cols = prior_ref.shape
    for r in range(share):
        lik = dot(load_ref[...], gap_refs[r][...])
        lik = lik[0:nfac] + lik[nfac : 2 * nfac]
        prior_ref[r] += lik[:, 0:cols] + lik[:, cols : 2 * cols]


def all_rows(land, right, wide, left, mix, scores, logits, posts, gaps, kept, acc, accw):
    share, _, cols = right.shape
    log_dens = jnp.zeros((1, cols), F32)
    tops = {}
    for r in range(share + 2):
        if r < share:
            tops[r] = row_scores(r, right, left, mix, scores[r % 2], logits[r % 2])
        if 0 <= r - 1 < share:
            p = r - 1
            log_dens = log_dens + row_shares(
                tops[p], land[p : p + 1, :], scores[p % 2], logits[p % 2], posts[p % 2], gaps[p % 2], kept[p]
            )
        if 0 <= r - 2:
            p = r - 2
            row_products(p, wide, posts[p % 2], gaps[p % 2], acc, accw)
    return log_dens


def param_grads(flat_ref, acc_ref, accw_ref, grad_ref, ncomp, nfac, flip=0):
    lane = lax.broadcasted_iota(jnp.int32, (LANES, LANES), 1)
    for q in range(ncomp // LANES):
        rows = pl.ds(q * LANES, LANES)
        lanes = slice(q * LANES, (q + 1) * LANES)
        mass = jnp.sum(jnp.where(lane < 3, acc_ref[rows, LANES : 2 * LANES], 0.0), axis=1, keepdims=True)
        group = flip ^ q
        grad_ref[pl.ds(pl.multiple_of(group * LANES, LANES), LANES), :] = acc_ref[rows, 0:LANES] - jnp.exp(flat_ref[rows, :]) * mass
        load = accw_ref[:, lanes]
        grad_ref[pl.ds(pl.multiple_of(ncomp + group * nfac, nfac), nfac), :] = load[0:nfac] + load[nfac : 2 * nfac] + load[2 * nfac : 3 * nfac]


def first_kernel(
    ncomp, rank_ref, counts_ref, field_ref, land_ref, logexp_ref, pmom_ref, wmom_ref, pack_ref, got_ref, others_ref, *refs
):
    gaps, refs = refs[: counts_ref.shape[0]], refs[counts_ref.shape[0] :]
    load, grad_ref, keep_ref, send_ref, flat, left, mix, right, wide, score0, score1, logit0, logit1, *refs = refs
    post0, post1, gap0, gap1, acc, accw = refs
    cells_rank, comp_rank = rank_ref[0], rank_ref[1]
    share, nfac, cols = field_ref.shape
    mine = pmom_ref.shape[0]
    size = mine + nfac
    middle = size // 2
    swap = cells_rank % 2 == 1
    lower, upper = got_ref[...], others_ref[...]
    one, two = jnp.where(swap, upper, lower), jnp.where(swap, lower, upper)
    three = jnp.concatenate([one[size : size + middle], two[size : size + middle]], axis=0)
    for k, source in enumerate((pack_ref[...], one, two, three)):
        flat[k * mine : (k + 1) * mine, :] = source[0:mine]
        flat[ncomp + k * nfac : ncomp + (k + 1) * nfac, :] = source[mine:size]
    here = pl.ds(pl.multiple_of(comp_rank * share, 8), share)
    land = land_ref[here, :].astype(F32)
    load_params(flat, left, mix, load, ncomp, nfac)
    load_cells(counts_ref, field_ref, logexp_ref[here, :], right, wide)
    all_rows(land, right, wide, left, mix, (score0, score1), (logit0, logit1), (post0, post1), (gap0, gap1), gaps, acc, accw)
    param_grads(flat, acc, accw, grad_ref, ncomp, nfac, comp_rank)
    nparam = grad_ref.shape[0]
    if flat.shape[0] > nparam:
        flat[nparam:, :] = jnp.zeros((flat.shape[0] - nparam, LANES), F32)
    flat[0:nparam, :] = 0.5 * STEP_PARAM * STEP_PARAM * grad_ref[...]
    own_prof, own_load = pack_ref[0:mine, :], pack_ref[mine:size, :]
    owner = cells_rank == 0
    base_prof = own_prof + STEP_PARAM * (pmom_ref[...] - 0.5 * STEP_PARAM * 0.25 * own_prof)
    base_load = own_load + STEP_PARAM * (wmom_ref[...] - 0.5 * STEP_PARAM * own_load)
    flat[pl.ds(pl.multiple_of(comp_rank * mine, mine), mine), :] += jnp.where(owner, base_prof, 0.0)
    flat[pl.ds(pl.multiple_of(ncomp + comp_rank * nfac, nfac), nfac), :] += jnp.where(owner, base_load, 0.0)
    spread_chunks(flat, keep_ref, send_ref, cells_rank)


def first_field(rank_ref, tau_ref, field_ref, mom_ref, land_ref, load_ref, *refs):
    gap_refs, refs = refs[: field_ref.shape[0]], refs[field_ref.shape[0] :]
    new_ref, half_ref, near_ref, far_ref, prior = refs
    comp_rank = rank_ref[1]
    share, nfac, cols = field_ref.shape
    land = land_ref[pl.ds(pl.multiple_of(comp_rank * share, 8), share), :].astype(F32)
    lands = [land[r : r + 1, :] for r in range(share)]
    tau = field_weights(tau_ref, nfac, cols)
    load_prior([None] + [field_ref[r] for r in range(share)] + [None], lands[:1] + lands + lands[-1:], tau, prior)
    field_grads(load_ref, gap_refs, prior)
    for r in range(share):
        half = mom_ref[r] + 0.5 * STEP_FIELD * prior[r]
        half_ref[r] = half
        new_ref[r] = field_ref[r] + STEP_FIELD * half
    even = comp_rank % 2 == 0
    end = share - 1
    for target, flag in ((near_ref, even), (far_ref, jnp.logical_not(even))):
        pack_edge(
            target,
            jnp.where(flag, field_ref[end], field_ref[0]),
            jnp.where(flag, new_ref[end], new_ref[0]),
            jnp.where(flag, lands[end], lands[0]),
        )


def edge_terms(ring, tiles, rank_ref, tau, lands, old_ref, edge_ref, other_ref):
    cells_rank, comp_rank = rank_ref[0], rank_ref[1]
    nfac, cols = tau.shape
    even = comp_rank % 2 == 0
    direct, relay = edge_ref[...], other_ref[...]
    above = unpack_edge(jnp.where(even, relay, direct), nfac, cols)
    below = unpack_edge(jnp.where(even, direct, relay), nfac, cols)
    land_above = jnp.where((comp_rank == 0) & (cells_rank == 0), 0.0, above[2])
    land_below = jnp.where((comp_rank == ring - 1) & (cells_rank == tiles - 1), 0.0, below[2])
    pull_up = -tau * (land_above * lands[0]) * (old_ref[0] - above[0])
    pull_down = -tau * (land_below * lands[-1]) * (old_ref[old_ref.shape[0] - 1] - below[0])
    return (above[1], below[1]), (land_above, land_below), (pull_up, pull_down)


def second_kernel(
    ncomp, chunk, ring, tiles, rank_ref, tau_ref, counts_ref, field_ref, land_ref, logexp_ref, pmom_ref, wmom_ref, old_ref,
    own_ref, near_ref, far_ref, edge_ref, other_ref, grad0_ref, *refs
):
    gaps, refs = refs[: counts_ref.shape[0]], refs[counts_ref.shape[0] :]
    load, new_ref, params_ref, stats_ref, keep_ref, send_ref, flat, left, mix, right, wide, *refs = refs
    score0, score1, logit0, logit1, post0, post1, gap0, gap1, acc, accw, out, grad = refs
    cells_rank, comp_rank = rank_ref[0], rank_ref[1]
    share, nfac, cols = field_ref.shape
    mine = pmom_ref.shape[0]
    nparam = grad0_ref.shape[0]
    gather_chunks(flat, near_ref, far_ref, cells_rank, chunk)
    new_prof = flat[pl.ds(pl.multiple_of(comp_rank * mine, mine), mine), :]
    new_load = flat[pl.ds(pl.multiple_of(ncomp + comp_rank * nfac, nfac), nfac), :]
    params_ref[0:mine, :] = new_prof
    params_ref[mine:, :] = new_load
    here = pl.ds(pl.multiple_of(comp_rank * share, 8), share)
    land = land_ref[here, :].astype(F32)
    lands = [land[r : r + 1, :] for r in range(share)]
    tau = field_weights(tau_ref, nfac, cols)
    _, _, pulls = edge_terms(ring, tiles, rank_ref, tau, lands, old_ref, edge_ref, other_ref)
    move = 0.5 * STEP_FIELD * STEP_FIELD
    for r in range(share):
        fresh = field_ref[r]
        if r == 0:
            fresh = fresh + move * pulls[0]
        if r == share - 1:
            fresh = fresh + move * pulls[1]
        new_ref[r] = fresh
    load_params(flat, left, mix, load, ncomp, nfac)
    load_cells(counts_ref, new_ref, logexp_ref[here, :], right, wide)
    log_dens = all_rows(land, right, wide, left, mix, (score0, score1), (logit0, logit1), (post0, post1), (gap0, gap1), gaps, acc, accw)
    param_grads(flat, acc, accw, grad, ncomp, nfac)
    first_device = (cells_rank == 0) & (comp_rank == 0)
    prof_all = flat[0:ncomp, :]
    load_all = flat[ncomp:nparam, :]
    param_energy = jnp.sum(0.125 * (prof_all * prof_all).reshape(ncomp // 8, 8, LANES), axis=0)
    param_energy = param_energy + jnp.sum(
        0.5 * (load_all * load_all).reshape((nparam - ncomp) // 8, 8, LANES), axis=0
    )
    stats_ref[0:8, :] = jnp.where(first_device, param_energy, 0.0)
    sub = lax.broadcasted_iota(jnp.int32, (8, LANES), 0)
    dens = jnp.zeros((8, LANES), F32)
    for b in range(cols // LANES):
        dens = jnp.where(sub == b, -log_dens[:, b * LANES : (b + 1) * LANES], dens)
    stats_ref[8:16, :] = dens
    out[...] = 0.5 * STEP_PARAM * (grad0_ref[...] + grad[...])
    owner = cells_rank == 0
    old_prof, old_load = own_ref[0:mine, :], own_ref[mine : mine + nfac, :]
    base_prof = pmom_ref[...] - 0.5 * STEP_PARAM * 0.25 * (old_prof + new_prof)
    base_load = wmom_ref[...] - 0.5 * STEP_PARAM * (old_load + new_load)
    out[pl.ds(pl.multiple_of(comp_rank * mine, mine), mine), :] += jnp.where(owner, base_prof, 0.0)
    out[pl.ds(pl.multiple_of(ncomp + comp_rank * nfac, nfac), nfac), :] += jnp.where(owner, base_load, 0.0)
    ring, rows, _ = keep_ref.shape
    upper = cells_rank % 2 == 1
    for k in range(ring):
        group = comp_rank ^ k
        start = pl.multiple_of(group * mine, mine)
        low = out[pl.ds(start, rows), :]
        tail = out[pl.ds(pl.multiple_of(ncomp + group * nfac, nfac), nfac), :]
        high = jnp.concatenate([out[pl.ds(start + rows, mine - rows), :], tail], axis=0)
        keep_ref[k] = jnp.where(upper, high, low)
        send_ref[k] = jnp.where(upper, low, high)


def second_field(
    ring, tiles, rank_ref, tau_ref, new_ref, half_ref, old_ref, land_ref, load_ref, stats_ref, edge_ref, other_ref, *refs
):
    gap_refs, (mom_ref, energy_ref, prior) = refs[: new_ref.shape[0]], refs[new_ref.shape[0] :]
    comp_rank = rank_ref[1]
    share, nfac, cols = new_ref.shape
    land = land_ref[pl.ds(pl.multiple_of(comp_rank * share, 8), share), :].astype(F32)
    lands = [land[r : r + 1, :] for r in range(share)]
    tau = field_weights(tau_ref, nfac, cols)
    (above, below), (land_above, land_below), (pull_up, pull_down) = edge_terms(
        ring, tiles, rank_ref, tau, lands, old_ref, edge_ref, other_ref
    )
    move = 0.5 * STEP_FIELD * STEP_FIELD
    rows = [above - move * pull_up] + [new_ref[r] for r in range(share)] + [below - move * pull_down]
    energy = load_prior(rows, [land_above] + lands + [land_below], tau, prior)
    prior[0] += pull_up
    prior[share - 1] += pull_down
    field_grads(load_ref, gap_refs, prior)
    for r in range(share):
        fresh = half_ref[r] + 0.5 * STEP_FIELD * prior[r]
        mom_ref[:, r, :] = fresh
        energy = energy + 0.5 * (fresh * fresh)
    tiles_sum = stats_ref[0:8, :] + stats_ref[8:16, :]
    for i in range(0, nfac, 8):
        for b in range(0, cols, LANES):
            tiles_sum = tiles_sum + energy[i : i + 8, b : b + LANES]
    energy_ref[...] = tiles_sum


def last_kernel(cells, *refs):
    total = refs[0][...]
    for part in refs[1:-1]:
        total = total + part[...]
    total = jnp.sum(jnp.sum(total, axis=0, keepdims=True), axis=1, keepdims=True)
    refs[-1][...] = total / cells


def fast_device(
    factor_field, profile, mixing, factor_mom, profile_mom, mixing_mom, field_tau, counts, land_mask, log_exposure
):
    nfac, share, cols = factor_field.shape
    mine, ncat = profile.shape
    tile_rows = land_mask.shape[0]
    ring = lax.axis_size("comp")
    tiles = lax.axis_size("cells")
    ncomp = mine * ring
    nparam = ncomp + nfac * ncomp // LANES
    pairs = tiles // 2
    edge = 2 * nfac * cols // LANES + 8
    round_up = lambda rows: -(-rows // (8 * tiles)) * 8
    chunk = round_up(nparam)
    comp_rank = lax.axis_index("comp")
    cells_rank = lax.axis_index("cells")
    ranks = jnp.stack([cells_rank, comp_rank]).astype(jnp.int32)
    pack = lax.optimization_barrier(jnp.pad(profile, ((0, nfac), (0, 0))) + jnp.pad(mixing, ((mine, 0), (0, 0))))
    got, others = gather_params(pack, cells_rank)
    count_rows = lax.dynamic_slice_in_dim(counts, comp_rank * share, share, 1).swapaxes(0, 1).astype(BF16)
    field_rows = factor_field.swapaxes(0, 1)
    mom_rows = factor_mom.swapaxes(0, 1)
    vmem = pl.BlockSpec(memory_space=pltpu.VMEM)
    smem = pl.BlockSpec(memory_space=pltpu.SMEM)
    shape = lambda *dims: jax.ShapeDtypeStruct(dims, F32)
    work = [
        pltpu.VMEM((tiles * chunk, LANES), F32),
        pltpu.VMEM((ncomp, 4 * LANES), BF16),
        pltpu.VMEM((ncomp, LANES), BF16),
        pltpu.VMEM((share, 4 * LANES, cols), BF16),
        pltpu.VMEM((share, 2 * LANES, 2 * cols), BF16),
    ]
    work += [pltpu.VMEM((ncomp, cols), F32)] * 4 + [pltpu.VMEM((ncomp, 2 * cols), BF16)] * 4
    work += [
        pltpu.VMEM((ncomp, 2 * LANES), F32),
        pltpu.VMEM((3 * nfac, ncomp), F32),
    ]
    field_shape = shape(share, nfac, cols)
    chunk_shape = shape(pairs, chunk, LANES)
    half_shape = shape(ring, (mine + nfac) // 2, LANES)
    gap_shapes = [jax.ShapeDtypeStruct((ncomp, 2 * cols), BF16)] * share
    load_shape = jax.ShapeDtypeStruct((2 * nfac, ncomp), BF16)
    field_flops = 2 * 2 * nfac * ncomp * 2 * cols * share
    field_cost = pl.CostEstimate(flops=field_flops, bytes_accessed=4 * share * ncomp * cols, transcendentals=0)

    def call(body, name, smem_count, vmem_count, outs, scratch, cost=None):
        return pl.pallas_call(
            body,
            name=name,
            in_specs=[smem] * smem_count + [vmem] * vmem_count,
            out_specs=[vmem] * len(outs),
            scratch_shapes=scratch,
            out_shape=outs,
            cost_estimate=cost,
            compiler_params=pltpu.CompilerParams(vmem_limit_bytes=40 * 1024 * 1024),
        )

    prior = [pltpu.VMEM((share, nfac, cols), F32)]
    first = call(
        functools.partial(first_kernel, ncomp),
        "first_gradient",
        1,
        9,
        gap_shapes + [load_shape, shape(nparam, LANES), chunk_shape, chunk_shape],
        work,
    )
    *gaps, load, grad, keep, send = first(
        ranks, count_rows, field_rows, land_mask, log_exposure, profile_mom, mixing_mom, pack, got, others
    )
    edge_shape = shape(edge, LANES)
    part_field, half, near_edge, far_edge = call(
        first_field, "first_field", 2, 4 + share, [field_shape, field_shape, edge_shape, edge_shape], prior, field_cost
    )(ranks, field_tau, field_rows, mom_rows, land_mask, load, *gaps)
    near, far, *edges = all_sum(keep, send, near_edge, far_edge)
    second = call(
        functools.partial(second_kernel, ncomp, chunk, ring, tiles),
        "second_gradient",
        2,
        13,
        gap_shapes
        + [
            load_shape,
            field_shape,
            shape(mine + nfac, ncat),
            shape(16, LANES),
            half_shape,
            half_shape,
        ],
        work + [pltpu.VMEM((nparam, LANES), F32)] * 2,
    )
    *gaps, load, new_field, new_params, stats, keep, send = second(
        ranks, field_tau, count_rows, part_field, land_mask, log_exposure, profile_mom, mixing_mom, field_rows, pack, near,
        far, *edges, grad,
    )
    new_mom, energy = call(
        functools.partial(second_field, ring, tiles), "second_field", 2, 8 + share, [shape(nfac, share, cols), shape(8, LANES)], prior, field_cost
    )(ranks, field_tau, new_field, half, field_rows, land_mask, load, stats, *edges, *gaps)
    done = (new_field.swapaxes(0, 1), new_params[:mine], new_params[mine:], new_mom)
    momenta, energy, done = group_sum(keep, send, energy, done)
    kinetic = jnp.sum(0.5 * (momenta * momenta).reshape(-1, 8, LANES), axis=0)
    total = energy + kinetic
    parts = [total] + [partner(total, "comp", k) for k in range(1, ring)]
    cells = tile_rows * cols * tiles
    (hamiltonian,) = call(functools.partial(last_kernel, cells), "total_energy", 0, ring, [shape(1, 1)], [])(*parts)
    return (
        *done,
        momenta[:mine],
        momenta[mine:],
        hamiltonian.reshape(()),
    )


def power_of_two(count):
    return count & (count - 1) == 0


def choose_device(*args):
    factor_field, profile, mixing = args[:3]
    nfac, share, cols = factor_field.shape
    mine, ncat = profile.shape
    tiles, ring = lax.axis_size("cells"), lax.axis_size("comp")
    fits = mine == LANES and ncat == LANES and nfac % 16 == 0 and 6 * nfac + EXTRA <= LANES
    fits = fits and (mine + nfac) % 16 == 0 and mine >= nfac and share % 8 == 0 and cols % LANES == 0 and cols <= 8 * LANES
    fits = fits and power_of_two(tiles) and tiles > 1 and ring == 4
    return fast_device(*args) if fits else plain_device(*args)


def solution(mesh):
    in_specs = (
        P(None, ("cells", "comp"), None),
        P("comp", None),
        P(None, "comp"),
        P(None, ("cells", "comp"), None),
        P("comp", None),
        P(None, "comp"),
        P(),
        P(None, "cells", None),
        P("cells", None),
        P("cells", None),
    )
    out_specs = (
        P(None, ("cells", "comp"), None),
        P("comp", None),
        P(None, "comp"),
        P(None, ("cells", "comp"), None),
        P("comp", None),
        P(None, "comp"),
        P(),
    )
    return jax.shard_map(
        choose_device, mesh=mesh, in_specs=in_specs, out_specs=out_specs, check_vma=False
    )
```
